32 devices in a mesh: groups: 2 (over x), role: 8 (over z, y), tp: 2 (over core).
Axes of the slice: x: 2, y: 2, z: 4, core: 2. Of those that a mesh axis runs over, the one named last changes fastest.
Arguments:
- q_lat: bfloat16 [64, 64, 576], P(('groups', 'role'), 'tp'), parts along dimension 0, may hold values from -10 to 10
- latent_cache: bfloat16 [64, 256, 576], P(('groups', 'role')), parts along dimension 0, may hold values from -16 to 16
- lengths: int32 [64], P('groups'), parts along dimension 0, may hold values from 1 to 256, 4915 in all
- placement: int32 [64], P('groups'), parts along dimension 0, may hold values from 0 to 31, each once
- tokens: bfloat16 [1536, 3584], P(('groups', 'role'), 'tp'), parts along dimension 0, may hold values from -6 to 6
- expert_ids: int32 [1536, 4], P(('groups', 'role')), parts along dimension 0, may hold values from 0 to 7, all different within a row; in each aligned block of 96 rows (0 to 95, 96 to 191, ...) at most 72 rows name the same one
- gate_weights: float32 [1536, 4], P(('groups', 'role')), parts along dimension 0, may hold values from 0.1 to 1
- w_gate: bfloat16 [8, 3584, 1024], P('role', None, 'tp'), may hold values from -0.09375 to 0.09375
- w_up: bfloat16 [8, 3584, 1024], P('role', None, 'tp'), may hold values from -0.09375 to 0.09375
- w_down: bfloat16 [8, 1024, 3584], P('role', 'tp'), may hold values from -0.1875 to 0.1875
Outputs:
- attended: bfloat16 [64, 64, 512], P(('groups', 'role'), 'tp'), parts along dimension 0
- moe_out: bfloat16 [1536, 3584], P(('groups', 'role'), 'tp'), parts along dimension 0
The draws below stay inside these ranges and needn't reach their ends.
There are 2 independent parts, one for each index of `groups`. The reference program is written for one: setup_inputs(seed, part) draws one part's arguments, and reference() takes and returns one part's arrays. A program takes and returns all parts, laid end to end along the dimension named above; an argument that names none is the same for every part. Nothing has to cross between parts.
Inputs may be any that keep to these rules, and one draw needn't show every extreme that they name: `expert_ids`: the rows of one device (96 tokens in a row) name no expert more than 72 times, and in every draw some expert is named exactly 72 times by the rows of some device. `placement`: each cache slot holds exactly one request.
All inputs are finite; a program needn't handle non-finite values.
Results may differ from the reference program's by a relative error of at most 0.0066.
Values may be sent and summed in bfloat16 or wider, within the bound.
No kernel may reach another device: no remote copies, remote signals or barrier semaphores. Data moves between devices by JAX's collectives and lax.ppermute only.
A program may use at most 64 MiB of HBM per device.

```python
import math
import jax
import jax.numpy as jnp
import numpy as np
from jax import lax

D = 3584
FF = 1024
HEADS = 64
KV_RANK = 512
TOPK = 4
CTX = 256
TOK_DEV = 96
LAT = 576
REQUESTS = 32
TOKENS = 768
EXPERTS = 8
CAP = 72
N_ROLE = 8
N_TP = 2


def draw_q_lat(key, part):
    key = jax.random.fold_in(key, 11)
    queries = 0.5 * jnp.clip(jax.random.normal(key, (REQUESTS, HEADS, LAT)), -6.0, 6.0)
    return queries.astype(jnp.float32).astype(jnp.bfloat16)


def draw_latent_cache(key, part):
    key = jax.random.fold_in(key, 12)
    noise_key, scale_key = jax.random.split(key)
    row_scale = jnp.exp(jax.random.uniform(scale_key, (REQUESTS, CTX, 1), minval=math.log(0.4), maxval=math.log(4.0)))
    latents = jnp.clip(jax.random.normal(noise_key, (REQUESTS, CTX, LAT)), -4.0, 4.0) * row_scale
    return latents.astype(jnp.float32).astype(jnp.bfloat16)


def levels(own_key, shape, cuts, smallest, top_value):
    level = 1.0
    for position, shards_of in cuts:
        steps = jax.random.uniform(jax.random.fold_in(jax.random.fold_in(own_key, 6), position), (shards_of,), jnp.float32, smallest / len(cuts), top_value / len(cuts))
        level = level * jnp.repeat(jnp.exp(steps), shape[position] // shards_of).reshape((-1,) + (1,) * (len(shape) - 1 - position))
    return level


def split_up(number_of, total, reach, skew):
    loads = [(1 << 20) // math.isqrt(rank ** skew) + 1 for rank in range(2, number_of + 1)]
    rest, given = total - reach - (number_of - 1), [1] * (number_of - 1)
    while rest > 0:
        movable = [i for i in range(number_of - 1) if given[i] < reach]
        mass, remaining = sum([loads[i] for i in movable]), rest
        for i in movable:
            more = min(reach - given[i], max(1, remaining * loads[i] // mass), rest)
            given[i] = given[i] + more
            rest = rest - more
    return np.array([reach] + given)


def ragged_sizes(rng, number_of, total, most, lean):
    if number_of == 2:
        one = jax.random.randint(rng, (), max(1, total - most), min(most, total - 1) + 1)
        return jnp.stack([one, total - one])
    sizes = jnp.asarray(split_up(number_of, total, most, lean), jnp.int32)
    pairs = (number_of - 1) // 2
    giver, receiver = sizes[1:1 + 2 * pairs:2], sizes[2:2 + 2 * pairs:2]
    slack = jnp.minimum(giver - 1, most - receiver)
    moved = jax.random.randint(jax.random.fold_in(rng, 1), (pairs,), 0, 1 << 20) % (slack + 1)
    sizes = sizes.at[1:1 + 2 * pairs:2].set(giver - moved).at[2:2 + 2 * pairs:2].set(receiver + moved)
    return sizes[jax.random.permutation(jax.random.fold_in(rng, 2), number_of)]


def assign_block(rng, own, number, rows, amount, top, most, slope):
    sequence = jax.random.permutation(rng, amount)
    heavy_load, common = shares(amount, rows * top, most, slope, True), shares(amount, rows * top, most, slope, False)
    places = jnp.arange(amount)

    def named(sizes, offset_by):
        used = int((sizes > 0).sum())
        fixed = max(1, used // 4)
        shifted = fixed + (places - fixed + offset_by * (used - fixed)) % max(1, amount - fixed)
        return jnp.zeros((amount,), jnp.int32).at[sequence[jnp.where(places < fixed, places, shifted)]].set(jnp.asarray(sizes, jnp.int32))

    sizes = jnp.where(number % 4 == 0, named(heavy_load, number // 4), named(common, number - number // 4 - 1))
    mixed = jax.random.permutation(jax.random.fold_in(own, 3), amount)
    giver, receiver = mixed[0:amount // 2 * 2:2], mixed[1:amount // 2 * 2:2]
    room = jnp.minimum(sizes[giver] - 1, most - sizes[receiver]) // 2
    room = jnp.where((giver == sequence[0]) | (receiver == sequence[0]) | (sizes[receiver] == 0), 0, jnp.maximum(room, 0))
    shifted = jax.random.randint(jax.random.fold_in(own, 4), (amount // 2,), 0, 1 << 20) % (room + 1)
    sizes = sizes.at[giver].add(-shifted).at[receiver].add(shifted)
    members = jnp.searchsorted(jnp.cumsum(sizes), jnp.arange(rows * top), side="right").astype(jnp.int32)
    grid = members.reshape(top, rows).T
    grid = grid[jax.random.permutation(jax.random.fold_in(own, 1), rows)]
    offset_by = jax.random.randint(jax.random.fold_in(own, 2), (rows, 1), 0, top)
    return jnp.take_along_axis(grid, (jnp.arange(top)[None, :] + offset_by) % top, axis=1)


def shares(number_of, total, reach, skew, full):
    weights = [(1 << 20) // math.isqrt(grade ** skew) + 1 for grade in range(1, number_of + 1)]
    largest = reach if full else min(reach, max(-(-total // number_of), total * weights[0] // sum(weights)))
    least = 1 if total - largest >= number_of - 1 else 0
    counts, spare = [largest] + [least] * (number_of - 1), total - largest - least * (number_of - 1)
    while spare > 0:
        movable = [i for i in range(1, number_of) if counts[i] < largest] or [i for i in range(1, number_of) if counts[i] < reach]
        pool, left = sum([weights[i] for i in movable]), spare
        for i in movable:
            addition = min(reach - counts[i], max(1, left * weights[i] // pool), spare)
            counts[i] = counts[i] + addition
            spare = spare - addition
    return np.array(counts)


def bell_draw(stream_key, extent, spread, reach, cuts=(), kind=jnp.bfloat16):
    values = spread * jax.random.normal(stream_key, extent, jnp.float32)
    if cuts:
        values = values * levels(stream_key, extent, cuts, -0.22, 0.18)
    return jnp.clip(values, -reach, reach).astype(kind)


def setup_inputs(seed: int = 0, part: int = 0) -> dict:
    key_of = jax.random.split(jax.random.key(seed), 11)
    part_keys = jax.random.split(jax.random.fold_in(key_of[10], part), 11)
    q_lat = draw_q_lat(jax.random.fold_in(jax.random.fold_in(key_of[10], part), 71), part)
    latent_cache = draw_latent_cache(jax.random.fold_in(jax.random.fold_in(key_of[10], part), 71), part)
    lengths = ragged_sizes(part_keys[2], REQUESTS, REQUESTS * CTX * 3 // 5, CTX, 2).astype(jnp.int32)
    placement = jax.random.permutation(part_keys[3], REQUESTS).astype(jnp.int32)
    tokens = bell_draw(part_keys[4], (TOKENS, D), 1.0, 6.0, ((0, 8), (1, 2)))
    expert_ids_keys = jax.random.split(jax.random.fold_in(part_keys[5], 1), TOKENS // TOK_DEV)
    expert_ids_turns = jax.random.permutation(jax.random.fold_in(part_keys[5], 3), TOKENS // TOK_DEV)
    expert_ids = jax.vmap(lambda own, number: assign_block(jax.random.fold_in(part_keys[5], 2), own, number, TOK_DEV, EXPERTS, TOPK, CAP, 2))(expert_ids_keys, expert_ids_turns).reshape((TOKENS, TOPK))
    gate_weights = jnp.clip(0.1 + 0.9 * jax.random.uniform(part_keys[6], (TOKENS, TOPK), jnp.float32) ** levels(part_keys[6], (TOKENS, TOPK), ((0, 8),), -0.2, 0.2), 0.1, 1.0)
    w_gate = bell_draw(key_of[7], (EXPERTS, D, FF), D ** -0.5, 0.09375, ((0, 8), (2, 2)))
    w_up = bell_draw(key_of[8], (EXPERTS, D, FF), D ** -0.5, 0.09375, ((0, 8), (2, 2)))
    w_down = bell_draw(key_of[9], (EXPERTS, FF, D), FF ** -0.5, 0.1875, ((0, 8), (1, 2)))
    return dict(q_lat=q_lat, latent_cache=latent_cache, lengths=lengths, placement=placement, tokens=tokens, expert_ids=expert_ids, gate_weights=gate_weights, w_gate=w_gate, w_up=w_up, w_down=w_down)


score_scale = 192.0 ** -0.5


def attend(q_lat, latent_cache, lengths, placement):
    slot_length = jnp.zeros((REQUESTS,), jnp.int32).at[placement].set(lengths.astype(jnp.int32))

    def one_slot(inputs):
        queries, latents, length_now = inputs
        scores = jnp.dot(queries, latents.T, preferred_element_type=jnp.float32) * score_scale
        visible = jnp.arange(CTX, dtype=jnp.int32) < length_now
        scores = jnp.where(visible[None, :], scores, -jnp.inf)
        highest = jnp.max(scores, axis=1, keepdims=True)
        raised = jnp.exp(scores - highest)
        attn_weights = (raised / jnp.sum(raised, axis=1, keepdims=True)).astype(jnp.bfloat16)
        return jnp.dot(attn_weights, latents[:, :KV_RANK], preferred_element_type=jnp.float32).astype(jnp.bfloat16)

    return lax.map(one_slot, (q_lat, latent_cache, slot_length))


def route_experts(tokens, expert_ids, gate_weights, w_gate, w_up, w_down):
    flat_ids = expert_ids.reshape(-1)
    pair_count = TOKENS * TOPK
    bound = N_ROLE * CAP
    block_width = FF // N_TP

    def one_expert(outputs, inputs):
        expert, gate_matrix, up_matrix, down_matrix = inputs
        picked = jnp.nonzero(flat_ids == expert, size=bound, fill_value=pair_count)[0].astype(jnp.int32)
        token_rows = tokens[jnp.minimum(picked // TOPK, TOKENS - 1)]
        gate_proj = jnp.dot(token_rows, gate_matrix, preferred_element_type=jnp.float32)
        up_proj = jnp.dot(token_rows, up_matrix, preferred_element_type=jnp.float32)
        expert_hidden = (jax.nn.silu(gate_proj) * up_proj).astype(jnp.bfloat16)
        total = jnp.zeros((bound, D), jnp.float32)
        for block in range(N_TP):
            lower = block * block_width
            part = jnp.dot(expert_hidden[:, lower:lower + block_width], down_matrix[lower:lower + block_width], preferred_element_type=jnp.float32)
            part = lax.optimization_barrier(part.astype(jnp.bfloat16))
            total = total + part.astype(jnp.float32)
        expert_out = total.astype(jnp.bfloat16)
        outputs = outputs.at[picked].set(expert_out, mode="drop")
        return outputs, None

    initial = jnp.zeros((pair_count, D), jnp.bfloat16)
    experts_idx = jnp.arange(EXPERTS, dtype=jnp.int32)
    outputs, _ = lax.scan(one_expert, initial, (experts_idx, w_gate, w_up, w_down))
    weighted = outputs.reshape(TOKENS, TOPK, D).astype(jnp.float32) * gate_weights[:, :, None]
    return jnp.sum(weighted, axis=1).astype(jnp.bfloat16)


def reference(q_lat, latent_cache, lengths, placement, tokens, expert_ids, gate_weights, w_gate, w_up, w_down):
    attended = attend(q_lat, latent_cache, lengths, placement)
    moe_out = route_experts(tokens, expert_ids, gate_weights, w_gate, w_up, w_down)
    return (attended, moe_out)
```

```python
import functools

import jax
import jax.numpy as jnp
from jax import lax
from jax.experimental import pallas as pl
from jax.experimental.pallas import tpu as pltpu
from jax.sharding import PartitionSpec as P

KV_RANK = 512


score_scale = 192.0 ** (-0.5)


def attend_local(q_lat, latent_cache, lengths, placement):
    slot_count = q_lat.shape[0]
    offset = lax.axis_index("role") * slot_count
    slot_ids = offset + jnp.arange(slot_count, dtype=jnp.int32)
    matches = placement[None, :] == slot_ids[:, None]
    slot_length = jnp.sum(jnp.where(matches, lengths[None, :], 0), axis=1)
    scores = (
        jnp.einsum("shc,stc->sht", q_lat, latent_cache, preferred_element_type=jnp.float32)
        * score_scale
    )
    position = jnp.arange(latent_cache.shape[1], dtype=jnp.int32)
    visible = position[None, None, :] < slot_length[:, None, None]
    scores = jnp.where(visible, scores, -jnp.inf)
    highest = jnp.max(scores, axis=2, keepdims=True)
    raised = jnp.exp(scores - highest)
    attn_weights = (raised / jnp.sum(raised, axis=2, keepdims=True)).astype(jnp.bfloat16)
    values = latent_cache[:, :, :KV_RANK]
    return jnp.einsum(
        "sht,stc->shc", attn_weights, values, preferred_element_type=jnp.float32
    ).astype(jnp.bfloat16)


def route_all_to_all(tokens, expert_ids, gate_weights, w_gate, w_up, w_down):
    role_count = lax.axis_size("role")
    token_count = expert_ids.shape[0]
    route_count = expert_ids.shape[1]
    capacity = 3 * token_count * route_count // (2 * role_count)
    flat_ids = expert_ids.reshape(-1)
    onehot = (flat_ids[:, None] == jnp.arange(role_count, dtype=jnp.int32)[None, :]).astype(
        jnp.int32
    )
    earlier = jnp.cumsum(onehot, axis=0) - onehot
    slot_index = jnp.sum(earlier * onehot, axis=1)
    target = flat_ids * capacity + slot_index
    source = jnp.arange(token_count * route_count, dtype=jnp.int32) // route_count
    outgoing = lax.all_gather(tokens, "tp", axis=1, tiled=True)
    columns = outgoing.shape[1]
    buffer_rows = (
        jnp.zeros((role_count * capacity, columns), jnp.bfloat16).at[target].set(outgoing[source])
    )
    buffer_rows = buffer_rows.reshape(role_count, capacity, columns)
    gate_matrix = w_gate[0]
    up_matrix = w_up[0]
    down_matrix = w_down[0]
    received = lax.all_to_all(buffer_rows, "role", split_axis=0, concat_axis=0, tiled=True)
    item_count = received.shape[1]
    arrived = received.reshape(role_count * item_count, columns)
    gate_proj = jnp.dot(arrived, gate_matrix, preferred_element_type=jnp.float32)
    up_proj = jnp.dot(arrived, up_matrix, preferred_element_type=jnp.float32)
    expert_hidden = (jax.nn.silu(gate_proj) * up_proj).astype(jnp.bfloat16)
    partial_out = jnp.dot(expert_hidden, down_matrix, preferred_element_type=jnp.float32)
    summed = lax.psum_scatter(
        partial_out.astype(jnp.bfloat16), "tp", scatter_dimension=1, tiled=True
    )
    summed = summed.reshape(role_count, item_count, summed.shape[1])
    returned = lax.all_to_all(summed, "role", split_axis=0, concat_axis=0, tiled=True)
    half_width = returned.shape[2]
    flat_back = returned.reshape(role_count * capacity, half_width)
    chosen_rows = (
        flat_back[target].reshape(token_count, route_count, half_width).astype(jnp.float32)
    )
    moe_result = jnp.sum(chosen_rows * gate_weights[:, :, None], axis=1).astype(jnp.bfloat16)
    return moe_result


LANES = 128
VMEM_LIMIT = 56 * 1024 * 1024


def round_up(value, unit):
    return -(-value // unit) * unit


def call(kernel, out_shape, flops, moved, **kwargs):
    return pl.pallas_call(
        kernel,
        out_shape=out_shape,
        compiler_params=pltpu.CompilerParams(vmem_limit_bytes=VMEM_LIMIT),
        cost_estimate=pl.CostEstimate(flops=flops, bytes_accessed=moved, transcendentals=0),
        **kwargs,
    )


def lane_index(rows):
    return lax.broadcasted_iota(jnp.int32, (rows, LANES), 1)


def decode_gate(pieces, expert, expert_count):
    lane = lane_index(pieces.shape[0])
    wanted = lane == expert
    for piece in (1, 2):
        wanted = wanted | (lane == expert + piece * expert_count)
    return jnp.sum(jnp.where(wanted, pieces, 0.0), axis=1, keepdims=True)


def slot_matrix(gate):
    rows = gate.shape[0]
    named = jnp.broadcast_to((gate > 0.0).astype(jnp.float32), (rows, LANES))
    lower = lax.broadcasted_iota(jnp.int32, (rows, rows), 0) >= lax.broadcasted_iota(
        jnp.int32, (rows, rows), 1
    )
    rank = jnp.dot(
        lower.astype(jnp.bfloat16), named.astype(jnp.bfloat16), preferred_element_type=jnp.float32
    )
    slot = lane_index(rows).astype(jnp.float32)
    return jnp.where((named > 0.0) & (rank - 1.0 == slot), 1.0, 0.0).astype(jnp.bfloat16)


def compact(gate, rows_in, capacity):
    picked = lax.dot_general(
        slot_matrix(gate),
        rows_in,
        (((0,), (0,)), ((), ())),
        preferred_element_type=jnp.float32,
    )
    return picked[:capacity].astype(jnp.bfloat16)


def prepare_kernel(expert_count, tokens_ref, ids_ref, gates_ref, wide_ref, cross_ref):
    rows, half = tokens_ref.shape
    lane = lane_index(rows)
    column = lane
    for piece in (1, 2):
        column = jnp.where(
            (lane >= piece * expert_count) & (lane < (piece + 1) * expert_count),
            lane - piece * expert_count,
            column,
        )
    dense = jnp.zeros((rows, LANES), jnp.float32)
    for choice in range(ids_ref.shape[1]):
        dense = dense + jnp.where(
            ids_ref[:, choice : choice + 1] == column, gates_ref[:, choice : choice + 1], 0.0
        )
    high = dense.astype(jnp.bfloat16).astype(jnp.float32)
    middle = (dense - high).astype(jnp.bfloat16).astype(jnp.float32)
    low = dense - high - middle
    pieces = jnp.where(
        lane < expert_count,
        high,
        jnp.where(
            lane < 2 * expert_count, middle, jnp.where(lane < 3 * expert_count, low, 0.0)
        ),
    ).astype(jnp.bfloat16)
    wide_ref[:, :half] = tokens_ref[...]
    wide_ref[:, half:] = pieces
    other = lax.axis_index("role") ^ 1
    gate = decode_gate(pieces.astype(jnp.float32), other, expert_count)
    cross_ref[...] = compact(gate, tokens_ref[...], cross_ref.shape[0])


def prepare(tokens, expert_ids, gate_weights, expert_count, capacity):
    rows, half = tokens.shape
    return call(
        functools.partial(prepare_kernel, expert_count),
        (
            jax.ShapeDtypeStruct((rows, half + LANES), jnp.bfloat16),
            jax.ShapeDtypeStruct((capacity, half), jnp.bfloat16),
        ),
        2 * rows * LANES * half,
        6 * rows * half,
        name="prepare",
    )(tokens, expert_ids, gate_weights)


def cross_kernel(expert_count, wide_ref, cross_ref):
    half = cross_ref.shape[1]
    other = lax.axis_index("role") ^ 1
    gate = decode_gate(wide_ref[:, half:].astype(jnp.float32), other, expert_count)
    cross_ref[...] = compact(gate, wide_ref[:, :half], cross_ref.shape[0])


def cross_rows(wide, expert_count, capacity):
    rows, width = wide.shape
    half = width - LANES
    return call(
        functools.partial(cross_kernel, expert_count),
        jax.ShapeDtypeStruct((capacity, half), jnp.bfloat16),
        2 * rows * LANES * half,
        4 * rows * half,
        name="cross_rows",
    )(wide)


def expert_kernel(starts, part_count, *refs):
    parts = refs[: 2 * part_count]
    gate_ref, up_ref, down_ref, keep_ref, send_ref, arrived, total = refs[2 * part_count :]
    half = keep_ref.shape[1]
    core = lax.axis_index("tp")
    own = pl.ds(pl.multiple_of(core * half, LANES), half)
    sibling = pl.ds(pl.multiple_of((1 - core) * half, LANES), half)
    step = pl.program_id(0)

    @pl.when(step == 0)
    def _():
        for index, start in enumerate(starts):
            near, far = parts[2 * index], parts[2 * index + 1]
            arrived[start : start + near.shape[0], own] = near[:, :half]
            arrived[start : start + near.shape[0], sibling] = far[:, :half]

    gate_proj = jnp.dot(arrived[...], gate_ref[...], preferred_element_type=jnp.float32)
    up_proj = jnp.dot(arrived[...], up_ref[...], preferred_element_type=jnp.float32)
    hidden = (jax.nn.silu(gate_proj) * up_proj).astype(jnp.bfloat16)
    width = half // 2
    for column in range(0, 2 * half, width):
        columns = slice(column, column + width)
        product = jnp.dot(hidden, down_ref[:, columns], preferred_element_type=jnp.float32)

        @pl.when(step == 0)
        def _():
            total[:, columns] = product

        @pl.when(step > 0)
        def _():
            total[:, columns] += product

    @pl.when(step == pl.num_programs(0) - 1)
    def _():
        keep_ref[...] = total[:, own].astype(jnp.bfloat16)
        send_ref[...] = total[:, sibling].astype(jnp.bfloat16)


def expert(parts, half, w_gate, w_up, w_down):
    _, depth, hidden_count = w_gate.shape
    starts, rows = [], 0
    for near, _ in parts:
        starts.append(rows)
        rows += near.shape[0]
    steps = 2
    width = hidden_count // steps
    operands = [ref for pair in parts for ref in pair]
    shape = jax.ShapeDtypeStruct((rows, half), jnp.bfloat16)
    whole = pl.BlockSpec((rows, half), lambda step: (0, 0))
    return call(
        functools.partial(expert_kernel, tuple(starts), len(parts)),
        (shape, shape),
        6 * rows * depth * hidden_count,
        6 * depth * hidden_count + 8 * rows * half,
        grid=(steps,),
        in_specs=[pl.BlockSpec(ref.shape, lambda step: (0, 0)) for ref in operands]
        + [
            pl.BlockSpec((None, depth, width), lambda step: (0, 0, step)),
            pl.BlockSpec((None, depth, width), lambda step: (0, 0, step)),
            pl.BlockSpec((None, width, depth), lambda step: (0, step, 0)),
        ],
        out_specs=(whole, whole),
        scratch_shapes=[
            pltpu.VMEM((rows, depth), jnp.bfloat16),
            pltpu.VMEM((rows, depth), jnp.float32),
        ],
        name="expert",
    )(*operands, w_gate, w_up, w_down)


def add_parts(keep, received):
    return (keep.astype(jnp.float32) + received.astype(jnp.float32)).astype(jnp.bfloat16)


def outputs_kernel(starts, keep_ref, received_ref, *out_refs):
    for start, out_ref in zip(starts, out_refs):
        rows = slice(start, start + out_ref.shape[0])
        out_ref[...] = add_parts(keep_ref[rows, :], received_ref[rows, :])


def outputs(keep, received, starts, capacity):
    half = keep.shape[1]
    return call(
        functools.partial(outputs_kernel, tuple(starts)),
        tuple(jax.ShapeDtypeStruct((capacity, half), jnp.bfloat16) for _ in starts),
        len(starts) * capacity * half,
        6 * len(starts) * capacity * half,
        name="outputs",
    )(keep, received)


def combine_kernel(expert_count, wide_ref, keep_ref, received_ref, back_ref, *refs):
    sums, out_ref = refs[:-1], refs[-1]
    half = out_ref.shape[1]
    me = lax.axis_index("role")
    pieces = wide_ref[:, half:].astype(jnp.float32)
    gate = decode_gate(pieces, me, expert_count)
    gate_other = decode_gate(pieces, me ^ 1, expert_count)
    slots = slot_matrix(gate_other)[:, : back_ref.shape[0]]
    spread = jnp.dot(slots, back_ref[...], preferred_element_type=jnp.float32)
    own = add_parts(keep_ref[...], received_ref[...]).astype(jnp.float32)
    result = gate * own + gate_other * spread
    for ref in sums:
        result = result + ref[...].astype(jnp.float32)
    out_ref[...] = result.astype(jnp.bfloat16)


def combine(wide, index, keep, received, back, sums, expert_count):
    rows = wide.shape[0]
    half = keep.shape[1]
    block = pl.BlockSpec((rows, half), lambda step: (index, 0))
    plain = pl.BlockSpec((rows, half), lambda step: (0, 0))
    return call(
        functools.partial(combine_kernel, expert_count),
        jax.ShapeDtypeStruct((rows, half), jnp.bfloat16),
        2 * rows * LANES * half,
        12 * rows * half,
        grid=(1,),
        in_specs=[
            pl.BlockSpec(wide.shape, lambda step: (0, 0)),
            block,
            block,
            pl.BlockSpec(back.shape, lambda step: (0, 0)),
        ]
        + [plain] * len(sums),
        out_specs=plain,
        name="combine",
    )(wide, keep, received, back, *sums)


def swap(array, bits):
    count = lax.axis_size("role")
    return lax.ppermute(array, "role", [(device, device ^ bits) for device in range(count)])


def swap_core(array):
    return lax.ppermute(array, "tp", [(0, 1), (1, 0)])


def route_multicast(tokens, expert_ids, gate_weights, w_gate, w_up, w_down):
    role_count = lax.axis_size("role")
    token_count, route_count = expert_ids.shape
    half = tokens.shape[1]
    capacity = round_up(3 * token_count * route_count // (2 * role_count), 16)
    pair, mirror, row = 2, 6, 1

    wide, cross = prepare(tokens, expert_ids, gate_weights, role_count, capacity)
    wide_mirror = swap(wide, mirror)
    wide_pair = swap(wide, pair)
    cross_in = swap(cross, row)
    cross_pair_in = swap(cross_rows(wide_pair, role_count, capacity), row)
    wide_far = swap(wide_mirror, pair)
    cross_mirror_in = swap(cross_rows(wide_mirror, role_count, capacity), row)
    cross_far_in = swap(cross_rows(wide_far, role_count, capacity), row)

    early = [wide, wide_pair, wide_mirror, cross_in, cross_pair_in]
    late = [wide_far, cross_mirror_in, cross_far_in]
    weights = (w_gate, w_up, w_down)
    keep_early, send_early = expert([(a, swap_core(a)) for a in early], half, *weights)
    received_early = swap_core(send_early)
    keep_late, send_late = expert([(a, swap_core(a)) for a in late], half, *weights)
    received_late = swap_core(send_late)

    after = 3 * token_count
    back_own, back_pair = outputs(
        keep_early, received_early, (after, after + capacity), capacity
    )
    after = token_count
    back_mirror, back_far = outputs(
        keep_late, received_late, (after, after + capacity), capacity
    )
    back_far = swap(back_far, row)
    back_mirror = swap(back_mirror, row)
    back_pair = swap(back_pair, row)
    back_own = swap(back_own, row)
    sum_far = combine(wide_far, 0, keep_late, received_late, back_far, (), role_count)
    from_far = swap(sum_far, pair)
    sum_pair = combine(wide_pair, 1, keep_early, received_early, back_pair, (), role_count)
    from_pair = swap(sum_pair, pair)
    sum_mirror = combine(
        wide_mirror, 2, keep_early, received_early, back_mirror, (from_far,), role_count
    )
    from_mirror = swap(sum_mirror, mirror)
    return combine(
        wide, 0, keep_early, received_early, back_own, (from_pair, from_mirror), role_count
    )


def shards(
    q_lat, latent_cache, lengths, placement, tokens, expert_ids, gate_weights, w_gate, w_up, w_down
):
    attended = attend_local(q_lat, latent_cache, lengths, placement)
    if lax.axis_size("role") == 8 and lax.axis_size("tp") == 2:
        route = route_multicast
    else:
        route = route_all_to_all
    return (attended, route(tokens, expert_ids, gate_weights, w_gate, w_up, w_down))


def solution(mesh):
    return jax.shard_map(
        shards,
        mesh=mesh,
        in_specs=(
            P(("groups", "role"), "tp", None),
            P(("groups", "role"), None, None),
            P("groups"),
            P("groups"),
            P(("groups", "role"), "tp"),
            P(("groups", "role"), None),
            P(("groups", "role"), None),
            P("role", None, "tp"),
            P("role", None, "tp"),
            P("role", "tp", None),
        ),
        out_specs=(P(("groups", "role"), "tp", None), P(("groups", "role"), "tp")),
        check_vma=False,
    )
```

```python
import functools

import jax
import jax.numpy as jnp
from jax import lax
from jax.experimental import pallas as pl
from jax.experimental.pallas import tpu as pltpu
from jax.sharding import PartitionSpec as P

KV_RANK = 512


score_scale = 192.0 ** (-0.5)


def attend_local(q_lat, latent_cache, lengths, placement):
    slot_count = q_lat.shape[0]
    offset = lax.axis_index("role") * slot_count
    slot_ids = offset + jnp.arange(slot_count, dtype=jnp.int32)
    matches = placement[None, :] == slot_ids[:, None]
    slot_length = jnp.sum(jnp.where(matches, lengths[None, :], 0), axis=1)
    scores = (
        jnp.einsum("shc,stc->sht", q_lat, latent_cache, preferred_element_type=jnp.float32)
        * score_scale
    )
    position = jnp.arange(latent_cache.shape[1], dtype=jnp.int32)
    visible = position[None, None, :] < slot_length[:, None, None]
    scores = jnp.where(visible, scores, -jnp.inf)
    highest = jnp.max(scores, axis=2, keepdims=True)
    raised = jnp.exp(scores - highest)
    attn_weights = (raised / jnp.sum(raised, axis=2, keepdims=True)).astype(jnp.bfloat16)
    values = latent_cache[:, :, :KV_RANK]
    return jnp.einsum(
        "sht,stc->shc", attn_weights, values, preferred_element_type=jnp.float32
    ).astype(jnp.bfloat16)


def route_all_to_all(tokens, expert_ids, gate_weights, w_gate, w_up, w_down):
    role_count = lax.axis_size("role")
    token_count = expert_ids.shape[0]
    route_count = expert_ids.shape[1]
    capacity = 3 * token_count * route_count // (2 * role_count)
    flat_ids = expert_ids.reshape(-1)
    onehot = (flat_ids[:, None] == jnp.arange(role_count, dtype=jnp.int32)[None, :]).astype(
        jnp.int32
    )
    earlier = jnp.cumsum(onehot, axis=0) - onehot
    slot_index = jnp.sum(earlier * onehot, axis=1)
    target = flat_ids * capacity + slot_index
    source = jnp.arange(token_count * route_count, dtype=jnp.int32) // route_count
    outgoing = lax.all_gather(tokens, "tp", axis=1, tiled=True)
    columns = outgoing.shape[1]
    buffer_rows = (
        jnp.zeros((role_count * capacity, columns), jnp.bfloat16).at[target].set(outgoing[source])
    )
    buffer_rows = buffer_rows.reshape(role_count, capacity, columns)
    gate_matrix = w_gate[0]
    up_matrix = w_up[0]
    down_matrix = w_down[0]
    received = lax.all_to_all(buffer_rows, "role", split_axis=0, concat_axis=0, tiled=True)
    item_count = received.shape[1]
    arrived = received.reshape(role_count * item_count, columns)
    gate_proj = jnp.dot(arrived, gate_matrix, preferred_element_type=jnp.float32)
    up_proj = jnp.dot(arrived, up_matrix, preferred_element_type=jnp.float32)
    expert_hidden = (jax.nn.silu(gate_proj) * up_proj).astype(jnp.bfloat16)
    partial_out = jnp.dot(expert_hidden, down_matrix, preferred_element_type=jnp.float32)
    summed = lax.psum_scatter(
        partial_out.astype(jnp.bfloat16), "tp", scatter_dimension=1, tiled=True
    )
    summed = summed.reshape(role_count, item_count, summed.shape[1])
    returned = lax.all_to_all(summed, "role", split_axis=0, concat_axis=0, tiled=True)
    half_width = returned.shape[2]
    flat_back = returned.reshape(role_count * capacity, half_width)
    chosen_rows = (
        flat_back[target].reshape(token_count, route_count, half_width).astype(jnp.float32)
    )
    moe_result = jnp.sum(chosen_rows * gate_weights[:, :, None], axis=1).astype(jnp.bfloat16)
    return moe_result


LANES = 128
VMEM_LIMIT = 16 * 1024 * 1024


def round_up(value, unit):
    return -(-value // unit) * unit


def call(kernel, operands, out_shapes, flops, name, scratch=(), types=None, last=False):
    place = pl.BlockSpec(memory_space=pltpu.VMEM)
    return pl.pallas_call(
        kernel,
        in_specs=[place] * len(operands),
        out_specs=[place] * len(out_shapes),
        out_shape=[
            (jax.ShapeDtypeStruct if last else pltpu.VMEM)(
                shape, jnp.bfloat16 if types is None else types[index]
            )
            for index, shape in enumerate(out_shapes)
        ],
        scratch_shapes=list(scratch),
        name=name,
        compiler_params=pltpu.CompilerParams(vmem_limit_bytes=VMEM_LIMIT),
        cost_estimate=pl.CostEstimate(flops=0, bytes_accessed=0, transcendentals=0),
    )(*[pltpu.with_memory_space_constraint(operand, pltpu.VMEM) for operand in operands])


def after(value, *earlier):
    return lax.optimization_barrier((value, *earlier))[0]


def lane_index(rows):
    return lax.broadcasted_iota(jnp.int32, (rows, LANES), 1)


def decode_gate(pieces, expert, expert_count):
    lane = lane_index(pieces.shape[0])
    wanted = lane == expert
    for piece in (1, 2):
        wanted = wanted | (lane == expert + piece * expert_count)
    return jnp.sum(jnp.where(wanted, pieces, 0.0), axis=1, keepdims=True)


def slot_matrix(gate):
    rows = gate.shape[0]
    named = jnp.broadcast_to((gate > 0.0).astype(jnp.float32), (rows, LANES))
    lower = lax.broadcasted_iota(jnp.int32, (rows, rows), 0) >= lax.broadcasted_iota(
        jnp.int32, (rows, rows), 1
    )
    rank = jnp.dot(
        lower.astype(jnp.bfloat16), named.astype(jnp.bfloat16), preferred_element_type=jnp.float32
    )
    slot = lane_index(rows).astype(jnp.float32)
    return jnp.where((named > 0.0) & (rank - 1.0 == slot), 1.0, 0.0).astype(jnp.bfloat16)


def compact(gate, rows_in, capacity):
    picked = lax.dot_general(
        slot_matrix(gate),
        rows_in,
        (((0,), (0,)), ((), ())),
        preferred_element_type=jnp.float32,
    )
    return picked[:capacity].astype(jnp.bfloat16)


def prepare_kernel(expert_count, tokens_ref, ids_ref, gates_ref, wide_ref, cross_ref):
    rows, half = tokens_ref.shape
    piece_rows = round_up(3 * expert_count, 16)
    line = lax.broadcasted_iota(jnp.int32, (piece_rows, rows), 0)
    named = line
    for piece in (1, 2):
        named = jnp.where(line >= piece * expert_count, line - piece * expert_count, named)
    dense = jnp.zeros((piece_rows, rows), jnp.float32)
    for choice in range(ids_ref.shape[0]):
        dense = dense + jnp.where(
            ids_ref[choice : choice + 1, :] == named, gates_ref[choice : choice + 1, :], 0.0
        )
    high = dense.astype(jnp.bfloat16).astype(jnp.float32)
    middle = (dense - high).astype(jnp.bfloat16).astype(jnp.float32)
    low = dense - high - middle
    pieces = jnp.where(line < expert_count, high, jnp.where(line < 2 * expert_count, middle, low))
    unit = lax.broadcasted_iota(jnp.int32, (piece_rows, LANES), 0) == lax.broadcasted_iota(
        jnp.int32, (piece_rows, LANES), 1
    )
    turned = lax.dot_general(
        pieces.astype(jnp.bfloat16),
        unit.astype(jnp.bfloat16),
        (((0,), (0,)), ((), ())),
        preferred_element_type=jnp.float32,
    )
    wide_ref[:, :half] = tokens_ref[...]
    wide_ref[:, half:] = turned.astype(jnp.bfloat16)
    gate = decode_gate(turned, lax.axis_index("role") ^ 1, expert_count)
    cross_ref[...] = compact(gate, tokens_ref[...], cross_ref.shape[0])


def prepare(tokens, expert_ids, gate_weights, expert_count, capacity):
    rows, half = tokens.shape
    return call(
        functools.partial(prepare_kernel, expert_count),
        (tokens, expert_ids.T, gate_weights.T),
        ((rows, half + LANES), (capacity, half)),
        2 * rows * LANES * half,
        "prepare",
    )


def cross_kernel(expert_count, wide_ref, cross_ref):
    half = cross_ref.shape[1]
    other = lax.axis_index("role") ^ 1
    gate = decode_gate(wide_ref[:, half:].astype(jnp.float32), other, expert_count)
    cross_ref[...] = compact(gate, wide_ref[:, :half], cross_ref.shape[0])


def cross_rows(wide, expert_count, capacity):
    rows, width = wide.shape
    half = width - LANES
    return call(
        functools.partial(cross_kernel, expert_count),
        (wide,),
        ((capacity, half),),
        2 * rows * LANES * half,
        "cross_rows",
    )[0]


def hidden_kernel(starts, part_count, *refs):
    parts = refs[: 2 * part_count]
    gate_ref, up_ref, hidden_ref, arrived = refs[2 * part_count :]
    half = arrived.shape[1] // 2
    core = lax.axis_index("tp")
    own = pl.multiple_of(core * half, LANES)
    sibling = pl.multiple_of((1 - core) * half, LANES)
    for index, start in enumerate(starts):
        near, far = parts[2 * index], parts[2 * index + 1]
        rows = slice(start, start + near.shape[0])
        arrived[rows, pl.ds(own, half)] = near[:, :half]
        arrived[rows, pl.ds(sibling, half)] = far[:, :half]
    width = 256
    for first in range(0, hidden_ref.shape[1], width):
        units = slice(first, first + width)
        gate_proj = jnp.dot(arrived[...], gate_ref[:, units], preferred_element_type=jnp.float32)
        up_proj = jnp.dot(arrived[...], up_ref[:, units], preferred_element_type=jnp.float32)
        hidden_ref[:, units] = (jax.nn.silu(gate_proj) * up_proj).astype(jnp.bfloat16)


def row_starts(parts):
    starts, rows = [], 0
    for part in parts:
        starts.append(rows)
        rows += round_up(part.shape[0], 16)
    return tuple(starts), rows


def hidden_units(pairs, w_gate, w_up):
    depth, hidden_count = w_gate.shape
    starts, rows = row_starts([near for near, _ in pairs])
    operands = [array for pair in pairs for array in pair]
    return call(
        functools.partial(hidden_kernel, starts, len(pairs)),
        (*operands, w_gate, w_up),
        ((rows, hidden_count),),
        4 * rows * depth * hidden_count,
        "hidden_units",
        (pltpu.VMEM((rows, depth), jnp.bfloat16),),
    )[0]


def down_kernel(expert_count, starts, wide_count, *refs):
    wides = refs[:wide_count]
    own_ref, other_ref, down_ref, down_other_ref = refs[wide_count : wide_count + 4]
    outs = refs[wide_count + 4 :]
    half = down_other_ref.shape[1]
    me = lax.axis_index("role")
    gates = [decode_gate(ref[:, half:].astype(jnp.float32), me, expert_count) for ref in wides]
    width = 256
    for first in range(0, half, width):
        columns = slice(first, first + width)
        result = jnp.dot(
            own_ref[...],
            down_ref[:, columns],
            preferred_element_type=jnp.float32,
        ) + jnp.dot(
            other_ref[...], down_other_ref[:, columns], preferred_element_type=jnp.float32
        )
        for index, (start, out_ref) in enumerate(zip(starts, outs)):
            block = result[start : start + out_ref.shape[0]].astype(jnp.bfloat16)
            if index < wide_count:
                block = gates[index] * block.astype(jnp.float32)
            out_ref[:, columns] = block


def down(wides, cross_count, hidden, hidden_other, w_down, down_other, capacity, expert_count):
    half = down_other.shape[1]
    shapes = [(wide.shape[0], half) for wide in wides] + [(capacity, half)] * cross_count
    starts, rows = [], 0
    for shape in shapes:
        starts.append(rows)
        rows += round_up(shape[0], 16)
    return call(
        functools.partial(down_kernel, expert_count, tuple(starts), len(wides)),
        (*wides, hidden, hidden_other, w_down, down_other),
        tuple(shapes),
        4 * rows * half * hidden.shape[1],
        "down",
        (),
        [jnp.float32] * len(wides) + [jnp.bfloat16] * cross_count,
    )


def attend_kernel(query_ref, latent_ref, lengths_ref, placement_ref, out_ref):
    slot_count, head_count, _ = query_ref.shape
    rank, context = out_ref.shape[2], latent_ref.shape[2]
    first = lax.axis_index("role") * slot_count
    position = lax.broadcasted_iota(jnp.int32, (head_count, context), 1)
    for slot in range(slot_count):
        here = placement_ref[...] == first + slot
        length = jnp.sum(jnp.where(here, lengths_ref[...], 0), axis=1, keepdims=True)
        scores = (
            jnp.dot(query_ref[slot], latent_ref[slot], preferred_element_type=jnp.float32)
            * score_scale
        )
        scores = jnp.where(position < length, scores, -jnp.inf)
        raised = jnp.exp(scores - jnp.max(scores, axis=1, keepdims=True))
        attn_weights = (raised / jnp.sum(raised, axis=1, keepdims=True)).astype(jnp.bfloat16)
        out_ref[slot] = lax.dot_general(
            attn_weights,
            latent_ref[slot, :rank, :],
            (((1,), (1,)), ((), ())),
            preferred_element_type=jnp.float32,
        ).astype(jnp.bfloat16)


def attend(q_lat, latent_cache, lengths, placement):
    slot_count, head_count, _ = q_lat.shape
    return pl.pallas_call(
        attend_kernel,
        out_shape=jax.ShapeDtypeStruct((slot_count, head_count, KV_RANK), jnp.bfloat16),
        name="attend",
        compiler_params=pltpu.CompilerParams(vmem_limit_bytes=VMEM_LIMIT),
        cost_estimate=pl.CostEstimate(flops=0, bytes_accessed=0, transcendentals=0),
    )(q_lat, latent_cache.transpose(0, 2, 1), lengths[None, :], placement[None, :])


def fetch_kernel(down_hbm, _, down_ref, away_ref, sems):
    half = down_ref.shape[1]
    core = lax.axis_index("tp")
    own = pl.multiple_of(core * half, LANES)
    sibling = pl.multiple_of((1 - core) * half, LANES)
    copies = [
        pltpu.make_async_copy(down_hbm.at[0, :, pl.ds(sibling, half)], away_ref, sems.at[0]),
        pltpu.make_async_copy(down_hbm.at[0, :, pl.ds(own, half)], down_ref, sems.at[1]),
    ]
    for copy in copies:
        copy.start()
    for copy in copies:
        copy.wait()


def fetch(w_down, earlier):
    _, hidden_count, depth = w_down.shape
    half = depth // 2
    shapes = [(hidden_count, half)] * 2
    return pl.pallas_call(
        fetch_kernel,
        in_specs=[pl.BlockSpec(memory_space=pltpu.HBM), pl.BlockSpec(memory_space=pl.ANY)],
        out_specs=[pl.BlockSpec(memory_space=pltpu.VMEM)] * 2,
        out_shape=[pltpu.VMEM(shape, jnp.bfloat16) for shape in shapes],
        scratch_shapes=[pltpu.SemaphoreType.DMA((2,))],
        name="fetch",
        compiler_params=pltpu.CompilerParams(vmem_limit_bytes=VMEM_LIMIT),
        cost_estimate=pl.CostEstimate(flops=0, bytes_accessed=0, transcendentals=0),
    )(pltpu.with_memory_space_constraint(w_down, pltpu.HBM), earlier)


def combine_kernel(expert_count, wide_ref, own_ref, back_ref, *refs):
    sums, out_ref = refs[:-1], refs[-1]
    half = out_ref.shape[1]
    other = lax.axis_index("role") ^ 1
    gate = decode_gate(wide_ref[:, half:].astype(jnp.float32), other, expert_count)
    slots = slot_matrix(gate)[:, : back_ref.shape[0]]
    width = 256
    for first in range(0, half, width):
        columns = slice(first, first + width)
        spread = jnp.dot(slots, back_ref[:, columns], preferred_element_type=jnp.float32)
        result = own_ref[:, columns] + gate * spread
        for ref in sums:
            result = result + ref[:, columns].astype(jnp.float32)
        out_ref[:, columns] = result.astype(jnp.bfloat16)


def combine(wide, own, back, sums, expert_count, last=False):
    rows, half = own.shape
    return call(
        functools.partial(combine_kernel, expert_count),
        (wide, own, back, *sums),
        ((rows, half),),
        2 * rows * LANES * half,
        "combine",
        last=last,
    )[0]


def swap(array, bits):
    count = lax.axis_size("role")
    return lax.ppermute(array, "role", [(device, device ^ bits) for device in range(count)])


def swap_core(array):
    return lax.ppermute(array, "tp", [(0, 1), (1, 0)])


def route_multicast(
    q_lat, latent_cache, lengths, placement, tokens, expert_ids, gate_weights, w_gate, w_up, w_down
):
    role_count = lax.axis_size("role")
    token_count, route_count = expert_ids.shape
    half = tokens.shape[1]
    capacity = 3 * token_count * route_count // (2 * role_count)
    pair, mirror, row = 2, 6, 1

    wide, cross = prepare(tokens, expert_ids, gate_weights, role_count, capacity)
    wide_mirror = swap(wide, mirror)
    wide_pair = swap(wide, pair)
    cross_in = swap(cross, row)
    wide_other = swap_core(wide)
    w_gate, w_up = w_gate[0], w_up[0]
    w_down, down_away = fetch(w_down, wide)
    attended = attend(after(q_lat, down_away), latent_cache, lengths, placement)
    cross_in = after(cross_in, attended)
    wide_pair = after(wide_pair, cross_in, wide_other)
    cross_pair = cross_rows(wide_pair, role_count, capacity)
    cross_pair_in = swap(cross_pair, row)
    wide_pair_other = swap_core(wide_pair)

    wide_mirror = after(wide_mirror, cross_pair)
    wide_far = swap(wide_mirror, pair)
    cross_mirror = cross_rows(wide_mirror, role_count, capacity)
    cross_mirror_in = swap(cross_mirror, row)
    wide_mirror_other = swap_core(wide_mirror)

    cross_pair_in = after(cross_pair_in, cross_mirror)
    cross_in_other = swap_core(cross_in)
    cross_pair_in_other = swap_core(cross_pair_in)

    wide_far = after(
        wide_far,
        wide_pair_other,
        wide_mirror_other,
        cross_in_other,
        cross_pair_in_other,
        cross_mirror_in,
    )
    cross_far = cross_rows(wide_far, role_count, capacity)
    cross_far_in = swap(cross_far, row)
    cross_mirror_in_other = swap_core(after(cross_mirror_in, cross_far))
    down_other = swap_core(after(down_away, cross_far))
    wide_far_other = swap_core(wide_far)
    hidden = hidden_units(
        [
            (wide, wide_other),
            (wide_pair, wide_pair_other),
            (wide_mirror, wide_mirror_other),
            (wide_far, wide_far_other),
            (cross_in, cross_in_other),
            (cross_pair_in, cross_pair_in_other),
            (cross_mirror_in, cross_mirror_in_other),
        ],
        w_gate,
        w_up,
    )
    hidden_other = swap_core(hidden)
    cross_far_in = after(cross_far_in, hidden)
    hidden_far = hidden_units([(cross_far_in, swap_core(cross_far_in))], w_gate, w_up)
    hidden_far_other = swap_core(hidden_far)
    (back_far,) = down(
        (), 1, hidden_far, hidden_far_other, w_down, down_other, capacity, role_count
    )
    blocks = (wide, wide_pair, wide_mirror, wide_far)
    own, own_pair, own_mirror, own_far, back, back_pair, back_mirror = down(
        blocks,
        3,
        hidden,
        after(hidden_other, back_far),
        w_down,
        down_other,
        capacity,
        role_count,
    )
    back_far = swap(back_far, row)
    back_mirror = swap(back_mirror, row)
    back_pair = swap(back_pair, row)
    back = swap(back, row)

    sum_far = combine(wide_far, own_far, back_far, (), role_count)
    from_far = swap(sum_far, pair)
    back_mirror = after(back_mirror, sum_far)
    sum_mirror = combine(wide_mirror, own_mirror, back_mirror, (from_far,), role_count)
    from_mirror = swap(sum_mirror, mirror)
    back_pair = after(back_pair, sum_mirror)
    sum_pair = combine(wide_pair, own_pair, back_pair, (), role_count)
    from_pair = swap(sum_pair, pair)
    back = after(back, sum_pair)
    moe_result = combine(
        wide, own, back, (from_pair, from_mirror), role_count, last=True
    )
    return (attended, moe_result)


def shards(
    q_lat, latent_cache, lengths, placement, tokens, expert_ids, gate_weights, w_gate, w_up, w_down
):
    if lax.axis_size("role") == 8 and lax.axis_size("tp") == 2:
        return route_multicast(
            q_lat,
            latent_cache,
            lengths,
            placement,
            tokens,
            expert_ids,
            gate_weights,
            w_gate,
            w_up,
            w_down,
        )
    attended = attend_local(q_lat, latent_cache, lengths, placement)
    routed = route_all_to_all(tokens, expert_ids, gate_weights, w_gate, w_up, w_down)
    return (attended, routed)


def solution(mesh):
    return jax.shard_map(
        shards,
        mesh=mesh,
        in_specs=(
            P(("groups", "role"), "tp", None),
            P(("groups", "role"), None, None),
            P("groups"),
            P("groups"),
            P(("groups", "role"), "tp"),
            P(("groups", "role"), None),
            P(("groups", "role"), None),
            P("role", None, "tp"),
            P("role", None, "tp"),
            P("role", "tp", None),
        ),
        out_specs=(P(("groups", "role"), "tp", None), P(("groups", "role"), "tp")),
        check_vma=False,
    )
```

```python
import functools

import jax
import jax.numpy as jnp
from jax import lax
from jax.experimental import pallas as pl
from jax.experimental.pallas import tpu as pltpu
from jax.sharding import PartitionSpec as P

KV_RANK = 512


score_scale = 192.0 ** (-0.5)


def attend_local(q_lat, latent_cache, lengths, placement):
    slot_count = q_lat.shape[0]
    offset = lax.axis_index("role") * slot_count
    slot_ids = offset + jnp.arange(slot_count, dtype=jnp.int32)
    matches = placement[None, :] == slot_ids[:, None]
    slot_length = jnp.sum(jnp.where(matches, lengths[None, :], 0), axis=1)
    scores = (
        jnp.einsum("shc,stc->sht", q_lat, latent_cache, preferred_element_type=jnp.float32)
        * score_scale
    )
    position = jnp.arange(latent_cache.shape[1], dtype=jnp.int32)
    visible = position[None, None, :] < slot_length[:, None, None]
    scores = jnp.where(visible, scores, -jnp.inf)
    highest = jnp.max(scores, axis=2, keepdims=True)
    raised = jnp.exp(scores - highest)
    attn_weights = (raised / jnp.sum(raised, axis=2, keepdims=True)).astype(jnp.bfloat16)
    values = latent_cache[:, :, :KV_RANK]
    return jnp.einsum(
        "sht,stc->shc", attn_weights, values, preferred_element_type=jnp.float32
    ).astype(jnp.bfloat16)


def route_all_to_all(tokens, expert_ids, gate_weights, w_gate, w_up, w_down):
    role_count = lax.axis_size("role")
    token_count = expert_ids.shape[0]
    route_count = expert_ids.shape[1]
    capacity = 3 * token_count * route_count // (2 * role_count)
    flat_ids = expert_ids.reshape(-1)
    onehot = (flat_ids[:, None] == jnp.arange(role_count, dtype=jnp.int32)[None, :]).astype(
        jnp.int32
    )
    earlier = jnp.cumsum(onehot, axis=0) - onehot
    slot_index = jnp.sum(earlier * onehot, axis=1)
    target = flat_ids * capacity + slot_index
    source = jnp.arange(token_count * route_count, dtype=jnp.int32) // route_count
    outgoing = lax.all_gather(tokens, "tp", axis=1, tiled=True)
    columns = outgoing.shape[1]
    buffer_rows = (
        jnp.zeros((role_count * capacity, columns), jnp.bfloat16).at[target].set(outgoing[source])
    )
    buffer_rows = buffer_rows.reshape(role_count, capacity, columns)
    gate_matrix = w_gate[0]
    up_matrix = w_up[0]
    down_matrix = w_down[0]
    received = lax.all_to_all(buffer_rows, "role", split_axis=0, concat_axis=0, tiled=True)
    item_count = received.shape[1]
    arrived = received.reshape(role_count * item_count, columns)
    gate_proj = jnp.dot(arrived, gate_matrix, preferred_element_type=jnp.float32)
    up_proj = jnp.dot(arrived, up_matrix, preferred_element_type=jnp.float32)
    expert_hidden = (jax.nn.silu(gate_proj) * up_proj).astype(jnp.bfloat16)
    partial_out = jnp.dot(expert_hidden, down_matrix, preferred_element_type=jnp.float32)
    summed = lax.psum_scatter(
        partial_out.astype(jnp.bfloat16), "tp", scatter_dimension=1, tiled=True
    )
    summed = summed.reshape(role_count, item_count, summed.shape[1])
    returned = lax.all_to_all(summed, "role", split_axis=0, concat_axis=0, tiled=True)
    half_width = returned.shape[2]
    flat_back = returned.reshape(role_count * capacity, half_width)
    chosen_rows = (
        flat_back[target].reshape(token_count, route_count, half_width).astype(jnp.float32)
    )
    moe_result = jnp.sum(chosen_rows * gate_weights[:, :, None], axis=1).astype(jnp.bfloat16)
    return moe_result


LANES = 128
VMEM_LIMIT = 16 * 1024 * 1024


def round_up(value, unit):
    return -(-value // unit) * unit


def call(kernel, operands, out_shapes, flops, name, scratch=(), types=None, last=False):
    place = pl.BlockSpec(memory_space=pltpu.VMEM)
    return pl.pallas_call(
        kernel,
        in_specs=[place] * len(operands),
        out_specs=[place] * len(out_shapes),
        out_shape=[
            (jax.ShapeDtypeStruct if last else pltpu.VMEM)(
                shape, jnp.bfloat16 if types is None else types[index]
            )
            for index, shape in enumerate(out_shapes)
        ],
        scratch_shapes=list(scratch),
        name=name,
        compiler_params=pltpu.CompilerParams(vmem_limit_bytes=VMEM_LIMIT),
        cost_estimate=pl.CostEstimate(flops=0, bytes_accessed=0, transcendentals=0),
    )(*[pltpu.with_memory_space_constraint(operand, pltpu.VMEM) for operand in operands])


def after(value, *earlier):
    return lax.optimization_barrier((value, *earlier))[0]


def lane_index(rows):
    return lax.broadcasted_iota(jnp.int32, (rows, LANES), 1)


def decode_gate(pieces, expert, expert_count):
    lane = lane_index(pieces.shape[0])
    wanted = lane == expert
    for piece in (1, 2):
        wanted = wanted | (lane == expert + piece * expert_count)
    return jnp.sum(jnp.where(wanted, pieces, 0.0), axis=1, keepdims=True)


def slot_matrix(gate):
    rows = gate.shape[0]
    named = jnp.broadcast_to((gate > 0.0).astype(jnp.float32), (rows, LANES))
    lower = lax.broadcasted_iota(jnp.int32, (rows, rows), 0) >= lax.broadcasted_iota(
        jnp.int32, (rows, rows), 1
    )
    rank = jnp.dot(
        lower.astype(jnp.bfloat16), named.astype(jnp.bfloat16), preferred_element_type=jnp.float32
    )
    slot = lane_index(rows).astype(jnp.float32)
    return jnp.where((named > 0.0) & (rank - 1.0 == slot), 1.0, 0.0).astype(jnp.bfloat16)


def compact(gate, rows_in, capacity):
    picked = lax.dot_general(
        slot_matrix(gate),
        rows_in,
        (((0,), (0,)), ((), ())),
        preferred_element_type=jnp.float32,
    )
    return picked[:capacity].astype(jnp.bfloat16)


def split_of(width):
    return round_up(3 * width // 4, LANES)


def prepare_kernel(
    expert_count,
    tokens_hbm,
    down_hbm,
    ids_ref,
    gates_ref,
    wide_ref,
    left_ref,
    right_ref,
    cross_ref,
    away_ref,
    sems,
):
    rows, half = tokens_hbm.shape
    copy = pltpu.make_async_copy(tokens_hbm, wide_ref.at[:, :half], sems.at[0])
    copy.start()
    sibling = pl.multiple_of((1 - lax.axis_index("tp")) * half, LANES)
    away = pltpu.make_async_copy(down_hbm.at[0, :, pl.ds(sibling, half)], away_ref, sems.at[1])
    away.start()
    piece_rows = round_up(3 * expert_count, 16)
    line = lax.broadcasted_iota(jnp.int32, (piece_rows, rows), 0)
    named = line
    for piece in (1, 2):
        named = jnp.where(line >= piece * expert_count, line - piece * expert_count, named)
    dense = jnp.zeros((piece_rows, rows), jnp.float32)
    for choice in range(ids_ref.shape[0]):
        dense = dense + jnp.where(
            ids_ref[choice : choice + 1, :] == named, gates_ref[choice : choice + 1, :], 0.0
        )
    high = dense.astype(jnp.bfloat16).astype(jnp.float32)
    middle = (dense - high).astype(jnp.bfloat16).astype(jnp.float32)
    low = dense - high - middle
    pieces = jnp.where(line < expert_count, high, jnp.where(line < 2 * expert_count, middle, low))
    unit = lax.broadcasted_iota(jnp.int32, (piece_rows, LANES), 0) == lax.broadcasted_iota(
        jnp.int32, (piece_rows, LANES), 1
    )
    turned = lax.dot_general(
        pieces.astype(jnp.bfloat16),
        unit.astype(jnp.bfloat16),
        (((0,), (0,)), ((), ())),
        preferred_element_type=jnp.float32,
    )
    wide_ref[:, half:] = turned.astype(jnp.bfloat16)
    copy.wait()
    split = left_ref.shape[1]
    left_ref[...] = wide_ref[:, :split]
    right_ref[...] = wide_ref[:, split:]
    gate = decode_gate(turned, lax.axis_index("role") ^ 1, expert_count)
    cross_ref[...] = compact(gate, wide_ref[:, :half], cross_ref.shape[0])
    away.wait()


def prepare(tokens, w_down, expert_ids, gate_weights, expert_count, capacity):
    rows, half = tokens.shape
    split = split_of(half)
    shapes = [
        (rows, half + LANES),
        (rows, split),
        (rows, half + LANES - split),
        (capacity, half),
        (w_down.shape[1], half),
    ]
    whole = pl.BlockSpec(memory_space=pltpu.VMEM)
    return pl.pallas_call(
        functools.partial(prepare_kernel, expert_count),
        in_specs=[pl.BlockSpec(memory_space=pltpu.HBM)] * 2 + [whole, whole],
        out_specs=[whole] * len(shapes),
        out_shape=[pltpu.VMEM(shape, jnp.bfloat16) for shape in shapes],
        scratch_shapes=[pltpu.SemaphoreType.DMA((2,))],
        name="prepare",
        compiler_params=pltpu.CompilerParams(vmem_limit_bytes=VMEM_LIMIT),
        cost_estimate=pl.CostEstimate(flops=0, bytes_accessed=0, transcendentals=0),
    )(
        pltpu.with_memory_space_constraint(tokens, pltpu.HBM),
        pltpu.with_memory_space_constraint(w_down, pltpu.HBM),
        expert_ids.T,
        gate_weights.T,
    )


def cross_kernel(expert_count, wide_ref, cross_ref):
    half = cross_ref.shape[1]
    other = lax.axis_index("role") ^ 1
    gate = decode_gate(wide_ref[:, half:].astype(jnp.float32), other, expert_count)
    cross_ref[...] = compact(gate, wide_ref[:, :half], cross_ref.shape[0])


def cross_rows(wide, expert_count, capacity):
    rows, width = wide.shape
    half = width - LANES
    return call(
        functools.partial(cross_kernel, expert_count),
        (wide,),
        ((capacity, half),),
        2 * rows * LANES * half,
        "cross_rows",
    )[0]


def joined_cross_kernel(expert_count, left_ref, right_ref, wide_ref, cross_ref):
    split = left_ref.shape[1]
    wide_ref[:, :split] = left_ref[...]
    wide_ref[:, split:] = right_ref[...]
    cross_kernel(expert_count, wide_ref, cross_ref)


def joined_cross_rows(left, right, expert_count, capacity):
    rows, width = left.shape[0], left.shape[1] + right.shape[1]
    half = width - LANES
    return call(
        functools.partial(joined_cross_kernel, expert_count),
        (left, right),
        ((rows, width), (capacity, half)),
        2 * rows * LANES * half,
        "joined_cross_rows",
    )


def row_starts(blocks):
    starts, rows = [], 0
    for block in blocks:
        starts.append(rows)
        rows += round_up(block.shape[0], 16)
    return tuple(starts), rows


def pack_kernel(starts, *refs):
    out_ref = refs[-1]
    for start, ref in zip(starts, refs):
        out_ref[start : start + ref.shape[0], :] = ref[:, : out_ref.shape[1]]


def pack(blocks, half):
    starts, rows = row_starts(blocks)
    return call(
        functools.partial(pack_kernel, starts), blocks, ((rows, half),), 0, "pack_rows"
    )[0]


def hidden_kernel(near_ref, far_ref, gate_ref, up_ref, hidden_ref):
    half = near_ref.shape[1]
    core = lax.axis_index("tp")
    own = pl.ds(pl.multiple_of(core * half, LANES), half)
    sibling = pl.ds(pl.multiple_of((1 - core) * half, LANES), half)
    width = 256
    for first in range(0, hidden_ref.shape[1], width):
        units = slice(first, first + width)
        gate_proj, up_proj = (
            jnp.dot(near_ref[...], ref[own, units], preferred_element_type=jnp.float32)
            + jnp.dot(far_ref[...], ref[sibling, units], preferred_element_type=jnp.float32)
            for ref in (gate_ref, up_ref)
        )
        hidden_ref[:, units] = (jax.nn.silu(gate_proj) * up_proj).astype(jnp.bfloat16)


def hidden_units(near, far, w_gate, w_up):
    return call(
        hidden_kernel,
        (near, far, w_gate, w_up),
        ((near.shape[0], w_gate.shape[1]),),
        0,
        "hidden_units",
    )[0]


def down_kernel(expert_count, starts, wide_count, *refs):
    wides = refs[:wide_count]
    own_ref, other_ref, down_ref, down_other_ref = refs[wide_count : wide_count + 4]
    outs = refs[wide_count + 4 :]
    half = down_other_ref.shape[1]
    me = lax.axis_index("role")
    base = pl.multiple_of(lax.axis_index("tp") * half, LANES)
    gates = [decode_gate(ref[:, half:].astype(jnp.float32), me, expert_count) for ref in wides]
    width = 256
    for first in range(0, half, width):
        columns = slice(first, first + width)
        result = jnp.dot(
            own_ref[...],
            down_ref[0, :, pl.ds(pl.multiple_of(base + first, LANES), width)],
            preferred_element_type=jnp.float32,
        ) + jnp.dot(
            other_ref[...], down_other_ref[:, columns], preferred_element_type=jnp.float32
        )
        for index, (start, out_ref) in enumerate(zip(starts, outs)):
            block = result[start : start + out_ref.shape[0]].astype(jnp.bfloat16)
            if index < wide_count:
                block = gates[index] * block.astype(jnp.float32)
            out_ref[:, columns] = block


def down(wides, cross_count, hidden, hidden_other, w_down, down_other, capacity, expert_count):
    half = down_other.shape[1]
    shapes = [(wide.shape[0], half) for wide in wides] + [(capacity, half)] * cross_count
    starts, rows = [], 0
    for shape in shapes:
        starts.append(rows)
        rows += round_up(shape[0], 16)
    return call(
        functools.partial(down_kernel, expert_count, tuple(starts), len(wides)),
        (*wides, hidden, hidden_other, w_down, down_other),
        tuple(shapes),
        4 * rows * half * hidden.shape[1],
        "down",
        (),
        [jnp.float32] * len(wides) + [jnp.bfloat16] * cross_count,
    )


def attend_kernel(query_ref, latent_ref, lengths_ref, placement_ref, out_ref):
    slot_count, head_count, _ = query_ref.shape
    rank, context = out_ref.shape[2], latent_ref.shape[2]
    first = lax.axis_index("role") * slot_count
    position = lax.broadcasted_iota(jnp.int32, (head_count, context), 1)
    for slot in range(slot_count):
        here = placement_ref[...] == first + slot
        length = jnp.sum(jnp.where(here, lengths_ref[...], 0), axis=1, keepdims=True)
        scores = (
            jnp.dot(query_ref[slot], latent_ref[slot], preferred_element_type=jnp.float32)
            * score_scale
        )
        scores = jnp.where(position < length, scores, -jnp.inf)
        raised = jnp.exp(scores - jnp.max(scores, axis=1, keepdims=True))
        attn_weights = (raised / jnp.sum(raised, axis=1, keepdims=True)).astype(jnp.bfloat16)
        out_ref[slot] = lax.dot_general(
            attn_weights,
            latent_ref[slot, :rank, :],
            (((1,), (1,)), ((), ())),
            preferred_element_type=jnp.float32,
        ).astype(jnp.bfloat16)


def attend(q_lat, latent_cache, lengths, placement):
    slot_count, head_count, _ = q_lat.shape
    return pl.pallas_call(
        attend_kernel,
        out_shape=jax.ShapeDtypeStruct((slot_count, head_count, KV_RANK), jnp.bfloat16),
        name="attend",
        compiler_params=pltpu.CompilerParams(vmem_limit_bytes=VMEM_LIMIT),
        cost_estimate=pl.CostEstimate(flops=0, bytes_accessed=0, transcendentals=0),
    )(q_lat, latent_cache.transpose(0, 2, 1), lengths[None, :], placement[None, :])


def combine_kernel(expert_count, first, sum_count, wide_ref, own_ref, back_ref, *refs):
    sums, outs = refs[:sum_count], refs[sum_count:]
    half = own_ref.shape[1]
    other = lax.axis_index("role") ^ 1
    gate = decode_gate(wide_ref[:, half:].astype(jnp.float32), other, expert_count)
    slots = slot_matrix(gate)[:, : back_ref.shape[0]]
    width = LANES
    for out_ref in outs:
        for column in range(0, out_ref.shape[1], width):
            columns = slice(first + column, first + column + width)
            spread = jnp.dot(slots, back_ref[:, columns], preferred_element_type=jnp.float32)
            result = own_ref[:, columns] + gate * spread
            for ref in sums:
                result = result + ref[:, column : column + width].astype(jnp.float32)
            out_ref[:, column : column + width] = result.astype(out_ref.dtype)
        first += out_ref.shape[1]


def combine(wide, own, back, sums, expert_count, first, widths, dtype=jnp.bfloat16):
    rows = own.shape[0]
    return call(
        functools.partial(combine_kernel, expert_count, first, len(sums)),
        (wide, own, back, *sums),
        tuple((rows, width) for width in widths),
        0,
        "combine",
        types=(dtype,) * len(widths),
    )


def add_kernel(*refs):
    out_ref = refs[-1]
    count = len(refs) // 2
    first = 0
    for total_ref, part_ref in zip(refs[:count], refs[count:-1]):
        result = total_ref[...] + part_ref[...].astype(jnp.float32)
        out_ref[:, first : first + part_ref.shape[1]] = result.astype(jnp.bfloat16)
        first += part_ref.shape[1]


def add_last(totals, parts):
    shape = (parts[0].shape[0], sum(part.shape[1] for part in parts))
    return call(add_kernel, (*totals, *parts), (shape,), 0, "add_last", last=True)[0]


def swap(array, bits):
    count = lax.axis_size("role")
    return lax.ppermute(array, "role", [(device, device ^ bits) for device in range(count)])


def swap_core(array):
    return lax.ppermute(array, "tp", [(0, 1), (1, 0)])


def route_multicast(
    q_lat, latent_cache, lengths, placement, tokens, expert_ids, gate_weights, w_gate, w_up, w_down
):
    role_count = lax.axis_size("role")
    token_count, route_count = expert_ids.shape
    half = tokens.shape[1]
    capacity = 3 * token_count * route_count // (2 * role_count)
    pair, mirror, row = 2, 6, 1

    wide, own_left, own_right, cross, down_away = prepare(
        tokens, w_down, expert_ids, gate_weights, role_count, capacity
    )
    mirror_left = swap(own_left, mirror)
    mirror_right = swap(own_right, mirror)
    wide_pair = swap(wide, pair)
    cross_in = swap(cross, row)
    w_gate, w_up = w_gate[0], w_up[0]
    down_other = swap_core(down_away)
    attended = attend(after(q_lat, wide), latent_cache, lengths, placement)
    cross_in = after(cross_in, attended)
    mirror_left = after(mirror_left, cross_in, down_other)
    far_left = swap(mirror_left, pair)
    wide_pair = after(wide_pair, mirror_left)
    cross_pair = cross_rows(wide_pair, role_count, capacity)
    cross_pair_in = swap(cross_pair, row)
    mirror_right = after(mirror_right, cross_pair)
    far_right = swap(mirror_right, pair)
    wide_mirror, cross_mirror = joined_cross_rows(
        mirror_left, mirror_right, role_count, capacity
    )
    cross_mirror_in = swap(cross_mirror, row)
    cross_pair_in = after(cross_pair_in, cross_mirror)
    far_left = after(far_left, cross_pair_in)
    far_right = after(far_right, far_left)
    cross_mirror_in = after(cross_mirror_in, far_right)
    far_right = after(far_right, cross_mirror_in)
    wide_far, cross_far = joined_cross_rows(far_left, far_right, role_count, capacity)
    cross_far_in = swap(cross_far, row)
    near_first = pack((after(wide, cross_far), wide_pair, wide_mirror, cross_in), half)
    far_first = swap_core(near_first)
    near_second = pack((wide_far, cross_pair_in, cross_mirror_in), half)
    far_second = swap_core(near_second)
    hidden = hidden_units(near_first, after(far_first, near_second), w_gate, w_up)
    hidden_other = swap_core(hidden)
    cross_far_in = after(cross_far_in, hidden)
    hidden_second = hidden_units(near_second, after(far_second, cross_far_in), w_gate, w_up)
    hidden_second_other = swap_core(hidden_second)
    far_third = swap_core(cross_far_in)
    far_third = after(far_third, hidden_second)
    hidden_third = hidden_units(cross_far_in, far_third, w_gate, w_up)
    hidden_third_other = swap_core(hidden_third)
    (back_far,) = down(
        (), 1, hidden_third, hidden_third_other, w_down, down_other, capacity, role_count
    )
    own, own_pair, own_mirror, back_own = down(
        (wide, wide_pair, wide_mirror),
        1,
        hidden,
        after(hidden_other, back_far),
        w_down,
        down_other,
        capacity,
        role_count,
    )
    own_far, back_pair, back_mirror = down(
        (wide_far,),
        2,
        hidden_second,
        after(hidden_second_other, back_far),
        w_down,
        down_other,
        capacity,
        role_count,
    )
    back_far = swap(back_far, row)
    back_mirror = swap(back_mirror, row)
    back_pair = swap(back_pair, row)
    back_own = swap(back_own, row)

    split = half // 2
    widths = (split, half - split)
    back_far = after(back_far, own, own_far)
    sum_far_left, sum_far_right = combine(
        wide_far, own_far, back_far, (), role_count, 0, widths
    )
    from_far_left = swap(sum_far_left, pair)
    from_far_right = swap(sum_far_right, pair)
    back_mirror = after(back_mirror, sum_far_left)
    from_far_left = after(from_far_left, back_mirror)
    (sum_mirror_left,) = combine(
        wide_mirror, own_mirror, back_mirror, (from_far_left,), role_count, 0, widths[:1]
    )
    from_mirror_left = swap(sum_mirror_left, mirror)
    from_far_right = after(from_far_right, sum_mirror_left)
    (sum_mirror_right,) = combine(
        wide_mirror, own_mirror, back_mirror, (from_far_right,), role_count, split, widths[1:]
    )
    from_mirror_right = swap(sum_mirror_right, mirror)
    back_pair = after(back_pair, sum_mirror_right)
    sum_pair_left, sum_pair_right = combine(
        wide_pair, own_pair, back_pair, (), role_count, 0, widths
    )
    from_pair_left = swap(sum_pair_left, pair)
    from_pair_right = swap(sum_pair_right, pair)
    back_own = after(back_own, sum_pair_left)
    from_mirror_left = after(from_mirror_left, back_own)
    (sum_left,) = combine(
        wide, own, back_own, (from_mirror_left,), role_count, 0, widths[:1], jnp.float32
    )
    from_mirror_right = after(from_mirror_right, sum_left)
    (sum_right,) = combine(
        wide, own, back_own, (from_mirror_right,), role_count, split, widths[1:], jnp.float32
    )
    from_pair_left = after(from_pair_left, sum_right)
    moe_result = add_last((sum_left, sum_right), (from_pair_left, from_pair_right))
    return (attended, moe_result)


def shards(
    q_lat, latent_cache, lengths, placement, tokens, expert_ids, gate_weights, w_gate, w_up, w_down
):
    if lax.axis_size("role") == 8 and lax.axis_size("tp") == 2:
        return route_multicast(
            q_lat,
            latent_cache,
            lengths,
            placement,
            tokens,
            expert_ids,
            gate_weights,
            w_gate,
            w_up,
            w_down,
        )
    attended = attend_local(q_lat, latent_cache, lengths, placement)
    routed = route_all_to_all(tokens, expert_ids, gate_weights, w_gate, w_up, w_down)
    return (attended, routed)


def solution(mesh):
    return jax.shard_map(
        shards,
        mesh=mesh,
        in_specs=(
            P(("groups", "role"), "tp", None),
            P(("groups", "role"), None, None),
            P("groups"),
            P("groups"),
            P(("groups", "role"), "tp"),
            P(("groups", "role"), None),
            P(("groups", "role"), None),
            P("role", None, "tp"),
            P("role", None, "tp"),
            P("role", "tp", None),
        ),
        out_specs=(P(("groups", "role"), "tp", None), P(("groups", "role"), "tp")),
        check_vma=False,
    )
```

```python
import functools

import jax
import jax.numpy as jnp
from jax import lax
from jax.experimental import pallas as pl
from jax.experimental.pallas import tpu as pltpu
from jax.sharding import PartitionSpec as P

KV_RANK = 512


score_scale = 192.0 ** (-0.5)


def attend_local(q_lat, latent_cache, lengths, placement):
    slot_count = q_lat.shape[0]
    offset = lax.axis_index("role") * slot_count
    slot_ids = offset + jnp.arange(slot_count, dtype=jnp.int32)
    matches = placement[None, :] == slot_ids[:, None]
    slot_length = jnp.sum(jnp.where(matches, lengths[None, :], 0), axis=1)
    scores = (
        jnp.einsum("shc,stc->sht", q_lat, latent_cache, preferred_element_type=jnp.float32)
        * score_scale
    )
    position = jnp.arange(latent_cache.shape[1], dtype=jnp.int32)
    visible = position[None, None, :] < slot_length[:, None, None]
    scores = jnp.where(visible, scores, -jnp.inf)
    highest = jnp.max(scores, axis=2, keepdims=True)
    raised = jnp.exp(scores - highest)
    attn_weights = (raised / jnp.sum(raised, axis=2, keepdims=True)).astype(jnp.bfloat16)
    values = latent_cache[:, :, :KV_RANK]
    return jnp.einsum(
        "sht,stc->shc", attn_weights, values, preferred_element_type=jnp.float32
    ).astype(jnp.bfloat16)


def route_all_to_all(tokens, expert_ids, gate_weights, w_gate, w_up, w_down):
    role_count = lax.axis_size("role")
    token_count = expert_ids.shape[0]
    route_count = expert_ids.shape[1]
    capacity = 3 * token_count * route_count // (2 * role_count)
    flat_ids = expert_ids.reshape(-1)
    onehot = (flat_ids[:, None] == jnp.arange(role_count, dtype=jnp.int32)[None, :]).astype(
        jnp.int32
    )
    earlier = jnp.cumsum(onehot, axis=0) - onehot
    slot_index = jnp.sum(earlier * onehot, axis=1)
    target = flat_ids * capacity + slot_index
    source = jnp.arange(token_count * route_count, dtype=jnp.int32) // route_count
    outgoing = lax.all_gather(tokens, "tp", axis=1, tiled=True)
    columns = outgoing.shape[1]
    buffer_rows = (
        jnp.zeros((role_count * capacity, columns), jnp.bfloat16).at[target].set(outgoing[source])
    )
    buffer_rows = buffer_rows.reshape(role_count, capacity, columns)
    gate_matrix = w_gate[0]
    up_matrix = w_up[0]
    down_matrix = w_down[0]
    received = lax.all_to_all(buffer_rows, "role", split_axis=0, concat_axis=0, tiled=True)
    item_count = received.shape[1]
    arrived = received.reshape(role_count * item_count, columns)
    gate_proj = jnp.dot(arrived, gate_matrix, preferred_element_type=jnp.float32)
    up_proj = jnp.dot(arrived, up_matrix, preferred_element_type=jnp.float32)
    expert_hidden = (jax.nn.silu(gate_proj) * up_proj).astype(jnp.bfloat16)
    partial_out = jnp.dot(expert_hidden, down_matrix, preferred_element_type=jnp.float32)
    summed = lax.psum_scatter(
        partial_out.astype(jnp.bfloat16), "tp", scatter_dimension=1, tiled=True
    )
    summed = summed.reshape(role_count, item_count, summed.shape[1])
    returned = lax.all_to_all(summed, "role", split_axis=0, concat_axis=0, tiled=True)
    half_width = returned.shape[2]
    flat_back = returned.reshape(role_count * capacity, half_width)
    chosen_rows = (
        flat_back[target].reshape(token_count, route_count, half_width).astype(jnp.float32)
    )
    moe_result = jnp.sum(chosen_rows * gate_weights[:, :, None], axis=1).astype(jnp.bfloat16)
    return moe_result


LANES = 128
VMEM_LIMIT = 16 * 1024 * 1024


def round_up(value, unit):
    return -(-value // unit) * unit


def call(kernel, operands, out_shapes, flops, name, scratch=(), types=None, last=False, hint=0):
    place = pl.BlockSpec(memory_space=pltpu.VMEM)
    return pl.pallas_call(
        kernel,
        in_specs=[place] * len(operands),
        out_specs=[place] * len(out_shapes),
        out_shape=[
            (jax.ShapeDtypeStruct if last else pltpu.VMEM)(
                shape, jnp.bfloat16 if types is None else types[index]
            )
            for index, shape in enumerate(out_shapes)
        ],
        scratch_shapes=list(scratch),
        name=name,
        compiler_params=pltpu.CompilerParams(vmem_limit_bytes=VMEM_LIMIT),
        cost_estimate=pl.CostEstimate(flops=hint, bytes_accessed=0, transcendentals=0),
    )(*[pltpu.with_memory_space_constraint(operand, pltpu.VMEM) for operand in operands])


def after(value, *earlier):
    return lax.optimization_barrier((value, *earlier))[0]


def lane_index(rows):
    return lax.broadcasted_iota(jnp.int32, (rows, LANES), 1)


def decode_gate(pieces, expert, expert_count):
    lane = lane_index(pieces.shape[0])
    wanted = lane == expert
    for piece in (1, 2):
        wanted = wanted | (lane == expert + piece * expert_count)
    return jnp.sum(jnp.where(wanted, pieces, 0.0), axis=1, keepdims=True)


def slot_matrix(gate):
    rows = gate.shape[0]
    named = jnp.broadcast_to((gate > 0.0).astype(jnp.float32), (rows, LANES))
    lower = lax.broadcasted_iota(jnp.int32, (rows, rows), 0) >= lax.broadcasted_iota(
        jnp.int32, (rows, rows), 1
    )
    rank = jnp.dot(
        lower.astype(jnp.bfloat16), named.astype(jnp.bfloat16), preferred_element_type=jnp.float32
    )
    slot = lane_index(rows).astype(jnp.float32)
    return jnp.where((named > 0.0) & (rank - 1.0 == slot), 1.0, 0.0).astype(jnp.bfloat16)


def compact(gate, rows_in, capacity):
    picked = lax.dot_general(
        slot_matrix(gate),
        rows_in,
        (((0,), (0,)), ((), ())),
        preferred_element_type=jnp.float32,
    )
    return picked[:capacity].astype(jnp.bfloat16)


def prepare_kernel(
    expert_count,
    tokens_hbm,
    down_hbm,
    ids_ref,
    gates_ref,
    wide_ref,
    cross_ref,
    away_ref,
    sems,
):
    rows, half = tokens_hbm.shape
    copy = pltpu.make_async_copy(tokens_hbm, wide_ref.at[:, :half], sems.at[0])
    copy.start()
    sibling = pl.multiple_of((1 - lax.axis_index("tp")) * half, LANES)
    away = pltpu.make_async_copy(down_hbm.at[0, :, pl.ds(sibling, half)], away_ref, sems.at[1])
    away.start()
    piece_rows = round_up(3 * expert_count, 16)
    line = lax.broadcasted_iota(jnp.int32, (piece_rows, rows), 0)
    named = line
    for piece in (1, 2):
        named = jnp.where(line >= piece * expert_count, line - piece * expert_count, named)
    dense = jnp.zeros((piece_rows, rows), jnp.float32)
    for choice in range(ids_ref.shape[0]):
        dense = dense + jnp.where(
            ids_ref[choice : choice + 1, :] == named, gates_ref[choice : choice + 1, :], 0.0
        )
    high = dense.astype(jnp.bfloat16).astype(jnp.float32)
    middle = (dense - high).astype(jnp.bfloat16).astype(jnp.float32)
    low = dense - high - middle
    pieces = jnp.where(line < expert_count, high, jnp.where(line < 2 * expert_count, middle, low))
    unit = lax.broadcasted_iota(jnp.int32, (piece_rows, LANES), 0) == lax.broadcasted_iota(
        jnp.int32, (piece_rows, LANES), 1
    )
    turned = lax.dot_general(
        pieces.astype(jnp.bfloat16),
        unit.astype(jnp.bfloat16),
        (((0,), (0,)), ((), ())),
        preferred_element_type=jnp.float32,
    )
    wide_ref[:, half:] = turned.astype(jnp.bfloat16)
    copy.wait()
    gate = decode_gate(turned, lax.axis_index("role") ^ 1, expert_count)
    cross_ref[...] = compact(gate, wide_ref[:, :half], cross_ref.shape[0])
    away.wait()


def prepare(tokens, w_down, expert_ids, gate_weights, expert_count, capacity):
    rows, half = tokens.shape
    shapes = [
        (rows, half + LANES),
        (capacity, half),
        (w_down.shape[1], half),
    ]
    whole = pl.BlockSpec(memory_space=pltpu.VMEM)
    return pl.pallas_call(
        functools.partial(prepare_kernel, expert_count),
        in_specs=[pl.BlockSpec(memory_space=pltpu.HBM)] * 2 + [whole, whole],
        out_specs=[whole] * len(shapes),
        out_shape=[pltpu.VMEM(shape, jnp.bfloat16) for shape in shapes],
        scratch_shapes=[pltpu.SemaphoreType.DMA((2,))],
        name="prepare",
        compiler_params=pltpu.CompilerParams(vmem_limit_bytes=VMEM_LIMIT),
        cost_estimate=pl.CostEstimate(flops=0, bytes_accessed=0, transcendentals=0),
    )(
        pltpu.with_memory_space_constraint(tokens, pltpu.HBM),
        pltpu.with_memory_space_constraint(w_down, pltpu.HBM),
        expert_ids.T,
        gate_weights.T,
    )


def cross_kernel(expert_count, wide_ref, cross_ref):
    half = cross_ref.shape[1]
    other = lax.axis_index("role") ^ 1
    gate = decode_gate(wide_ref[:, half:].astype(jnp.float32), other, expert_count)
    cross_ref[...] = compact(gate, wide_ref[:, :half], cross_ref.shape[0])


def cross_rows(wide, expert_count, capacity):
    rows, width = wide.shape
    half = width - LANES
    return call(
        functools.partial(cross_kernel, expert_count),
        (wide,),
        ((capacity, half),),
        2 * rows * LANES * half,
        "cross_rows",
    )[0]


def is_inner():
    place = lax.axis_index("role") // 2
    return (place == 1) | (place == 2)


def picked_cross_kernel(expert_count, inner_ref, outer_ref, wide_ref, cross_ref):
    inner = is_inner()

    @pl.when(inner)
    def _():
        wide_ref[...] = inner_ref[...]

    @pl.when(jnp.logical_not(inner))
    def _():
        wide_ref[...] = outer_ref[...]

    cross_kernel(expert_count, wide_ref, cross_ref)


def picked_cross_rows(inner, outer, expert_count, capacity, hint=0):
    rows, width = inner.shape
    return call(
        functools.partial(picked_cross_kernel, expert_count),
        (inner, outer),
        ((rows, width), (capacity, width - LANES)),
        0,
        "picked_cross_rows",
        hint=hint,
    )


def row_starts(blocks):
    starts, rows = [], 0
    for block in blocks:
        starts.append(rows)
        rows += round_up(block.shape[0], 16)
    return tuple(starts), rows


def pack_kernel(starts, *refs):
    out_ref = refs[-1]
    for start, ref in zip(starts, refs):
        out_ref[start : start + ref.shape[0], :] = ref[:, : out_ref.shape[1]]


def pack(blocks, half):
    starts, rows = row_starts(blocks)
    return call(
        functools.partial(pack_kernel, starts), blocks, ((rows, half),), 0, "pack_rows"
    )[0]


def hidden_kernel(near_ref, far_ref, gate_ref, up_ref, hidden_ref):
    half = near_ref.shape[1]
    core = lax.axis_index("tp")
    own = pl.ds(pl.multiple_of(core * half, LANES), half)
    sibling = pl.ds(pl.multiple_of((1 - core) * half, LANES), half)
    width = 256
    for first in range(0, hidden_ref.shape[1], width):
        units = slice(first, first + width)
        gate_proj, up_proj = (
            jnp.dot(near_ref[...], ref[own, units], preferred_element_type=jnp.float32)
            + jnp.dot(far_ref[...], ref[sibling, units], preferred_element_type=jnp.float32)
            for ref in (gate_ref, up_ref)
        )
        hidden_ref[:, units] = (jax.nn.silu(gate_proj) * up_proj).astype(jnp.bfloat16)


def hidden_units(near, far, w_gate, w_up):
    return call(
        hidden_kernel,
        (near, far, w_gate, w_up),
        ((near.shape[0], w_gate.shape[1]),),
        0,
        "hidden_units",
    )[0]


def down_kernel(expert_count, starts, wide_count, *refs):
    wides = refs[:wide_count]
    own_ref, other_ref, down_ref, down_other_ref = refs[wide_count : wide_count + 4]
    outs = refs[wide_count + 4 :]
    half = down_other_ref.shape[1]
    me = lax.axis_index("role")
    base = pl.multiple_of(lax.axis_index("tp") * half, LANES)
    gates = [decode_gate(ref[:, half:].astype(jnp.float32), me, expert_count) for ref in wides]
    width = 256
    for first in range(0, half, width):
        columns = slice(first, first + width)
        result = jnp.dot(
            own_ref[...],
            down_ref[0, :, pl.ds(pl.multiple_of(base + first, LANES), width)],
            preferred_element_type=jnp.float32,
        ) + jnp.dot(
            other_ref[...], down_other_ref[:, columns], preferred_element_type=jnp.float32
        )
        for index, (start, out_ref) in enumerate(zip(starts, outs)):
            block = result[start : start + out_ref.shape[0]].astype(jnp.bfloat16)
            if index < wide_count:
                block = gates[index] * block.astype(jnp.float32)
            out_ref[:, columns] = block


def down(wides, cross_count, hidden, hidden_other, w_down, down_other, capacity, expert_count):
    half = down_other.shape[1]
    shapes = [(wide.shape[0], half) for wide in wides] + [(capacity, half)] * cross_count
    starts, rows = [], 0
    for shape in shapes:
        starts.append(rows)
        rows += round_up(shape[0], 16)
    return call(
        functools.partial(down_kernel, expert_count, tuple(starts), len(wides)),
        (*wides, hidden, hidden_other, w_down, down_other),
        tuple(shapes),
        4 * rows * half * hidden.shape[1],
        "down",
        (),
        [jnp.float32] * len(wides) + [jnp.bfloat16] * cross_count,
    )


def attend_kernel(query_ref, latent_ref, lengths_ref, placement_ref, out_ref):
    slot_count, head_count, _ = query_ref.shape
    rank, context = out_ref.shape[2], latent_ref.shape[2]
    first = lax.axis_index("role") * slot_count
    position = lax.broadcasted_iota(jnp.int32, (head_count, context), 1)
    for slot in range(slot_count):
        here = placement_ref[...] == first + slot
        length = jnp.sum(jnp.where(here, lengths_ref[...], 0), axis=1, keepdims=True)
        scores = (
            jnp.dot(query_ref[slot], latent_ref[slot], preferred_element_type=jnp.float32)
            * score_scale
        )
        scores = jnp.where(position < length, scores, -jnp.inf)
        raised = jnp.exp(scores - jnp.max(scores, axis=1, keepdims=True))
        attn_weights = (raised / jnp.sum(raised, axis=1, keepdims=True)).astype(jnp.bfloat16)
        out_ref[slot] = lax.dot_general(
            attn_weights,
            latent_ref[slot, :rank, :],
            (((1,), (1,)), ((), ())),
            preferred_element_type=jnp.float32,
        ).astype(jnp.bfloat16)


def attend(q_lat, latent_cache, lengths, placement):
    slot_count, head_count, _ = q_lat.shape
    return pl.pallas_call(
        attend_kernel,
        out_shape=jax.ShapeDtypeStruct((slot_count, head_count, KV_RANK), jnp.bfloat16),
        name="attend",
        compiler_params=pltpu.CompilerParams(vmem_limit_bytes=VMEM_LIMIT),
        cost_estimate=pl.CostEstimate(flops=0, bytes_accessed=0, transcendentals=0),
    )(q_lat, latent_cache.transpose(0, 2, 1), lengths[None, :], placement[None, :])


def combine_kernel(expert_count, sum_count, wide_ref, own_ref, back_ref, *refs):
    sums, outs = refs[:sum_count], refs[sum_count:]
    half = own_ref.shape[1]
    other = lax.axis_index("role") ^ 1
    gate = decode_gate(wide_ref[:, half:].astype(jnp.float32), other, expert_count)
    slots = slot_matrix(gate)[:, : back_ref.shape[0]]
    width = 256
    for first in range(0, half, width):
        columns = slice(first, first + width)
        spread = jnp.dot(slots, back_ref[:, columns], preferred_element_type=jnp.float32)
        result = own_ref[:, columns] + gate * spread
        for ref in sums:
            result = result + ref[:, columns].astype(jnp.float32)
        for out_ref in outs:
            out_ref[:, columns] = result.astype(out_ref.dtype)


def combine(wide, own, back, sums, expert_count, types, hint=0):
    return call(
        functools.partial(combine_kernel, expert_count, len(sums)),
        (wide, own, back, *sums),
        (own.shape,) * len(types),
        0,
        "combine",
        types=types,
        hint=hint,
    )


def add_kernel(*refs):
    out_ref = refs[-1]
    result = refs[0][...]
    for ref in refs[1:-1]:
        result = result + ref[...].astype(jnp.float32)
    out_ref[...] = result.astype(out_ref.dtype)


def add_all(total, parts, last=False):
    return call(add_kernel, (total, *parts), (total.shape,), 0, "add_all", last=last)[0]


def swap(array, bits, places=(0, 1, 2, 3)):
    count = lax.axis_size("role")
    pairs = [(device, device ^ bits) for device in range(count) if device // 2 in places]
    return lax.ppermute(array, "role", pairs)


def swap_core(array):
    return lax.ppermute(array, "tp", [(0, 1), (1, 0)])


def route_multicast(
    q_lat, latent_cache, lengths, placement, tokens, expert_ids, gate_weights, w_gate, w_up, w_down
):
    role_count = lax.axis_size("role")
    token_count, route_count = expert_ids.shape
    half = tokens.shape[1]
    capacity = 3 * token_count * route_count // (2 * role_count)
    pair, mirror, row = 2, 6, 1
    inner, outer = (1, 2), (0, 3)
    narrow, exact = jnp.bfloat16, jnp.float32

    wide, cross, down_away = prepare(
        tokens, w_down, expert_ids, gate_weights, role_count, capacity
    )
    wide_pair = swap(wide, pair)
    mirror_inner = swap(wide, mirror, inner)
    mirror_outer = swap(wide, mirror, outer)
    cross_in = swap(cross, row)
    w_gate, w_up = w_gate[0], w_up[0]
    down_other = swap_core(down_away)
    attended = attend(after(q_lat, wide), latent_cache, lengths, placement)
    cross_in = after(cross_in, attended)
    wide_pair = after(wide_pair, cross_in, down_other)
    cross_pair = cross_rows(wide_pair, role_count, capacity)
    cross_pair_in = swap(cross_pair, row)
    far_inner = swap(wide_pair, mirror, inner)
    mirror_inner = after(mirror_inner, cross_pair)
    far_outer = swap(mirror_inner, pair, inner)
    mirror_outer = after(mirror_outer, mirror_inner)
    mirror_outer = after(mirror_outer, cross_pair_in)
    wide_mirror, cross_mirror = picked_cross_rows(
        mirror_inner, mirror_outer, role_count, capacity
    )
    cross_mirror_in = swap(cross_mirror, row)
    near_first = pack((wide, wide_pair, wide_mirror, cross_in), half)
    far_first = swap_core(near_first)
    far_inner = after(far_inner, near_first)
    far_outer = after(far_outer, far_inner)
    cross_mirror_in = after(cross_mirror_in, far_outer)
    far_outer = after(far_outer, cross_mirror_in)
    wide_far, cross_far = picked_cross_rows(
        far_inner, far_outer, role_count, capacity, 10**10
    )
    cross_far_in = swap(cross_far, row)
    near_second = pack((wide_far, cross_pair_in, cross_mirror_in), half)
    far_second = swap_core(near_second)
    hidden = hidden_units(near_first, after(far_first, near_second), w_gate, w_up)
    hidden_other = swap_core(hidden)
    hidden_second = hidden_units(near_second, after(far_second, hidden), w_gate, w_up)
    hidden_second_other = swap_core(hidden_second)
    cross_far_in = after(cross_far_in, hidden_second)
    far_third = swap_core(cross_far_in)
    down_weights = (w_down, down_other)
    hidden_other = after(hidden_other, cross_far_in)
    own, own_pair, own_mirror, back_own = down(
        (wide, wide_pair, wide_mirror),
        1,
        hidden,
        hidden_other,
        *down_weights,
        capacity,
        role_count,
    )
    far_third = after(far_third, own)
    hidden_third = hidden_units(cross_far_in, far_third, w_gate, w_up)
    hidden_third_other = swap_core(hidden_third)
    hidden_second_other = after(hidden_second_other, hidden_third)
    own_far, back_pair, back_mirror = down(
        (wide_far,), 2, hidden_second, hidden_second_other, *down_weights, capacity, role_count
    )
    hidden_third_other = after(hidden_third_other, own_far)
    (back_far,) = down(
        (), 1, hidden_third, hidden_third_other, *down_weights, capacity, role_count
    )
    back_far = swap(back_far, row)
    back_mirror = swap(back_mirror, row)
    back_pair = swap(back_pair, row)
    back_own = swap(back_own, row)

    (sum_far,) = combine(wide_far, own_far, back_far, (), role_count, (narrow,))
    from_far_outer = swap(sum_far, pair, outer)
    from_far_inner = swap(sum_far, mirror, inner)
    back_mirror = after(back_mirror, sum_far)
    sum_mirror, sum_mirror_sent = combine(
        wide_mirror, own_mirror, back_mirror, (), role_count, (exact, narrow), 10**10
    )
    from_mirror_outer = swap(sum_mirror_sent, mirror, outer)
    from_far_outer = after(from_far_outer, sum_mirror)
    sum_mirror_far = add_all(sum_mirror, (from_far_outer,))
    from_mirror_inner = swap(sum_mirror_far, mirror, inner)
    back_pair = after(back_pair, sum_mirror_far)
    from_far_inner = after(from_far_inner, back_pair)
    (sum_pair,) = combine(
        wide_pair, own_pair, back_pair, (from_far_inner,), role_count, (narrow,)
    )
    from_pair = swap(sum_pair, pair)
    back_own = after(back_own, sum_pair)
    (sum_own,) = combine(wide, own, back_own, (), role_count, (exact,))
    from_mirror_outer = after(from_mirror_outer, sum_own)
    moe_result = add_all(
        sum_own, (from_mirror_outer, from_mirror_inner, from_pair), last=True
    )
    return (attended, moe_result)


def shards(
    q_lat, latent_cache, lengths, placement, tokens, expert_ids, gate_weights, w_gate, w_up, w_down
):
    if lax.axis_size("role") == 8 and lax.axis_size("tp") == 2:
        return route_multicast(
            q_lat,
            latent_cache,
            lengths,
            placement,
            tokens,
            expert_ids,
            gate_weights,
            w_gate,
            w_up,
            w_down,
        )
    attended = attend_local(q_lat, latent_cache, lengths, placement)
    routed = route_all_to_all(tokens, expert_ids, gate_weights, w_gate, w_up, w_down)
    return (attended, routed)


def solution(mesh):
    return jax.shard_map(
        shards,
        mesh=mesh,
        in_specs=(
            P(("groups", "role"), "tp", None),
            P(("groups", "role"), None, None),
            P("groups"),
            P("groups"),
            P(("groups", "role"), "tp"),
            P(("groups", "role"), None),
            P(("groups", "role"), None),
            P("role", None, "tp"),
            P("role", None, "tp"),
            P("role", "tp", None),
        ),
        out_specs=(P(("groups", "role"), "tp", None), P(("groups", "role"), "tp")),
        check_vma=False,
    )
```

```python
import functools

import jax
import jax.numpy as jnp
from jax import lax
from jax.experimental import pallas as pl
from jax.experimental.pallas import tpu as pltpu
from jax.sharding import PartitionSpec as P

KV_RANK = 512


score_scale = 192.0 ** (-0.5)


def attend_local(q_lat, latent_cache, lengths, placement):
    slot_count = q_lat.shape[0]
    offset = lax.axis_index("role") * slot_count
    slot_ids = offset + jnp.arange(slot_count, dtype=jnp.int32)
    matches = placement[None, :] == slot_ids[:, None]
    slot_length = jnp.sum(jnp.where(matches, lengths[None, :], 0), axis=1)
    scores = (
        jnp.einsum("shc,stc->sht", q_lat, latent_cache, preferred_element_type=jnp.float32)
        * score_scale
    )
    position = jnp.arange(latent_cache.shape[1], dtype=jnp.int32)
    visible = position[None, None, :] < slot_length[:, None, None]
    scores = jnp.where(visible, scores, -jnp.inf)
    highest = jnp.max(scores, axis=2, keepdims=True)
    raised = jnp.exp(scores - highest)
    attn_weights = (raised / jnp.sum(raised, axis=2, keepdims=True)).astype(jnp.bfloat16)
    values = latent_cache[:, :, :KV_RANK]
    return jnp.einsum(
        "sht,stc->shc", attn_weights, values, preferred_element_type=jnp.float32
    ).astype(jnp.bfloat16)


def route_all_to_all(tokens, expert_ids, gate_weights, w_gate, w_up, w_down):
    role_count = lax.axis_size("role")
    token_count = expert_ids.shape[0]
    route_count = expert_ids.shape[1]
    capacity = 3 * token_count * route_count // (2 * role_count)
    flat_ids = expert_ids.reshape(-1)
    onehot = (flat_ids[:, None] == jnp.arange(role_count, dtype=jnp.int32)[None, :]).astype(
        jnp.int32
    )
    earlier = jnp.cumsum(onehot, axis=0) - onehot
    slot_index = jnp.sum(earlier * onehot, axis=1)
    target = flat_ids * capacity + slot_index
    source = jnp.arange(token_count * route_count, dtype=jnp.int32) // route_count
    outgoing = lax.all_gather(tokens, "tp", axis=1, tiled=True)
    columns = outgoing.shape[1]
    buffer_rows = (
        jnp.zeros((role_count * capacity, columns), jnp.bfloat16).at[target].set(outgoing[source])
    )
    buffer_rows = buffer_rows.reshape(role_count, capacity, columns)
    gate_matrix = w_gate[0]
    up_matrix = w_up[0]
    down_matrix = w_down[0]
    received = lax.all_to_all(buffer_rows, "role", split_axis=0, concat_axis=0, tiled=True)
    item_count = received.shape[1]
    arrived = received.reshape(role_count * item_count, columns)
    gate_proj = jnp.dot(arrived, gate_matrix, preferred_element_type=jnp.float32)
    up_proj = jnp.dot(arrived, up_matrix, preferred_element_type=jnp.float32)
    expert_hidden = (jax.nn.silu(gate_proj) * up_proj).astype(jnp.bfloat16)
    partial_out = jnp.dot(expert_hidden, down_matrix, preferred_element_type=jnp.float32)
    summed = lax.psum_scatter(
        partial_out.astype(jnp.bfloat16), "tp", scatter_dimension=1, tiled=True
    )
    summed = summed.reshape(role_count, item_count, summed.shape[1])
    returned = lax.all_to_all(summed, "role", split_axis=0, concat_axis=0, tiled=True)
    half_width = returned.shape[2]
    flat_back = returned.reshape(role_count * capacity, half_width)
    chosen_rows = (
        flat_back[target].reshape(token_count, route_count, half_width).astype(jnp.float32)
    )
    moe_result = jnp.sum(chosen_rows * gate_weights[:, :, None], axis=1).astype(jnp.bfloat16)
    return moe_result


LANES = 128
VMEM_LIMIT = 16 * 1024 * 1024


def round_up(value, unit):
    return -(-value // unit) * unit


def call(kernel, operands, out_shapes, flops, name, scratch=(), types=None, last=False, hint=0):
    place = pl.BlockSpec(memory_space=pltpu.VMEM)
    return pl.pallas_call(
        kernel,
        in_specs=[place] * len(operands),
        out_specs=[place] * len(out_shapes),
        out_shape=[
            (jax.ShapeDtypeStruct if last else pltpu.VMEM)(
                shape, jnp.bfloat16 if types is None else types[index]
            )
            for index, shape in enumerate(out_shapes)
        ],
        scratch_shapes=list(scratch),
        name=name,
        compiler_params=pltpu.CompilerParams(vmem_limit_bytes=VMEM_LIMIT),
        cost_estimate=pl.CostEstimate(flops=hint, bytes_accessed=0, transcendentals=0),
    )(*[pltpu.with_memory_space_constraint(operand, pltpu.VMEM) for operand in operands])


def after(value, *earlier):
    return lax.optimization_barrier((value, *earlier))[0]


def lane_index(rows):
    return lax.broadcasted_iota(jnp.int32, (rows, LANES), 1)


def decode_gate(pieces, expert, expert_count):
    lane = lane_index(pieces.shape[0])
    wanted = lane == expert
    for piece in (1, 2):
        wanted = wanted | (lane == expert + piece * expert_count)
    return jnp.sum(jnp.where(wanted, pieces, 0.0), axis=1, keepdims=True)


def slot_matrix(gate):
    rows = gate.shape[0]
    named = jnp.broadcast_to((gate > 0.0).astype(jnp.float32), (rows, LANES))
    lower = lax.broadcasted_iota(jnp.int32, (rows, rows), 0) >= lax.broadcasted_iota(
        jnp.int32, (rows, rows), 1
    )
    rank = jnp.dot(
        lower.astype(jnp.bfloat16), named.astype(jnp.bfloat16), preferred_element_type=jnp.float32
    )
    slot = lane_index(rows).astype(jnp.float32)
    return jnp.where((named > 0.0) & (rank - 1.0 == slot), 1.0, 0.0).astype(jnp.bfloat16)


def compact(gate, rows_in, capacity):
    picked = lax.dot_general(
        slot_matrix(gate),
        rows_in,
        (((0,), (0,)), ((), ())),
        preferred_element_type=jnp.float32,
    )
    return picked[:capacity].astype(jnp.bfloat16)


def prepare_kernel(
    expert_count,
    tokens_hbm,
    down_hbm,
    ids_hbm,
    gates_hbm,
    wide_ref,
    cross_ref,
    away_ref,
    ids_ref,
    gates_ref,
    sems,
):
    rows, half = tokens_hbm.shape
    copy = pltpu.make_async_copy(tokens_hbm, wide_ref.at[:, :half], sems.at[0])
    first = [
        pltpu.make_async_copy(ids_hbm, ids_ref, sems.at[2]),
        pltpu.make_async_copy(gates_hbm, gates_ref, sems.at[3]),
    ]
    for part in first:
        part.start()
    copy.start()
    sibling = pl.multiple_of((1 - lax.axis_index("tp")) * half, LANES)
    away = pltpu.make_async_copy(down_hbm.at[0, :, pl.ds(sibling, half)], away_ref, sems.at[1])
    away.start()
    for part in first:
        part.wait()
    piece_rows = round_up(3 * expert_count, 16)
    line = lax.broadcasted_iota(jnp.int32, (piece_rows, rows), 0)
    named = line
    for piece in (1, 2):
        named = jnp.where(line >= piece * expert_count, line - piece * expert_count, named)
    dense = jnp.zeros((piece_rows, rows), jnp.float32)
    for choice in range(ids_ref.shape[0]):
        dense = dense + jnp.where(
            ids_ref[choice : choice + 1, :] == named, gates_ref[choice : choice + 1, :], 0.0
        )
    high = dense.astype(jnp.bfloat16).astype(jnp.float32)
    middle = (dense - high).astype(jnp.bfloat16).astype(jnp.float32)
    low = dense - high - middle
    pieces = jnp.where(line < expert_count, high, jnp.where(line < 2 * expert_count, middle, low))
    unit = lax.broadcasted_iota(jnp.int32, (piece_rows, LANES), 0) == lax.broadcasted_iota(
        jnp.int32, (piece_rows, LANES), 1
    )
    turned = lax.dot_general(
        pieces.astype(jnp.bfloat16),
        unit.astype(jnp.bfloat16),
        (((0,), (0,)), ((), ())),
        preferred_element_type=jnp.float32,
    )
    wide_ref[:, half:] = turned.astype(jnp.bfloat16)
    copy.wait()
    gate = decode_gate(turned, lax.axis_index("role") ^ 1, expert_count)
    cross_ref[...] = compact(gate, wide_ref[:, :half], cross_ref.shape[0])
    away.wait()


def prepare(tokens, w_down, expert_ids, gate_weights, expert_count, capacity):
    rows, half = tokens.shape
    shapes = [
        (rows, half + LANES),
        (capacity, half),
        (w_down.shape[1], half),
    ]
    whole = pl.BlockSpec(memory_space=pltpu.VMEM)
    return pl.pallas_call(
        functools.partial(prepare_kernel, expert_count),
        in_specs=[pl.BlockSpec(memory_space=pltpu.HBM)] * 4,
        out_specs=[whole] * len(shapes),
        out_shape=[pltpu.VMEM(shape, jnp.bfloat16) for shape in shapes],
        scratch_shapes=[
            pltpu.VMEM(expert_ids.shape[::-1], jnp.int32),
            pltpu.VMEM(gate_weights.shape[::-1], jnp.float32),
            pltpu.SemaphoreType.DMA((4,)),
        ],
        name="prepare",
        compiler_params=pltpu.CompilerParams(vmem_limit_bytes=VMEM_LIMIT),
        cost_estimate=pl.CostEstimate(flops=0, bytes_accessed=0, transcendentals=0),
    )(
        pltpu.with_memory_space_constraint(tokens, pltpu.HBM),
        pltpu.with_memory_space_constraint(w_down, pltpu.HBM),
        pltpu.with_memory_space_constraint(expert_ids.T, pltpu.HBM),
        pltpu.with_memory_space_constraint(gate_weights.T, pltpu.HBM),
    )


def cross_kernel(expert_count, wide_ref, cross_ref):
    half = cross_ref.shape[1]
    other = lax.axis_index("role") ^ 1
    gate = decode_gate(wide_ref[:, half:].astype(jnp.float32), other, expert_count)
    cross_ref[...] = compact(gate, wide_ref[:, :half], cross_ref.shape[0])


def cross_rows(wide, expert_count, capacity, hint=0):
    rows, width = wide.shape
    half = width - LANES
    return call(
        functools.partial(cross_kernel, expert_count),
        (wide,),
        ((capacity, half),),
        0,
        "cross_rows",
        hint=hint,
    )[0]


def row_starts(blocks):
    starts, rows = [], 0
    for block in blocks:
        starts.append(rows)
        rows += round_up(block.shape[0], 16)
    return tuple(starts), rows


def pack_kernel(starts, *refs):
    out_ref = refs[-1]
    for start, ref in zip(starts, refs):
        out_ref[start : start + ref.shape[0], :] = ref[:, : out_ref.shape[1]]


def pack(blocks, half):
    starts, rows = row_starts(blocks)
    return call(
        functools.partial(pack_kernel, starts), blocks, ((rows, half),), 0, "pack_rows"
    )[0]


def hidden_kernel(near_ref, far_ref, gate_ref, up_ref, hidden_ref):
    half = near_ref.shape[1]
    core = lax.axis_index("tp")
    own = pl.ds(pl.multiple_of(core * half, LANES), half)
    sibling = pl.ds(pl.multiple_of((1 - core) * half, LANES), half)
    width = 256
    for first in range(0, hidden_ref.shape[1], width):
        units = slice(first, first + width)
        gate_proj, up_proj = (
            jnp.dot(near_ref[...], ref[own, units], preferred_element_type=jnp.float32)
            + jnp.dot(far_ref[...], ref[sibling, units], preferred_element_type=jnp.float32)
            for ref in (gate_ref, up_ref)
        )
        hidden_ref[:, units] = (jax.nn.silu(gate_proj) * up_proj).astype(jnp.bfloat16)


def hidden_units(near, far, w_gate, w_up):
    return call(
        hidden_kernel,
        (near, far, w_gate, w_up),
        ((near.shape[0], w_gate.shape[1]),),
        0,
        "hidden_units",
    )[0]


def down_kernel(expert_count, starts, wide_count, *refs):
    wides = refs[:wide_count]
    own_ref, other_ref, down_ref, down_other_ref = refs[wide_count : wide_count + 4]
    outs = refs[wide_count + 4 :]
    half = down_other_ref.shape[1]
    me = lax.axis_index("role")
    base = pl.multiple_of(lax.axis_index("tp") * half, LANES)
    gates = [decode_gate(ref[:, half:].astype(jnp.float32), me, expert_count) for ref in wides]
    width = 256
    for first in range(0, half, width):
        columns = slice(first, first + width)
        result = jnp.dot(
            own_ref[...],
            down_ref[0, :, pl.ds(pl.multiple_of(base + first, LANES), width)],
            preferred_element_type=jnp.float32,
        ) + jnp.dot(
            other_ref[...], down_other_ref[:, columns], preferred_element_type=jnp.float32
        )
        for index, (start, out_ref) in enumerate(zip(starts, outs)):
            block = result[start : start + out_ref.shape[0]].astype(jnp.bfloat16)
            if index < wide_count:
                block = gates[index] * block.astype(jnp.float32)
            out_ref[:, columns] = block


def down(wides, cross_count, hidden, hidden_other, w_down, down_other, capacity, expert_count):
    half = down_other.shape[1]
    shapes = [(wide.shape[0], half) for wide in wides] + [(capacity, half)] * cross_count
    starts, rows = [], 0
    for shape in shapes:
        starts.append(rows)
        rows += round_up(shape[0], 16)
    return call(
        functools.partial(down_kernel, expert_count, tuple(starts), len(wides)),
        (*wides, hidden, hidden_other, w_down, down_other),
        tuple(shapes),
        4 * rows * half * hidden.shape[1],
        "down",
        (),
        [jnp.float32] * len(wides) + [jnp.bfloat16] * cross_count,
    )


def attend_kernel(query_ref, latent_ref, lengths_ref, placement_ref, out_ref):
    slot_count, head_count, _ = query_ref.shape
    rank, context = out_ref.shape[2], latent_ref.shape[2]
    first = lax.axis_index("role") * slot_count
    position = lax.broadcasted_iota(jnp.int32, (head_count, context), 1)
    for slot in range(slot_count):
        here = placement_ref[...] == first + slot
        length = jnp.sum(jnp.where(here, lengths_ref[...], 0), axis=1, keepdims=True)
        scores = (
            jnp.dot(query_ref[slot], latent_ref[slot], preferred_element_type=jnp.float32)
            * score_scale
        )
        scores = jnp.where(position < length, scores, -jnp.inf)
        raised = jnp.exp(scores - jnp.max(scores, axis=1, keepdims=True))
        attn_weights = (raised / jnp.sum(raised, axis=1, keepdims=True)).astype(jnp.bfloat16)
        out_ref[slot] = lax.dot_general(
            attn_weights,
            latent_ref[slot, :rank, :],
            (((1,), (1,)), ((), ())),
            preferred_element_type=jnp.float32,
        ).astype(jnp.bfloat16)


def attend(q_lat, latent_cache, lengths, placement):
    slot_count, head_count, _ = q_lat.shape
    return pl.pallas_call(
        attend_kernel,
        out_shape=jax.ShapeDtypeStruct((slot_count, head_count, KV_RANK), jnp.bfloat16),
        name="attend",
        compiler_params=pltpu.CompilerParams(vmem_limit_bytes=VMEM_LIMIT),
        cost_estimate=pl.CostEstimate(flops=0, bytes_accessed=0, transcendentals=0),
    )(q_lat, latent_cache.transpose(0, 2, 1), lengths[None, :], placement[None, :])


def combine_kernel(expert_count, first, sum_count, wide_ref, own_ref, back_ref, *refs):
    sums, outs = refs[:sum_count], refs[sum_count:]
    half = own_ref.shape[1]
    other = lax.axis_index("role") ^ 1
    gate = decode_gate(wide_ref[:, half:].astype(jnp.float32), other, expert_count)
    slots = slot_matrix(gate)[:, : back_ref.shape[0]]
    width = LANES
    for out_ref in outs:
        for column in range(0, out_ref.shape[1], width):
            columns = slice(first + column, first + column + width)
            spread = jnp.dot(slots, back_ref[:, columns], preferred_element_type=jnp.float32)
            result = own_ref[:, columns] + gate * spread
            for ref in sums:
                result = result + ref[:, column : column + width].astype(jnp.float32)
            out_ref[:, column : column + width] = result.astype(out_ref.dtype)
        first += out_ref.shape[1]


def combine(wide, own, back, sums, expert_count, first, widths, dtype=jnp.bfloat16):
    rows = own.shape[0]
    return call(
        functools.partial(combine_kernel, expert_count, first, len(sums)),
        (wide, own, back, *sums),
        tuple((rows, width) for width in widths),
        0,
        "combine",
        types=(dtype,) * len(widths),
    )


def add_kernel(*refs):
    out_ref = refs[-1]
    count = len(refs) // 2
    first = 0
    for total_ref, part_ref in zip(refs[:count], refs[count:-1]):
        result = total_ref[...] + part_ref[...].astype(jnp.float32)
        out_ref[:, first : first + part_ref.shape[1]] = result.astype(jnp.bfloat16)
        first += part_ref.shape[1]


def add_last(totals, parts):
    shape = (parts[0].shape[0], sum(part.shape[1] for part in parts))
    return call(add_kernel, (*totals, *parts), (shape,), 0, "add_last", last=True)[0]


def swap(array, bits, places=(0, 1, 2, 3)):
    count = lax.axis_size("role")
    pairs = [(device, device ^ bits) for device in range(count) if device // 2 in places]
    return lax.ppermute(array, "role", pairs)


def swap_core(array):
    return lax.ppermute(array, "tp", [(0, 1), (1, 0)])


def route_multicast(
    q_lat, latent_cache, lengths, placement, tokens, expert_ids, gate_weights, w_gate, w_up, w_down
):
    role_count = lax.axis_size("role")
    token_count, route_count = expert_ids.shape
    half = tokens.shape[1]
    capacity = 3 * token_count * route_count // (2 * role_count)
    pair, mirror, row = 2, 6, 1

    wide, cross, down_away = prepare(
        tokens, w_down, expert_ids, gate_weights, role_count, capacity
    )
    wide_mirror = swap(wide, mirror)
    wide_pair = swap(wide, pair)
    cross_in = swap(cross, row)
    w_gate, w_up = w_gate[0], w_up[0]
    down_other = swap_core(down_away)
    attended = attend(after(q_lat, wide), latent_cache, lengths, placement)
    wide_pair = after(wide_pair, attended, down_other)
    cross_pair = cross_rows(wide_pair, role_count, capacity)
    cross_pair_in = swap(cross_pair, row)
    cross_in = after(cross_in, cross_pair)
    wide_mirror = after(wide_mirror, cross_in)
    wide_far = swap(wide_mirror, pair)
    wide_mirror_ready = after(wide_mirror, cross_pair_in)
    cross_mirror = cross_rows(wide_mirror_ready, role_count, capacity)
    cross_mirror_in = swap(cross_mirror, row)
    near_first = pack((wide, wide_pair, after(wide_mirror, cross_mirror), cross_in), half)
    far_first = swap_core(near_first)
    wide_far = after(wide_far, near_first)
    cross_mirror_in = after(cross_mirror_in, wide_far)
    wide_far = after(wide_far, cross_mirror_in)
    cross_far = cross_rows(wide_far, role_count, capacity, 10**10)
    cross_far_in = swap(cross_far, row)
    near_second = pack((wide_far, cross_pair_in, cross_mirror_in), half)
    far_second = swap_core(near_second)
    hidden = hidden_units(near_first, after(far_first, near_second), w_gate, w_up)
    hidden_other = swap_core(hidden)
    hidden_second = hidden_units(near_second, after(far_second, hidden), w_gate, w_up)
    hidden_second_other = swap_core(hidden_second)
    cross_far_in = after(cross_far_in, hidden_second)
    far_third = swap_core(cross_far_in)
    down_weights = (w_down, down_other)
    hidden_other = after(hidden_other, cross_far_in)
    own, own_pair, own_mirror, back_own = down(
        (wide, wide_pair, wide_mirror),
        1,
        hidden,
        hidden_other,
        *down_weights,
        capacity,
        role_count,
    )
    far_third = after(far_third, own)
    hidden_third = hidden_units(cross_far_in, far_third, w_gate, w_up)
    hidden_third_other = swap_core(hidden_third)
    hidden_second_other = after(hidden_second_other, hidden_third)
    own_far, back_pair, back_mirror = down(
        (wide_far,), 2, hidden_second, hidden_second_other, *down_weights, capacity, role_count
    )
    hidden_third_other = after(hidden_third_other, own_far)
    (back_far,) = down(
        (), 1, hidden_third, hidden_third_other, *down_weights, capacity, role_count
    )
    back_far = swap(back_far, row)
    back_mirror = swap(back_mirror, row)
    back_pair = swap(back_pair, row)
    back_own = swap(back_own, row)

    split = half // 2
    widths = (split, half - split)
    sum_far_left, sum_far_right = combine(
        wide_far, own_far, back_far, (), role_count, 0, widths
    )
    from_far_left = swap(sum_far_left, pair)
    from_far_right = swap(sum_far_right, pair)
    back_mirror = after(back_mirror, sum_far_left)
    from_far_left = after(from_far_left, back_mirror)
    (sum_mirror_left,) = combine(
        wide_mirror, own_mirror, back_mirror, (from_far_left,), role_count, 0, widths[:1]
    )
    from_mirror_left = swap(sum_mirror_left, mirror)
    from_far_right = after(from_far_right, sum_mirror_left)
    (sum_mirror_right,) = combine(
        wide_mirror, own_mirror, back_mirror, (from_far_right,), role_count, split, widths[1:]
    )
    from_mirror_right = swap(sum_mirror_right, mirror)
    back_pair = after(back_pair, sum_mirror_right)
    sum_pair_left, sum_pair_right = combine(
        wide_pair, own_pair, back_pair, (), role_count, 0, widths
    )
    from_pair_left = swap(sum_pair_left, pair)
    from_pair_right = swap(sum_pair_right, pair)
    back_own = after(back_own, sum_pair_left)
    from_mirror_left = after(from_mirror_left, back_own)
    (sum_left,) = combine(
        wide, own, back_own, (from_mirror_left,), role_count, 0, widths[:1], jnp.float32
    )
    from_mirror_right = after(from_mirror_right, sum_left)
    (sum_right,) = combine(
        wide, own, back_own, (from_mirror_right,), role_count, split, widths[1:], jnp.float32
    )
    from_pair_left = after(from_pair_left, sum_right)
    moe_result = add_last((sum_left, sum_right), (from_pair_left, from_pair_right))
    return (attended, moe_result)


def shards(
    q_lat, latent_cache, lengths, placement, tokens, expert_ids, gate_weights, w_gate, w_up, w_down
):
    if lax.axis_size("role") == 8 and lax.axis_size("tp") == 2:
        return route_multicast(
            q_lat,
            latent_cache,
            lengths,
            placement,
            tokens,
            expert_ids,
            gate_weights,
            w_gate,
            w_up,
            w_down,
        )
    attended = attend_local(q_lat, latent_cache, lengths, placement)
    routed = route_all_to_all(tokens, expert_ids, gate_weights, w_gate, w_up, w_down)
    return (attended, routed)


def solution(mesh):
    return jax.shard_map(
        shards,
        mesh=mesh,
        in_specs=(
            P(("groups", "role"), "tp", None),
            P(("groups", "role"), None, None),
            P("groups"),
            P("groups"),
            P(("groups", "role"), "tp"),
            P(("groups", "role"), None),
            P(("groups", "role"), None),
            P("role", None, "tp"),
            P("role", None, "tp"),
            P("role", "tp", None),
        ),
        out_specs=(P(("groups", "role"), "tp", None), P(("groups", "role"), "tp")),
        check_vma=False,
    )
```

```python
import functools

import jax
import jax.numpy as jnp
from jax import lax
from jax.experimental import pallas as pl
from jax.experimental.pallas import tpu as pltpu
from jax.sharding import PartitionSpec as P

KV_RANK = 512


score_scale = 192.0 ** (-0.5)


def attend_local(q_lat, latent_cache, lengths, placement):
    slot_count = q_lat.shape[0]
    offset = lax.axis_index("role") * slot_count
    slot_ids = offset + jnp.arange(slot_count, dtype=jnp.int32)
    matches = placement[None, :] == slot_ids[:, None]
    slot_length = jnp.sum(jnp.where(matches, lengths[None, :], 0), axis=1)
    scores = (
        jnp.einsum("shc,stc->sht", q_lat, latent_cache, preferred_element_type=jnp.float32)
        * score_scale
    )
    position = jnp.arange(latent_cache.shape[1], dtype=jnp.int32)
    visible = position[None, None, :] < slot_length[:, None, None]
    scores = jnp.where(visible, scores, -jnp.inf)
    highest = jnp.max(scores, axis=2, keepdims=True)
    raised = jnp.exp(scores - highest)
    attn_weights = (raised / jnp.sum(raised, axis=2, keepdims=True)).astype(jnp.bfloat16)
    values = latent_cache[:, :, :KV_RANK]
    return jnp.einsum(
        "sht,stc->shc", attn_weights, values, preferred_element_type=jnp.float32
    ).astype(jnp.bfloat16)


def route_all_to_all(tokens, expert_ids, gate_weights, w_gate, w_up, w_down):
    role_count = lax.axis_size("role")
    token_count = expert_ids.shape[0]
    route_count = expert_ids.shape[1]
    capacity = 3 * token_count * route_count // (2 * role_count)
    flat_ids = expert_ids.reshape(-1)
    onehot = (flat_ids[:, None] == jnp.arange(role_count, dtype=jnp.int32)[None, :]).astype(
        jnp.int32
    )
    earlier = jnp.cumsum(onehot, axis=0) - onehot
    slot_index = jnp.sum(earlier * onehot, axis=1)
    target = flat_ids * capacity + slot_index
    source = jnp.arange(token_count * route_count, dtype=jnp.int32) // route_count
    outgoing = lax.all_gather(tokens, "tp", axis=1, tiled=True)
    columns = outgoing.shape[1]
    buffer_rows = (
        jnp.zeros((role_count * capacity, columns), jnp.bfloat16).at[target].set(outgoing[source])
    )
    buffer_rows = buffer_rows.reshape(role_count, capacity, columns)
    gate_matrix = w_gate[0]
    up_matrix = w_up[0]
    down_matrix = w_down[0]
    received = lax.all_to_all(buffer_rows, "role", split_axis=0, concat_axis=0, tiled=True)
    item_count = received.shape[1]
    arrived = received.reshape(role_count * item_count, columns)
    gate_proj = jnp.dot(arrived, gate_matrix, preferred_element_type=jnp.float32)
    up_proj = jnp.dot(arrived, up_matrix, preferred_element_type=jnp.float32)
    expert_hidden = (jax.nn.silu(gate_proj) * up_proj).astype(jnp.bfloat16)
    partial_out = jnp.dot(expert_hidden, down_matrix, preferred_element_type=jnp.float32)
    summed = lax.psum_scatter(
        partial_out.astype(jnp.bfloat16), "tp", scatter_dimension=1, tiled=True
    )
    summed = summed.reshape(role_count, item_count, summed.shape[1])
    returned = lax.all_to_all(summed, "role", split_axis=0, concat_axis=0, tiled=True)
    half_width = returned.shape[2]
    flat_back = returned.reshape(role_count * capacity, half_width)
    chosen_rows = (
        flat_back[target].reshape(token_count, route_count, half_width).astype(jnp.float32)
    )
    moe_result = jnp.sum(chosen_rows * gate_weights[:, :, None], axis=1).astype(jnp.bfloat16)
    return moe_result


LANES = 128
VMEM_LIMIT = 16 * 1024 * 1024


def round_up(value, unit):
    return -(-value // unit) * unit


def call(kernel, operands, out_shapes, flops, name, scratch=(), types=None, last=False, hint=0):
    place = pl.BlockSpec(memory_space=pltpu.VMEM)
    return pl.pallas_call(
        kernel,
        in_specs=[place] * len(operands),
        out_specs=[place] * len(out_shapes),
        out_shape=[
            (jax.ShapeDtypeStruct if last else pltpu.VMEM)(
                shape, jnp.bfloat16 if types is None else types[index]
            )
            for index, shape in enumerate(out_shapes)
        ],
        scratch_shapes=list(scratch),
        name=name,
        compiler_params=pltpu.CompilerParams(vmem_limit_bytes=VMEM_LIMIT),
        cost_estimate=pl.CostEstimate(flops=hint, bytes_accessed=0, transcendentals=0),
    )(*[pltpu.with_memory_space_constraint(operand, pltpu.VMEM) for operand in operands])


def after(value, *earlier):
    return lax.optimization_barrier((value, *earlier))[0]


def lane_index(rows):
    return lax.broadcasted_iota(jnp.int32, (rows, LANES), 1)


def decode_gate(pieces, expert, expert_count):
    lane = lane_index(pieces.shape[0])
    wanted = lane == expert
    for piece in (1, 2):
        wanted = wanted | (lane == expert + piece * expert_count)
    return jnp.sum(jnp.where(wanted, pieces, 0.0), axis=1, keepdims=True)


def slot_matrix(gate):
    rows = gate.shape[0]
    named = jnp.broadcast_to((gate > 0.0).astype(jnp.float32), (rows, LANES))
    lower = lax.broadcasted_iota(jnp.int32, (rows, rows), 0) >= lax.broadcasted_iota(
        jnp.int32, (rows, rows), 1
    )
    rank = jnp.dot(
        lower.astype(jnp.bfloat16), named.astype(jnp.bfloat16), preferred_element_type=jnp.float32
    )
    slot = lane_index(rows).astype(jnp.float32)
    return jnp.where((named > 0.0) & (rank - 1.0 == slot), 1.0, 0.0).astype(jnp.bfloat16)


def compact(gate, rows_in, capacity):
    picked = lax.dot_general(
        slot_matrix(gate),
        rows_in,
        (((0,), (0,)), ((), ())),
        preferred_element_type=jnp.float32,
    )
    return picked[:capacity].astype(jnp.bfloat16)


def prepare_kernel(
    expert_count,
    tokens_hbm,
    down_hbm,
    ids_hbm,
    gates_hbm,
    wide_ref,
    cross_ref,
    away_ref,
    ids_ref,
    gates_ref,
    sems,
):
    rows, half = tokens_hbm.shape
    copy = pltpu.make_async_copy(tokens_hbm, wide_ref.at[:, :half], sems.at[0])
    first = [
        pltpu.make_async_copy(ids_hbm, ids_ref, sems.at[2]),
        pltpu.make_async_copy(gates_hbm, gates_ref, sems.at[3]),
    ]
    for part in first:
        part.start()
    copy.start()
    sibling = pl.multiple_of((1 - lax.axis_index("tp")) * half, LANES)
    away = pltpu.make_async_copy(down_hbm.at[0, :, pl.ds(sibling, half)], away_ref, sems.at[1])
    away.start()
    for part in first:
        part.wait()
    piece_rows = round_up(3 * expert_count, 16)
    line = lax.broadcasted_iota(jnp.int32, (piece_rows, rows), 0)
    named = line
    for piece in (1, 2):
        named = jnp.where(line >= piece * expert_count, line - piece * expert_count, named)
    dense = jnp.zeros((piece_rows, rows), jnp.float32)
    for choice in range(ids_ref.shape[0]):
        dense = dense + jnp.where(
            ids_ref[choice : choice + 1, :] == named, gates_ref[choice : choice + 1, :], 0.0
        )
    high = dense.astype(jnp.bfloat16).astype(jnp.float32)
    middle = (dense - high).astype(jnp.bfloat16).astype(jnp.float32)
    low = dense - high - middle
    pieces = jnp.where(line < expert_count, high, jnp.where(line < 2 * expert_count, middle, low))
    unit = lax.broadcasted_iota(jnp.int32, (piece_rows, LANES), 0) == lax.broadcasted_iota(
        jnp.int32, (piece_rows, LANES), 1
    )
    turned = lax.dot_general(
        pieces.astype(jnp.bfloat16),
        unit.astype(jnp.bfloat16),
        (((0,), (0,)), ((), ())),
        preferred_element_type=jnp.float32,
    )
    wide_ref[:, half:] = turned.astype(jnp.bfloat16)
    copy.wait()
    gate = decode_gate(turned, lax.axis_index("role") ^ 1, expert_count)
    cross_ref[...] = compact(gate, wide_ref[:, :half], cross_ref.shape[0])
    away.wait()


def prepare(tokens, w_down, expert_ids, gate_weights, expert_count, capacity):
    rows, half = tokens.shape
    shapes = [
        (rows, half + LANES),
        (capacity, half),
        (w_down.shape[1], half),
    ]
    whole = pl.BlockSpec(memory_space=pltpu.VMEM)
    return pl.pallas_call(
        functools.partial(prepare_kernel, expert_count),
        in_specs=[pl.BlockSpec(memory_space=pltpu.HBM)] * 4,
        out_specs=[whole] * len(shapes),
        out_shape=[pltpu.VMEM(shape, jnp.bfloat16) for shape in shapes],
        scratch_shapes=[
            pltpu.VMEM(expert_ids.shape[::-1], jnp.int32),
            pltpu.VMEM(gate_weights.shape[::-1], jnp.float32),
            pltpu.SemaphoreType.DMA((4,)),
        ],
        name="prepare",
        compiler_params=pltpu.CompilerParams(vmem_limit_bytes=VMEM_LIMIT),
        cost_estimate=pl.CostEstimate(flops=0, bytes_accessed=0, transcendentals=0),
    )(
        pltpu.with_memory_space_constraint(tokens, pltpu.HBM),
        pltpu.with_memory_space_constraint(w_down, pltpu.HBM),
        pltpu.with_memory_space_constraint(expert_ids.T, pltpu.HBM),
        pltpu.with_memory_space_constraint(gate_weights.T, pltpu.HBM),
    )


def cross_kernel(expert_count, wide_ref, cross_ref):
    half = cross_ref.shape[1]
    other = lax.axis_index("role") ^ 1
    gate = decode_gate(wide_ref[:, half:].astype(jnp.float32), other, expert_count)
    cross_ref[...] = compact(gate, wide_ref[:, :half], cross_ref.shape[0])


def cross_rows(wide, expert_count, capacity, hint=0):
    rows, width = wide.shape
    half = width - LANES
    return call(
        functools.partial(cross_kernel, expert_count),
        (wide,),
        ((capacity, half),),
        0,
        "cross_rows",
        hint=hint,
    )[0]


def row_starts(blocks):
    starts, rows = [], 0
    for block in blocks:
        starts.append(rows)
        rows += round_up(block.shape[0], 16)
    return tuple(starts), rows


def pack_kernel(starts, *refs):
    out_ref = refs[-1]
    for start, ref in zip(starts, refs):
        out_ref[start : start + ref.shape[0], :] = ref[:, : out_ref.shape[1]]


def pack(blocks, half):
    starts, rows = row_starts(blocks)
    return call(
        functools.partial(pack_kernel, starts), blocks, ((rows, half),), 0, "pack_rows"
    )[0]


def hidden_kernel(near_ref, far_ref, gate_ref, up_ref, hidden_ref):
    half = near_ref.shape[1]
    core = lax.axis_index("tp")
    own = pl.ds(pl.multiple_of(core * half, LANES), half)
    sibling = pl.ds(pl.multiple_of((1 - core) * half, LANES), half)
    width = 256
    for first in range(0, hidden_ref.shape[1], width):
        units = slice(first, first + width)
        gate_proj, up_proj = (
            jnp.dot(near_ref[...], ref[own, units], preferred_element_type=jnp.float32)
            + jnp.dot(far_ref[...], ref[sibling, units], preferred_element_type=jnp.float32)
            for ref in (gate_ref, up_ref)
        )
        hidden_ref[:, units] = (jax.nn.silu(gate_proj) * up_proj).astype(jnp.bfloat16)


def hidden_units(near, far, w_gate, w_up):
    return call(
        hidden_kernel,
        (near, far, w_gate, w_up),
        ((near.shape[0], w_gate.shape[1]),),
        0,
        "hidden_units",
    )[0]


def down_kernel(expert_count, starts, wide_count, *refs):
    wides = refs[:wide_count]
    own_ref, other_ref, down_ref, down_other_ref = refs[wide_count : wide_count + 4]
    outs = refs[wide_count + 4 :]
    half = down_other_ref.shape[1]
    me = lax.axis_index("role")
    base = pl.multiple_of(lax.axis_index("tp") * half, LANES)
    gates = [decode_gate(ref[:, half:].astype(jnp.float32), me, expert_count) for ref in wides]
    width = 256
    for first in range(0, half, width):
        columns = slice(first, first + width)
        result = jnp.dot(
            own_ref[...],
            down_ref[0, :, pl.ds(pl.multiple_of(base + first, LANES), width)],
            preferred_element_type=jnp.float32,
        ) + jnp.dot(
            other_ref[...], down_other_ref[:, columns], preferred_element_type=jnp.float32
        )
        for index, (start, out_ref) in enumerate(zip(starts, outs)):
            block = result[start : start + out_ref.shape[0]].astype(jnp.bfloat16)
            if index < wide_count:
                block = gates[index] * block.astype(jnp.float32)
            out_ref[:, columns] = block


def down(wides, cross_count, hidden, hidden_other, w_down, down_other, capacity, expert_count):
    half = down_other.shape[1]
    shapes = [(wide.shape[0], half) for wide in wides] + [(capacity, half)] * cross_count
    starts, rows = [], 0
    for shape in shapes:
        starts.append(rows)
        rows += round_up(shape[0], 16)
    return call(
        functools.partial(down_kernel, expert_count, tuple(starts), len(wides)),
        (*wides, hidden, hidden_other, w_down, down_other),
        tuple(shapes),
        4 * rows * half * hidden.shape[1],
        "down",
        (),
        [jnp.float32] * len(wides) + [jnp.bfloat16] * cross_count,
    )


def attend_kernel(query_ref, latent_ref, lengths_ref, placement_ref, out_ref):
    slot_count, head_count, _ = query_ref.shape
    rank, context = out_ref.shape[2], latent_ref.shape[2]
    first = lax.axis_index("role") * slot_count
    position = lax.broadcasted_iota(jnp.int32, (head_count, context), 1)
    for slot in range(slot_count):
        here = placement_ref[...] == first + slot
        length = jnp.sum(jnp.where(here, lengths_ref[...], 0), axis=1, keepdims=True)
        scores = (
            jnp.dot(query_ref[slot], latent_ref[slot], preferred_element_type=jnp.float32)
            * score_scale
        )
        scores = jnp.where(position < length, scores, -jnp.inf)
        raised = jnp.exp(scores - jnp.max(scores, axis=1, keepdims=True))
        attn_weights = (raised / jnp.sum(raised, axis=1, keepdims=True)).astype(jnp.bfloat16)
        out_ref[slot] = lax.dot_general(
            attn_weights,
            latent_ref[slot, :rank, :],
            (((1,), (1,)), ((), ())),
            preferred_element_type=jnp.float32,
        ).astype(jnp.bfloat16)


def attend(q_lat, latent_cache, lengths, placement):
    slot_count, head_count, _ = q_lat.shape
    return pl.pallas_call(
        attend_kernel,
        out_shape=jax.ShapeDtypeStruct((slot_count, head_count, KV_RANK), jnp.bfloat16),
        name="attend",
        compiler_params=pltpu.CompilerParams(vmem_limit_bytes=VMEM_LIMIT),
        cost_estimate=pl.CostEstimate(flops=0, bytes_accessed=0, transcendentals=0),
    )(q_lat, latent_cache.transpose(0, 2, 1), lengths[None, :], placement[None, :])


def combine_kernel(expert_count, first, sum_count, wide_ref, own_ref, back_ref, *refs):
    sums, outs = refs[:sum_count], refs[sum_count:]
    half = own_ref.shape[1]
    other = lax.axis_index("role") ^ 1
    gate = decode_gate(wide_ref[:, half:].astype(jnp.float32), other, expert_count)
    slots = slot_matrix(gate)[:, : back_ref.shape[0]]
    width = LANES
    for out_ref in outs:
        for column in range(0, out_ref.shape[1], width):
            columns = slice(first + column, first + column + width)
            spread = jnp.dot(slots, back_ref[:, columns], preferred_element_type=jnp.float32)
            result = own_ref[:, columns] + gate * spread
            for ref in sums:
                result = result + ref[:, column : column + width].astype(jnp.float32)
            out_ref[:, column : column + width] = result.astype(out_ref.dtype)
        first += out_ref.shape[1]


def combine(wide, own, back, sums, expert_count, first, widths, dtype=jnp.bfloat16):
    rows = own.shape[0]
    return call(
        functools.partial(combine_kernel, expert_count, first, len(sums)),
        (wide, own, back, *sums),
        tuple((rows, width) for width in widths),
        0,
        "combine",
        types=(dtype,) * len(widths),
    )


def add_kernel(*refs):
    out_ref = refs[-1]
    count = len(refs) // 2
    first = 0
    for total_ref, part_ref in zip(refs[:count], refs[count:-1]):
        result = total_ref[...] + part_ref[...].astype(jnp.float32)
        out_ref[:, first : first + part_ref.shape[1]] = result.astype(jnp.bfloat16)
        first += part_ref.shape[1]


def add_last(totals, parts):
    shape = (parts[0].shape[0], sum(part.shape[1] for part in parts))
    return call(add_kernel, (*totals, *parts), (shape,), 0, "add_last", last=True)[0]


def swap(array, bits, places=(0, 1, 2, 3)):
    count = lax.axis_size("role")
    pairs = [(device, device ^ bits) for device in range(count) if device // 2 in places]
    return lax.ppermute(array, "role", pairs)


def swap_core(array):
    return lax.ppermute(array, "tp", [(0, 1), (1, 0)])


def route_multicast(
    q_lat, latent_cache, lengths, placement, tokens, expert_ids, gate_weights, w_gate, w_up, w_down
):
    role_count = lax.axis_size("role")
    token_count, route_count = expert_ids.shape
    half = tokens.shape[1]
    capacity = 3 * token_count * route_count // (2 * role_count)
    pair, mirror, row = 2, 6, 1

    wide, cross, down_away = prepare(
        tokens, w_down, expert_ids, gate_weights, role_count, capacity
    )
    wide_mirror = swap(wide, mirror)
    wide_pair = swap(wide, pair)
    cross_in = swap(cross, row)
    w_gate, w_up = w_gate[0], w_up[0]
    down_other = swap_core(down_away)
    attended = attend(after(q_lat, wide), latent_cache, lengths, placement)
    cross_in = after(cross_in, attended)
    wide_pair = after(wide_pair, cross_in, down_other)
    cross_pair = cross_rows(wide_pair, role_count, capacity)
    cross_pair_in = swap(cross_pair, row)
    wide_mirror = after(wide_mirror, cross_pair)
    wide_far = swap(wide_mirror, pair)
    wide_mirror_ready = after(wide_mirror, cross_pair_in)
    cross_mirror = cross_rows(wide_mirror_ready, role_count, capacity)
    cross_mirror_in = swap(cross_mirror, row)
    near_first = pack((wide, wide_pair, after(wide_mirror, cross_mirror), cross_in), half)
    far_first = swap_core(near_first)
    wide_far = after(wide_far, near_first)
    cross_mirror_in = after(cross_mirror_in, wide_far)
    wide_far = after(wide_far, cross_mirror_in)
    cross_far = cross_rows(wide_far, role_count, capacity, 10**10)
    cross_far_in = swap(cross_far, row)
    near_second = pack((wide_far, cross_pair_in, cross_mirror_in), half)
    far_second = swap_core(near_second)
    hidden = hidden_units(near_first, after(far_first, near_second), w_gate, w_up)
    hidden_other = swap_core(hidden)
    hidden_second = hidden_units(near_second, after(far_second, hidden), w_gate, w_up)
    hidden_second_other = swap_core(hidden_second)
    cross_far_in = after(cross_far_in, hidden_second)
    far_third = swap_core(cross_far_in)
    down_weights = (w_down, down_other)
    hidden_other = after(hidden_other, cross_far_in)
    own, own_pair, own_mirror, back_own = down(
        (wide, wide_pair, wide_mirror),
        1,
        hidden,
        hidden_other,
        *down_weights,
        capacity,
        role_count,
    )
    far_third = after(far_third, own)
    hidden_third = hidden_units(cross_far_in, far_third, w_gate, w_up)
    hidden_third_other = swap_core(hidden_third)
    hidden_second_other = after(hidden_second_other, hidden_third)
    own_far, back_pair, back_mirror = down(
        (wide_far,), 2, hidden_second, hidden_second_other, *down_weights, capacity, role_count
    )
    hidden_third_other = after(hidden_third_other, own_far)
    (back_far,) = down(
        (), 1, hidden_third, hidden_third_other, *down_weights, capacity, role_count
    )
    back_far = swap(back_far, row)
    back_mirror = swap(back_mirror, row)
    back_pair = swap(back_pair, row)
    back_own = swap(back_own, row)

    split = half // 2
    widths = (split, half - split)
    sum_far_left, sum_far_right = combine(
        wide_far, own_far, back_far, (), role_count, 0, widths
    )
    from_far_left = swap(sum_far_left, pair)
    from_far_right = swap(sum_far_right, pair)
    back_mirror = after(back_mirror, sum_far_left)
    from_far_left = after(from_far_left, back_mirror)
    (sum_mirror_left,) = combine(
        wide_mirror, own_mirror, back_mirror, (from_far_left,), role_count, 0, widths[:1]
    )
    from_mirror_left = swap(sum_mirror_left, mirror)
    from_far_right = after(from_far_right, sum_mirror_left)
    (sum_mirror_right,) = combine(
        wide_mirror, own_mirror, back_mirror, (from_far_right,), role_count, split, widths[1:]
    )
    from_mirror_right = swap(sum_mirror_right, mirror)
    back_pair = after(back_pair, sum_mirror_right)
    sum_pair_left, sum_pair_right = combine(
        wide_pair, own_pair, back_pair, (), role_count, 0, widths
    )
    from_pair_left = swap(sum_pair_left, pair)
    from_pair_right = swap(sum_pair_right, pair)
    back_own = after(back_own, sum_pair_left)
    from_mirror_left = after(from_mirror_left, back_own)
    (sum_left,) = combine(
        wide, own, back_own, (from_mirror_left,), role_count, 0, widths[:1], jnp.float32
    )
    from_mirror_right = after(from_mirror_right, sum_left)
    (sum_right,) = combine(
        wide, own, back_own, (from_mirror_right,), role_count, split, widths[1:], jnp.float32
    )
    from_pair_left = after(from_pair_left, sum_right)
    moe_result = add_last((sum_left, sum_right), (from_pair_left, from_pair_right))
    return (attended, moe_result)


def shards(
    q_lat, latent_cache, lengths, placement, tokens, expert_ids, gate_weights, w_gate, w_up, w_down
):
    if lax.axis_size("role") == 8 and lax.axis_size("tp") == 2:
        return route_multicast(
            q_lat,
            latent_cache,
            lengths,
            placement,
            tokens,
            expert_ids,
            gate_weights,
            w_gate,
            w_up,
            w_down,
        )
    attended = attend_local(q_lat, latent_cache, lengths, placement)
    routed = route_all_to_all(tokens, expert_ids, gate_weights, w_gate, w_up, w_down)
    return (attended, routed)


def solution(mesh):
    return jax.shard_map(
        shards,
        mesh=mesh,
        in_specs=(
            P(("groups", "role"), "tp", None),
            P(("groups", "role"), None, None),
            P("groups"),
            P("groups"),
            P(("groups", "role"), "tp"),
            P(("groups", "role"), None),
            P(("groups", "role"), None),
            P("role", None, "tp"),
            P("role", None, "tp"),
            P("role", "tp", None),
        ),
        out_specs=(P(("groups", "role"), "tp", None), P(("groups", "role"), "tp")),
        check_vma=False,
    )
```

```python
import functools

import jax
import jax.numpy as jnp
from jax import lax
from jax.experimental import pallas as pl
from jax.experimental.pallas import tpu as pltpu
from jax.sharding import PartitionSpec as P

KV_RANK = 512


score_scale = 192.0 ** (-0.5)


def attend_local(q_lat, latent_cache, lengths, placement):
    slot_count = q_lat.shape[0]
    offset = lax.axis_index("role") * slot_count
    slot_ids = offset + jnp.arange(slot_count, dtype=jnp.int32)
    matches = placement[None, :] == slot_ids[:, None]
    slot_length = jnp.sum(jnp.where(matches, lengths[None, :], 0), axis=1)
    scores = (
        jnp.einsum("shc,stc->sht", q_lat, latent_cache, preferred_element_type=jnp.float32)
        * score_scale
    )
    position = jnp.arange(latent_cache.shape[1], dtype=jnp.int32)
    visible = position[None, None, :] < slot_length[:, None, None]
    scores = jnp.where(visible, scores, -jnp.inf)
    highest = jnp.max(scores, axis=2, keepdims=True)
    raised = jnp.exp(scores - highest)
    attn_weights = (raised / jnp.sum(raised, axis=2, keepdims=True)).astype(jnp.bfloat16)
    values = latent_cache[:, :, :KV_RANK]
    return jnp.einsum(
        "sht,stc->shc", attn_weights, values, preferred_element_type=jnp.float32
    ).astype(jnp.bfloat16)


def route_all_to_all(tokens, expert_ids, gate_weights, w_gate, w_up, w_down):
    role_count = lax.axis_size("role")
    token_count = expert_ids.shape[0]
    route_count = expert_ids.shape[1]
    capacity = 3 * token_count * route_count // (2 * role_count)
    flat_ids = expert_ids.reshape(-1)
    onehot = (flat_ids[:, None] == jnp.arange(role_count, dtype=jnp.int32)[None, :]).astype(
        jnp.int32
    )
    earlier = jnp.cumsum(onehot, axis=0) - onehot
    slot_index = jnp.sum(earlier * onehot, axis=1)
    target = flat_ids * capacity + slot_index
    source = jnp.arange(token_count * route_count, dtype=jnp.int32) // route_count
    outgoing = lax.all_gather(tokens, "tp", axis=1, tiled=True)
    columns = outgoing.shape[1]
    buffer_rows = (
        jnp.zeros((role_count * capacity, columns), jnp.bfloat16).at[target].set(outgoing[source])
    )
    buffer_rows = buffer_rows.reshape(role_count, capacity, columns)
    gate_matrix = w_gate[0]
    up_matrix = w_up[0]
    down_matrix = w_down[0]
    received = lax.all_to_all(buffer_rows, "role", split_axis=0, concat_axis=0, tiled=True)
    item_count = received.shape[1]
    arrived = received.reshape(role_count * item_count, columns)
    gate_proj = jnp.dot(arrived, gate_matrix, preferred_element_type=jnp.float32)
    up_proj = jnp.dot(arrived, up_matrix, preferred_element_type=jnp.float32)
    expert_hidden = (jax.nn.silu(gate_proj) * up_proj).astype(jnp.bfloat16)
    partial_out = jnp.dot(expert_hidden, down_matrix, preferred_element_type=jnp.float32)
    summed = lax.psum_scatter(
        partial_out.astype(jnp.bfloat16), "tp", scatter_dimension=1, tiled=True
    )
    summed = summed.reshape(role_count, item_count, summed.shape[1])
    returned = lax.all_to_all(summed, "role", split_axis=0, concat_axis=0, tiled=True)
    half_width = returned.shape[2]
    flat_back = returned.reshape(role_count * capacity, half_width)
    chosen_rows = (
        flat_back[target].reshape(token_count, route_count, half_width).astype(jnp.float32)
    )
    moe_result = jnp.sum(chosen_rows * gate_weights[:, :, None], axis=1).astype(jnp.bfloat16)
    return moe_result


LANES = 128
VMEM_LIMIT = 16 * 1024 * 1024


def round_up(value, unit):
    return -(-value // unit) * unit


def call(kernel, operands, out_shapes, flops, name, scratch=(), types=None, last=False, hint=0):
    place = pl.BlockSpec(memory_space=pltpu.VMEM)
    return pl.pallas_call(
        kernel,
        in_specs=[place] * len(operands),
        out_specs=[place] * len(out_shapes),
        out_shape=[
            (jax.ShapeDtypeStruct if last else pltpu.VMEM)(
                shape, jnp.bfloat16 if types is None else types[index]
            )
            for index, shape in enumerate(out_shapes)
        ],
        scratch_shapes=list(scratch),
        name=name,
        compiler_params=pltpu.CompilerParams(vmem_limit_bytes=VMEM_LIMIT),
        cost_estimate=pl.CostEstimate(flops=hint, bytes_accessed=0, transcendentals=0),
    )(*[pltpu.with_memory_space_constraint(operand, pltpu.VMEM) for operand in operands])


def after(value, *earlier):
    return lax.optimization_barrier((value, *earlier))[0]


def lane_index(rows):
    return lax.broadcasted_iota(jnp.int32, (rows, LANES), 1)


def decode_gate(pieces, expert, expert_count):
    lane = lane_index(pieces.shape[0])
    wanted = lane == expert
    for piece in (1, 2):
        wanted = wanted | (lane == expert + piece * expert_count)
    return jnp.sum(jnp.where(wanted, pieces, 0.0), axis=1, keepdims=True)


def slot_matrix(gate):
    rows = gate.shape[0]
    named = jnp.broadcast_to((gate > 0.0).astype(jnp.float32), (rows, LANES))
    lower = lax.broadcasted_iota(jnp.int32, (rows, rows), 0) >= lax.broadcasted_iota(
        jnp.int32, (rows, rows), 1
    )
    rank = jnp.dot(
        lower.astype(jnp.bfloat16), named.astype(jnp.bfloat16), preferred_element_type=jnp.float32
    )
    slot = lane_index(rows).astype(jnp.float32)
    return jnp.where((named > 0.0) & (rank - 1.0 == slot), 1.0, 0.0).astype(jnp.bfloat16)


def compact(gate, rows_in, capacity):
    picked = lax.dot_general(
        slot_matrix(gate),
        rows_in,
        (((0,), (0,)), ((), ())),
        preferred_element_type=jnp.float32,
    )
    return picked[:capacity].astype(jnp.bfloat16)


def prepare_kernel(
    expert_count,
    tokens_hbm,
    down_hbm,
    ids_hbm,
    gates_hbm,
    wide_ref,
    cross_ref,
    away_ref,
    ids_ref,
    gates_ref,
    sems,
):
    rows, half = tokens_hbm.shape
    copy = pltpu.make_async_copy(tokens_hbm, wide_ref.at[:, :half], sems.at[0])
    first = [
        pltpu.make_async_copy(ids_hbm, ids_ref, sems.at[2]),
        pltpu.make_async_copy(gates_hbm, gates_ref, sems.at[3]),
    ]
    for part in first:
        part.start()
    copy.start()
    sibling = pl.multiple_of((1 - lax.axis_index("tp")) * half, LANES)
    away = pltpu.make_async_copy(down_hbm.at[0, :, pl.ds(sibling, half)], away_ref, sems.at[1])
    away.start()
    for part in first:
        part.wait()
    piece_rows = round_up(3 * expert_count, 16)
    line = lax.broadcasted_iota(jnp.int32, (piece_rows, rows), 0)
    named = line
    for piece in (1, 2):
        named = jnp.where(line >= piece * expert_count, line - piece * expert_count, named)
    dense = jnp.zeros((piece_rows, rows), jnp.float32)
    for choice in range(ids_ref.shape[0]):
        dense = dense + jnp.where(
            ids_ref[choice : choice + 1, :] == named, gates_ref[choice : choice + 1, :], 0.0
        )
    high = dense.astype(jnp.bfloat16).astype(jnp.float32)
    middle = (dense - high).astype(jnp.bfloat16).astype(jnp.float32)
    low = dense - high - middle
    pieces = jnp.where(line < expert_count, high, jnp.where(line < 2 * expert_count, middle, low))
    unit = lax.broadcasted_iota(jnp.int32, (piece_rows, LANES), 0) == lax.broadcasted_iota(
        jnp.int32, (piece_rows, LANES), 1
    )
    turned = lax.dot_general(
        pieces.astype(jnp.bfloat16),
        unit.astype(jnp.bfloat16),
        (((0,), (0,)), ((), ())),
        preferred_element_type=jnp.float32,
    )
    wide_ref[:, half:] = turned.astype(jnp.bfloat16)
    copy.wait()
    gate = decode_gate(turned, lax.axis_index("role") ^ 1, expert_count)
    cross_ref[...] = compact(gate, wide_ref[:, :half], cross_ref.shape[0])
    away.wait()


def prepare(tokens, w_down, expert_ids, gate_weights, expert_count, capacity):
    rows, half = tokens.shape
    shapes = [
        (rows, half + LANES),
        (capacity, half),
        (w_down.shape[1], half),
    ]
    whole = pl.BlockSpec(memory_space=pltpu.VMEM)
    return pl.pallas_call(
        functools.partial(prepare_kernel, expert_count),
        in_specs=[pl.BlockSpec(memory_space=pltpu.HBM)] * 4,
        out_specs=[whole] * len(shapes),
        out_shape=[pltpu.VMEM(shape, jnp.bfloat16) for shape in shapes],
        scratch_shapes=[
            pltpu.VMEM(expert_ids.shape[::-1], jnp.int32),
            pltpu.VMEM(gate_weights.shape[::-1], jnp.float32),
            pltpu.SemaphoreType.DMA((4,)),
        ],
        name="prepare",
        compiler_params=pltpu.CompilerParams(vmem_limit_bytes=VMEM_LIMIT),
        cost_estimate=pl.CostEstimate(flops=0, bytes_accessed=0, transcendentals=0),
    )(
        pltpu.with_memory_space_constraint(tokens, pltpu.HBM),
        pltpu.with_memory_space_constraint(w_down, pltpu.HBM),
        pltpu.with_memory_space_constraint(expert_ids.T, pltpu.HBM),
        pltpu.with_memory_space_constraint(gate_weights.T, pltpu.HBM),
    )


def cross_kernel(expert_count, wide_ref, cross_ref):
    half = cross_ref.shape[1]
    other = lax.axis_index("role") ^ 1
    gate = decode_gate(wide_ref[:, half:].astype(jnp.float32), other, expert_count)
    cross_ref[...] = compact(gate, wide_ref[:, :half], cross_ref.shape[0])


def cross_rows(wide, expert_count, capacity, hint=0):
    rows, width = wide.shape
    half = width - LANES
    return call(
        functools.partial(cross_kernel, expert_count),
        (wide,),
        ((capacity, half),),
        0,
        "cross_rows",
        hint=hint,
    )[0]


def row_starts(blocks):
    starts, rows = [], 0
    for block in blocks:
        starts.append(rows)
        rows += round_up(block.shape[0], 16)
    return tuple(starts), rows


def pack_kernel(starts, *refs):
    out_ref = refs[-1]
    for start, ref in zip(starts, refs):
        out_ref[start : start + ref.shape[0], :] = ref[:, : out_ref.shape[1]]


def pack(blocks, half, hint=0):
    starts, rows = row_starts(blocks)
    return call(
        functools.partial(pack_kernel, starts),
        blocks,
        ((rows, half),),
        0,
        "pack_rows",
        hint=hint,
    )[0]


def hidden_kernel(near_ref, far_ref, gate_ref, up_ref, hidden_ref):
    half = near_ref.shape[1]
    core = lax.axis_index("tp")
    own = pl.ds(pl.multiple_of(core * half, LANES), half)
    sibling = pl.ds(pl.multiple_of((1 - core) * half, LANES), half)
    width = 256
    for first in range(0, hidden_ref.shape[1], width):
        units = slice(first, first + width)
        gate_proj, up_proj = (
            jnp.dot(near_ref[...], ref[own, units], preferred_element_type=jnp.float32)
            + jnp.dot(far_ref[...], ref[sibling, units], preferred_element_type=jnp.float32)
            for ref in (gate_ref, up_ref)
        )
        hidden_ref[:, units] = (jax.nn.silu(gate_proj) * up_proj).astype(jnp.bfloat16)


def hidden_units(near, far, w_gate, w_up):
    return call(
        hidden_kernel,
        (near, far, w_gate, w_up),
        ((near.shape[0], w_gate.shape[1]),),
        0,
        "hidden_units",
    )[0]


def down_kernel(expert_count, starts, wide_count, *refs):
    wides = refs[:wide_count]
    own_ref, other_ref, down_ref, down_other_ref = refs[wide_count : wide_count + 4]
    outs = refs[wide_count + 4 :]
    half = down_other_ref.shape[1]
    me = lax.axis_index("role")
    base = pl.multiple_of(lax.axis_index("tp") * half, LANES)
    gates = [decode_gate(ref[:, half:].astype(jnp.float32), me, expert_count) for ref in wides]
    width = 256
    for first in range(0, half, width):
        columns = slice(first, first + width)
        result = jnp.dot(
            own_ref[...],
            down_ref[0, :, pl.ds(pl.multiple_of(base + first, LANES), width)],
            preferred_element_type=jnp.float32,
        ) + jnp.dot(
            other_ref[...], down_other_ref[:, columns], preferred_element_type=jnp.float32
        )
        for index, (start, out_ref) in enumerate(zip(starts, outs)):
            block = result[start : start + out_ref.shape[0]].astype(jnp.bfloat16)
            if index < wide_count:
                block = gates[index] * block.astype(jnp.float32)
            out_ref[:, columns] = block


def down(wides, cross_count, hidden, hidden_other, w_down, down_other, capacity, expert_count):
    half = down_other.shape[1]
    shapes = [(wide.shape[0], half) for wide in wides] + [(capacity, half)] * cross_count
    starts, rows = [], 0
    for shape in shapes:
        starts.append(rows)
        rows += round_up(shape[0], 16)
    return call(
        functools.partial(down_kernel, expert_count, tuple(starts), len(wides)),
        (*wides, hidden, hidden_other, w_down, down_other),
        tuple(shapes),
        4 * rows * half * hidden.shape[1],
        "down",
        (),
        [jnp.float32] * len(wides) + [jnp.bfloat16] * cross_count,
    )


def attend_kernel(query_ref, latent_ref, lengths_ref, placement_ref, out_ref):
    slot_count, head_count, _ = query_ref.shape
    rank, context = out_ref.shape[2], latent_ref.shape[2]
    first = lax.axis_index("role") * slot_count
    position = lax.broadcasted_iota(jnp.int32, (head_count, context), 1)
    for slot in range(slot_count):
        here = placement_ref[...] == first + slot
        length = jnp.sum(jnp.where(here, lengths_ref[...], 0), axis=1, keepdims=True)
        scores = (
            jnp.dot(query_ref[slot], latent_ref[slot], preferred_element_type=jnp.float32)
            * score_scale
        )
        scores = jnp.where(position < length, scores, -jnp.inf)
        raised = jnp.exp(scores - jnp.max(scores, axis=1, keepdims=True))
        attn_weights = (raised / jnp.sum(raised, axis=1, keepdims=True)).astype(jnp.bfloat16)
        out_ref[slot] = lax.dot_general(
            attn_weights,
            latent_ref[slot, :rank, :],
            (((1,), (1,)), ((), ())),
            preferred_element_type=jnp.float32,
        ).astype(jnp.bfloat16)


def attend(q_lat, latent_cache, lengths, placement):
    slot_count, head_count, _ = q_lat.shape
    return pl.pallas_call(
        attend_kernel,
        out_shape=jax.ShapeDtypeStruct((slot_count, head_count, KV_RANK), jnp.bfloat16),
        name="attend",
        compiler_params=pltpu.CompilerParams(vmem_limit_bytes=VMEM_LIMIT),
        cost_estimate=pl.CostEstimate(flops=0, bytes_accessed=0, transcendentals=0),
    )(q_lat, latent_cache.transpose(0, 2, 1), lengths[None, :], placement[None, :])


def combine_kernel(expert_count, first, sum_count, wide_ref, own_ref, back_ref, *refs):
    sums, outs = refs[:sum_count], refs[sum_count:]
    half = own_ref.shape[1]
    other = lax.axis_index("role") ^ 1
    gate = decode_gate(wide_ref[:, half:].astype(jnp.float32), other, expert_count)
    slots = slot_matrix(gate)[:, : back_ref.shape[0]]
    width = LANES
    for out_ref in outs:
        for column in range(0, out_ref.shape[1], width):
            columns = slice(first + column, first + column + width)
            spread = jnp.dot(slots, back_ref[:, columns], preferred_element_type=jnp.float32)
            result = own_ref[:, columns] + gate * spread
            for ref in sums:
                result = result + ref[:, column : column + width].astype(jnp.float32)
            out_ref[:, column : column + width] = result.astype(out_ref.dtype)
        first += out_ref.shape[1]


def combine(wide, own, back, sums, expert_count, first, widths, dtype=jnp.bfloat16):
    rows = own.shape[0]
    return call(
        functools.partial(combine_kernel, expert_count, first, len(sums)),
        (wide, own, back, *sums),
        tuple((rows, width) for width in widths),
        0,
        "combine",
        types=(dtype,) * len(widths),
    )


def add_kernel(*refs):
    out_ref = refs[-1]
    count = len(refs) // 2
    first = 0
    for total_ref, part_ref in zip(refs[:count], refs[count:-1]):
        result = total_ref[...] + part_ref[...].astype(jnp.float32)
        out_ref[:, first : first + part_ref.shape[1]] = result.astype(jnp.bfloat16)
        first += part_ref.shape[1]


def add_last(totals, parts):
    shape = (parts[0].shape[0], sum(part.shape[1] for part in parts))
    return call(add_kernel, (*totals, *parts), (shape,), 0, "add_last", last=True)[0]


def swap(array, bits, places=(0, 1, 2, 3)):
    count = lax.axis_size("role")
    pairs = [(device, device ^ bits) for device in range(count) if device // 2 in places]
    return lax.ppermute(array, "role", pairs)


def swap_core(array):
    return lax.ppermute(array, "tp", [(0, 1), (1, 0)])


def route_multicast(
    q_lat, latent_cache, lengths, placement, tokens, expert_ids, gate_weights, w_gate, w_up, w_down
):
    role_count = lax.axis_size("role")
    token_count, route_count = expert_ids.shape
    half = tokens.shape[1]
    capacity = 3 * token_count * route_count // (2 * role_count)
    pair, mirror, row = 2, 6, 1

    wide, cross, down_away = prepare(
        tokens, w_down, expert_ids, gate_weights, role_count, capacity
    )
    wide_pair = swap(wide, pair)
    cross_in = swap(cross, row)
    w_gate, w_up = w_gate[0], w_up[0]
    down_other = swap_core(down_away)
    attended = attend(after(q_lat, wide), latent_cache, lengths, placement)
    wide_mirror = swap(after(wide, attended), mirror)
    cross_in = after(cross_in, attended)
    wide_pair = after(wide_pair, cross_in, down_other)
    cross_pair = cross_rows(wide_pair, role_count, capacity)
    cross_pair_in = swap(cross_pair, row)
    wide_mirror = after(wide_mirror, cross_pair)
    wide_far = swap(wide_mirror, pair)
    cross_mirror = cross_rows(wide_mirror, role_count, capacity)
    cross_mirror_in = swap(cross_mirror, row)
    cross_pair_in = after(cross_pair_in, cross_mirror)
    near_first = pack((after(wide, cross_pair_in), wide_pair, wide_mirror, cross_in), half)
    far_first = swap_core(near_first)
    wide_far = after(wide_far, near_first)
    cross_mirror_in = after(cross_mirror_in, wide_far)
    wide_far = after(wide_far, cross_mirror_in)
    cross_far = cross_rows(wide_far, role_count, capacity, 10**10)
    cross_far_in = swap(cross_far, row)
    near_second = pack((wide_far, cross_pair_in, cross_mirror_in), half)
    far_second = swap_core(near_second)
    hidden = hidden_units(near_first, after(far_first, near_second), w_gate, w_up)
    hidden_other = swap_core(hidden)
    hidden_second = hidden_units(near_second, after(far_second, hidden), w_gate, w_up)
    hidden_second_other = swap_core(hidden_second)
    cross_far_in = after(cross_far_in, hidden_second)
    far_third = swap_core(cross_far_in)
    down_weights = (w_down, down_other)
    hidden_other = after(hidden_other, cross_far_in)
    own, own_pair, own_mirror, back_own = down(
        (wide, wide_pair, wide_mirror),
        1,
        hidden,
        hidden_other,
        *down_weights,
        capacity,
        role_count,
    )
    far_third = after(far_third, own)
    hidden_third = hidden_units(cross_far_in, far_third, w_gate, w_up)
    hidden_third_other = swap_core(hidden_third)
    hidden_second_other = after(hidden_second_other, hidden_third)
    own_far, back_pair, back_mirror = down(
        (wide_far,), 2, hidden_second, hidden_second_other, *down_weights, capacity, role_count
    )
    hidden_third_other = after(hidden_third_other, own_far)
    (back_far,) = down(
        (), 1, hidden_third, hidden_third_other, *down_weights, capacity, role_count
    )
    back_far = swap(back_far, row)
    back_mirror = swap(back_mirror, row)
    back_pair = swap(back_pair, row)
    back_own = swap(back_own, row)

    split = half // 2
    widths = (split, half - split)
    sum_far_left, sum_far_right = combine(
        wide_far, own_far, back_far, (), role_count, 0, widths
    )
    from_far_left = swap(sum_far_left, pair)
    from_far_right = swap(sum_far_right, pair)
    back_mirror = after(back_mirror, sum_far_left)
    from_far_left = after(from_far_left, back_mirror)
    (sum_mirror_left,) = combine(
        wide_mirror, own_mirror, back_mirror, (from_far_left,), role_count, 0, widths[:1]
    )
    from_mirror_left = swap(sum_mirror_left, mirror)
    from_far_right = after(from_far_right, sum_mirror_left)
    (sum_mirror_right,) = combine(
        wide_mirror, own_mirror, back_mirror, (from_far_right,), role_count, split, widths[1:]
    )
    from_mirror_right = swap(sum_mirror_right, mirror)
    back_pair = after(back_pair, sum_mirror_right)
    sum_pair_left, sum_pair_right = combine(
        wide_pair, own_pair, back_pair, (), role_count, 0, widths
    )
    from_pair_left = swap(sum_pair_left, pair)
    from_pair_right = swap(sum_pair_right, pair)
    back_own = after(back_own, sum_pair_left)
    from_mirror_left = after(from_mirror_left, back_own)
    (sum_left,) = combine(
        wide, own, back_own, (from_mirror_left,), role_count, 0, widths[:1], jnp.float32
    )
    from_mirror_right = after(from_mirror_right, sum_left)
    (sum_right,) = combine(
        wide, own, back_own, (from_mirror_right,), role_count, split, widths[1:], jnp.float32
    )
    from_pair_left = after(from_pair_left, sum_right)
    moe_result = add_last((sum_left, sum_right), (from_pair_left, from_pair_right))
    return (attended, moe_result)


def shards(
    q_lat, latent_cache, lengths, placement, tokens, expert_ids, gate_weights, w_gate, w_up, w_down
):
    if lax.axis_size("role") == 8 and lax.axis_size("tp") == 2:
        return route_multicast(
            q_lat,
            latent_cache,
            lengths,
            placement,
            tokens,
            expert_ids,
            gate_weights,
            w_gate,
            w_up,
            w_down,
        )
    attended = attend_local(q_lat, latent_cache, lengths, placement)
    routed = route_all_to_all(tokens, expert_ids, gate_weights, w_gate, w_up, w_down)
    return (attended, routed)


def solution(mesh):
    return jax.shard_map(
        shards,
        mesh=mesh,
        in_specs=(
            P(("groups", "role"), "tp", None),
            P(("groups", "role"), None, None),
            P("groups"),
            P("groups"),
            P(("groups", "role"), "tp"),
            P(("groups", "role"), None),
            P(("groups", "role"), None),
            P("role", None, "tp"),
            P("role", None, "tp"),
            P("role", "tp", None),
        ),
        out_specs=(P(("groups", "role"), "tp", None), P(("groups", "role"), "tp")),
        check_vma=False,
    )
```

```python
import functools

import jax
import jax.numpy as jnp
from jax import lax
from jax.experimental import pallas as pl
from jax.experimental.pallas import tpu as pltpu
from jax.sharding import PartitionSpec as P

KV_RANK = 512


score_scale = 192.0 ** (-0.5)


def attend_local(q_lat, latent_cache, lengths, placement):
    slot_count = q_lat.shape[0]
    offset = lax.axis_index("role") * slot_count
    slot_ids = offset + jnp.arange(slot_count, dtype=jnp.int32)
    matches = placement[None, :] == slot_ids[:, None]
    slot_length = jnp.sum(jnp.where(matches, lengths[None, :], 0), axis=1)
    scores = (
        jnp.einsum("shc,stc->sht", q_lat, latent_cache, preferred_element_type=jnp.float32)
        * score_scale
    )
    position = jnp.arange(latent_cache.shape[1], dtype=jnp.int32)
    visible = position[None, None, :] < slot_length[:, None, None]
    scores = jnp.where(visible, scores, -jnp.inf)
    highest = jnp.max(scores, axis=2, keepdims=True)
    raised = jnp.exp(scores - highest)
    attn_weights = (raised / jnp.sum(raised, axis=2, keepdims=True)).astype(jnp.bfloat16)
    values = latent_cache[:, :, :KV_RANK]
    return jnp.einsum(
        "sht,stc->shc", attn_weights, values, preferred_element_type=jnp.float32
    ).astype(jnp.bfloat16)


def route_all_to_all(tokens, expert_ids, gate_weights, w_gate, w_up, w_down):
    role_count = lax.axis_size("role")
    token_count = expert_ids.shape[0]
    route_count = expert_ids.shape[1]
    capacity = 3 * token_count * route_count // (2 * role_count)
    flat_ids = expert_ids.reshape(-1)
    onehot = (flat_ids[:, None] == jnp.arange(role_count, dtype=jnp.int32)[None, :]).astype(
        jnp.int32
    )
    earlier = jnp.cumsum(onehot, axis=0) - onehot
    slot_index = jnp.sum(earlier * onehot, axis=1)
    target = flat_ids * capacity + slot_index
    source = jnp.arange(token_count * route_count, dtype=jnp.int32) // route_count
    outgoing = lax.all_gather(tokens, "tp", axis=1, tiled=True)
    columns = outgoing.shape[1]
    buffer_rows = (
        jnp.zeros((role_count * capacity, columns), jnp.bfloat16).at[target].set(outgoing[source])
    )
    buffer_rows = buffer_rows.reshape(role_count, capacity, columns)
    gate_matrix = w_gate[0]
    up_matrix = w_up[0]
    down_matrix = w_down[0]
    received = lax.all_to_all(buffer_rows, "role", split_axis=0, concat_axis=0, tiled=True)
    item_count = received.shape[1]
    arrived = received.reshape(role_count * item_count, columns)
    gate_proj = jnp.dot(arrived, gate_matrix, preferred_element_type=jnp.float32)
    up_proj = jnp.dot(arrived, up_matrix, preferred_element_type=jnp.float32)
    expert_hidden = (jax.nn.silu(gate_proj) * up_proj).astype(jnp.bfloat16)
    partial_out = jnp.dot(expert_hidden, down_matrix, preferred_element_type=jnp.float32)
    summed = lax.psum_scatter(
        partial_out.astype(jnp.bfloat16), "tp", scatter_dimension=1, tiled=True
    )
    summed = summed.reshape(role_count, item_count, summed.shape[1])
    returned = lax.all_to_all(summed, "role", split_axis=0, concat_axis=0, tiled=True)
    half_width = returned.shape[2]
    flat_back = returned.reshape(role_count * capacity, half_width)
    chosen_rows = (
        flat_back[target].reshape(token_count, route_count, half_width).astype(jnp.float32)
    )
    moe_result = jnp.sum(chosen_rows * gate_weights[:, :, None], axis=1).astype(jnp.bfloat16)
    return moe_result


LANES = 128
VMEM_LIMIT = 16 * 1024 * 1024


def round_up(value, unit):
    return -(-value // unit) * unit


def call(kernel, operands, out_shapes, flops, name, scratch=(), types=None, last=False, hint=0):
    place = pl.BlockSpec(memory_space=pltpu.VMEM)
    return pl.pallas_call(
        kernel,
        in_specs=[place] * len(operands),
        out_specs=[place] * len(out_shapes),
        out_shape=[
            (jax.ShapeDtypeStruct if last else pltpu.VMEM)(
                shape, jnp.bfloat16 if types is None else types[index]
            )
            for index, shape in enumerate(out_shapes)
        ],
        scratch_shapes=list(scratch),
        name=name,
        compiler_params=pltpu.CompilerParams(vmem_limit_bytes=VMEM_LIMIT),
        cost_estimate=pl.CostEstimate(flops=hint, bytes_accessed=0, transcendentals=0),
    )(*[pltpu.with_memory_space_constraint(operand, pltpu.VMEM) for operand in operands])


def after(value, *earlier):
    return lax.optimization_barrier((value, *earlier))[0]


def lane_index(rows):
    return lax.broadcasted_iota(jnp.int32, (rows, LANES), 1)


def decode_gate(pieces, expert, expert_count):
    lane = lane_index(pieces.shape[0])
    wanted = lane == expert
    for piece in (1, 2):
        wanted = wanted | (lane == expert + piece * expert_count)
    return jnp.sum(jnp.where(wanted, pieces, 0.0), axis=1, keepdims=True)


def slot_matrix(gate):
    rows = gate.shape[0]
    named = jnp.broadcast_to((gate > 0.0).astype(jnp.float32), (rows, LANES))
    lower = lax.broadcasted_iota(jnp.int32, (rows, rows), 0) >= lax.broadcasted_iota(
        jnp.int32, (rows, rows), 1
    )
    rank = jnp.dot(
        lower.astype(jnp.bfloat16), named.astype(jnp.bfloat16), preferred_element_type=jnp.float32
    )
    slot = lane_index(rows).astype(jnp.float32)
    return jnp.where((named > 0.0) & (rank - 1.0 == slot), 1.0, 0.0).astype(jnp.bfloat16)


def compact(gate, rows_in, capacity):
    picked = lax.dot_general(
        slot_matrix(gate),
        rows_in,
        (((0,), (0,)), ((), ())),
        preferred_element_type=jnp.float32,
    )
    return picked[:capacity].astype(jnp.bfloat16)


def prepare_kernel(
    expert_count,
    tokens_hbm,
    down_hbm,
    ids_hbm,
    gates_hbm,
    wide_ref,
    cross_ref,
    away_ref,
    ids_ref,
    gates_ref,
    sems,
):
    rows, half = tokens_hbm.shape
    copy = pltpu.make_async_copy(tokens_hbm, wide_ref.at[:, :half], sems.at[0])
    first = [
        pltpu.make_async_copy(ids_hbm, ids_ref, sems.at[2]),
        pltpu.make_async_copy(gates_hbm, gates_ref, sems.at[3]),
    ]
    for part in first:
        part.start()
    copy.start()
    sibling = pl.multiple_of((1 - lax.axis_index("tp")) * half, LANES)
    away = pltpu.make_async_copy(down_hbm.at[0, :, pl.ds(sibling, half)], away_ref, sems.at[1])
    away.start()
    for part in first:
        part.wait()
    piece_rows = round_up(3 * expert_count, 16)
    line = lax.broadcasted_iota(jnp.int32, (piece_rows, rows), 0)
    named = line
    for piece in (1, 2):
        named = jnp.where(line >= piece * expert_count, line - piece * expert_count, named)
    dense = jnp.zeros((piece_rows, rows), jnp.float32)
    for choice in range(ids_ref.shape[0]):
        dense = dense + jnp.where(
            ids_ref[choice : choice + 1, :] == named, gates_ref[choice : choice + 1, :], 0.0
        )
    high = dense.astype(jnp.bfloat16).astype(jnp.float32)
    middle = (dense - high).astype(jnp.bfloat16).astype(jnp.float32)
    low = dense - high - middle
    pieces = jnp.where(line < expert_count, high, jnp.where(line < 2 * expert_count, middle, low))
    unit = lax.broadcasted_iota(jnp.int32, (piece_rows, LANES), 0) == lax.broadcasted_iota(
        jnp.int32, (piece_rows, LANES), 1
    )
    turned = lax.dot_general(
        pieces.astype(jnp.bfloat16),
        unit.astype(jnp.bfloat16),
        (((0,), (0,)), ((), ())),
        preferred_element_type=jnp.float32,
    )
    wide_ref[:, half:] = turned.astype(jnp.bfloat16)
    copy.wait()
    gate = decode_gate(turned, lax.axis_index("role") ^ 1, expert_count)
    cross_ref[...] = compact(gate, wide_ref[:, :half], cross_ref.shape[0])
    away.wait()


def prepare(tokens, w_down, expert_ids, gate_weights, expert_count, capacity):
    rows, half = tokens.shape
    shapes = [
        (rows, half + LANES),
        (capacity, half),
        (w_down.shape[1], half),
    ]
    whole = pl.BlockSpec(memory_space=pltpu.VMEM)
    return pl.pallas_call(
        functools.partial(prepare_kernel, expert_count),
        in_specs=[pl.BlockSpec(memory_space=pltpu.HBM)] * 4,
        out_specs=[whole] * len(shapes),
        out_shape=[pltpu.VMEM(shape, jnp.bfloat16) for shape in shapes],
        scratch_shapes=[
            pltpu.VMEM(expert_ids.shape[::-1], jnp.int32),
            pltpu.VMEM(gate_weights.shape[::-1], jnp.float32),
            pltpu.SemaphoreType.DMA((4,)),
        ],
        name="prepare",
        compiler_params=pltpu.CompilerParams(vmem_limit_bytes=VMEM_LIMIT),
        cost_estimate=pl.CostEstimate(flops=0, bytes_accessed=0, transcendentals=0),
    )(
        pltpu.with_memory_space_constraint(tokens, pltpu.HBM),
        pltpu.with_memory_space_constraint(w_down, pltpu.HBM),
        pltpu.with_memory_space_constraint(expert_ids.T, pltpu.HBM),
        pltpu.with_memory_space_constraint(gate_weights.T, pltpu.HBM),
    )


def cross_kernel(expert_count, wide_ref, cross_ref):
    half = cross_ref.shape[1]
    other = lax.axis_index("role") ^ 1
    gate = decode_gate(wide_ref[:, half:].astype(jnp.float32), other, expert_count)
    cross_ref[...] = compact(gate, wide_ref[:, :half], cross_ref.shape[0])


def cross_rows(wide, expert_count, capacity, hint=0):
    rows, width = wide.shape
    half = width - LANES
    return call(
        functools.partial(cross_kernel, expert_count),
        (wide,),
        ((capacity, half),),
        0,
        "cross_rows",
        hint=hint,
    )[0]


def row_starts(blocks):
    starts, rows = [], 0
    for block in blocks:
        starts.append(rows)
        rows += round_up(block.shape[0], 16)
    return tuple(starts), rows


def pack_kernel(starts, *refs):
    out_ref = refs[-1]
    for start, ref in zip(starts, refs):
        out_ref[start : start + ref.shape[0], :] = ref[:, : out_ref.shape[1]]


def pack(blocks, half, hint=0):
    starts, rows = row_starts(blocks)
    return call(
        functools.partial(pack_kernel, starts),
        blocks,
        ((rows, half),),
        0,
        "pack_rows",
        hint=hint,
    )[0]


def hidden_kernel(near_ref, far_ref, gate_ref, up_ref, hidden_ref):
    half = near_ref.shape[1]
    core = lax.axis_index("tp")
    own = pl.ds(pl.multiple_of(core * half, LANES), half)
    sibling = pl.ds(pl.multiple_of((1 - core) * half, LANES), half)
    width = 256
    for first in range(0, hidden_ref.shape[1], width):
        units = slice(first, first + width)
        gate_proj, up_proj = (
            jnp.dot(near_ref[...], ref[own, units], preferred_element_type=jnp.float32)
            + jnp.dot(far_ref[...], ref[sibling, units], preferred_element_type=jnp.float32)
            for ref in (gate_ref, up_ref)
        )
        hidden_ref[:, units] = (jax.nn.silu(gate_proj) * up_proj).astype(jnp.bfloat16)


def hidden_units(near, far, w_gate, w_up):
    return call(
        hidden_kernel,
        (near, far, w_gate, w_up),
        ((near.shape[0], w_gate.shape[1]),),
        0,
        "hidden_units",
    )[0]


def down_kernel(expert_count, starts, wide_count, *refs):
    wides = refs[:wide_count]
    own_ref, other_ref, down_ref, down_other_ref = refs[wide_count : wide_count + 4]
    outs = refs[wide_count + 4 :]
    half = down_other_ref.shape[1]
    me = lax.axis_index("role")
    base = pl.multiple_of(lax.axis_index("tp") * half, LANES)
    gates = [decode_gate(ref[:, half:].astype(jnp.float32), me, expert_count) for ref in wides]
    width = 256
    for first in range(0, half, width):
        columns = slice(first, first + width)
        result = jnp.dot(
            own_ref[...],
            down_ref[0, :, pl.ds(pl.multiple_of(base + first, LANES), width)],
            preferred_element_type=jnp.float32,
        ) + jnp.dot(
            other_ref[...], down_other_ref[:, columns], preferred_element_type=jnp.float32
        )
        for index, (start, out_ref) in enumerate(zip(starts, outs)):
            block = result[start : start + out_ref.shape[0]].astype(jnp.bfloat16)
            if index < wide_count:
                block = gates[index] * block.astype(jnp.float32)
            out_ref[:, columns] = block


def down(wides, cross_count, hidden, hidden_other, w_down, down_other, capacity, expert_count):
    half = down_other.shape[1]
    shapes = [(wide.shape[0], half) for wide in wides] + [(capacity, half)] * cross_count
    starts, rows = [], 0
    for shape in shapes:
        starts.append(rows)
        rows += round_up(shape[0], 16)
    return call(
        functools.partial(down_kernel, expert_count, tuple(starts), len(wides)),
        (*wides, hidden, hidden_other, w_down, down_other),
        tuple(shapes),
        4 * rows * half * hidden.shape[1],
        "down",
        (),
        [jnp.float32] * len(wides) + [jnp.bfloat16] * cross_count,
    )


def attend_kernel(query_ref, latent_ref, lengths_ref, placement_ref, out_ref):
    slot_count, head_count, _ = query_ref.shape
    rank, context = out_ref.shape[2], latent_ref.shape[2]
    first = lax.axis_index("role") * slot_count
    position = lax.broadcasted_iota(jnp.int32, (head_count, context), 1)
    for slot in range(slot_count):
        here = placement_ref[...] == first + slot
        length = jnp.sum(jnp.where(here, lengths_ref[...], 0), axis=1, keepdims=True)
        scores = (
            jnp.dot(query_ref[slot], latent_ref[slot], preferred_element_type=jnp.float32)
            * score_scale
        )
        scores = jnp.where(position < length, scores, -jnp.inf)
        raised = jnp.exp(scores - jnp.max(scores, axis=1, keepdims=True))
        attn_weights = (raised / jnp.sum(raised, axis=1, keepdims=True)).astype(jnp.bfloat16)
        out_ref[slot] = lax.dot_general(
            attn_weights,
            latent_ref[slot, :rank, :],
            (((1,), (1,)), ((), ())),
            preferred_element_type=jnp.float32,
        ).astype(jnp.bfloat16)


def attend(q_lat, latent_cache, lengths, placement):
    slot_count, head_count, _ = q_lat.shape
    return pl.pallas_call(
        attend_kernel,
        out_shape=jax.ShapeDtypeStruct((slot_count, head_count, KV_RANK), jnp.bfloat16),
        name="attend",
        compiler_params=pltpu.CompilerParams(vmem_limit_bytes=VMEM_LIMIT),
        cost_estimate=pl.CostEstimate(flops=0, bytes_accessed=0, transcendentals=0),
    )(q_lat, latent_cache.transpose(0, 2, 1), lengths[None, :], placement[None, :])


def last_down_kernel(own_ref, other_ref, down_ref, down_other_ref, *outs):
    half = down_other_ref.shape[1]
    base = pl.multiple_of(lax.axis_index("tp") * half, LANES)
    start = 0
    for out_ref in outs:
        for first in range(0, out_ref.shape[1], 256):
            width = min(256, out_ref.shape[1] - first)
            column = start + first
            result = jnp.dot(
                own_ref[...],
                down_ref[0, :, pl.ds(pl.multiple_of(base + column, LANES), width)],
                preferred_element_type=jnp.float32,
            ) + jnp.dot(
                other_ref[...],
                down_other_ref[:, column : column + width],
                preferred_element_type=jnp.float32,
            )
            out_ref[:, first : first + width] = result[: out_ref.shape[0]].astype(jnp.bfloat16)
        start += out_ref.shape[1]


def last_down(hidden, hidden_other, w_down, down_other, capacity, widths):
    return call(
        last_down_kernel,
        (hidden, hidden_other, w_down, down_other),
        tuple((capacity, width) for width in widths),
        0,
        "last_down",
    )


def combine_kernel(expert_count, first, shift, sum_count, wide_ref, own_ref, back_ref, *refs):
    sums, outs = refs[:sum_count], refs[sum_count:]
    half = own_ref.shape[1]
    other = lax.axis_index("role") ^ 1
    gate = decode_gate(wide_ref[:, half:].astype(jnp.float32), other, expert_count)
    slots = slot_matrix(gate)[:, : back_ref.shape[0]]
    width = LANES
    for out_ref in outs:
        for column in range(0, out_ref.shape[1], width):
            columns = slice(first + column, first + column + width)
            spread = jnp.dot(
                slots,
                back_ref[:, columns.start - shift : columns.stop - shift],
                preferred_element_type=jnp.float32,
            )
            result = own_ref[:, columns] + gate * spread
            for ref in sums:
                result = result + ref[:, column : column + width].astype(jnp.float32)
            out_ref[:, column : column + width] = result.astype(out_ref.dtype)
        first += out_ref.shape[1]


def combine(
    wide, own, back, sums, expert_count, first, widths, dtype=jnp.bfloat16, shift=0, hint=0
):
    rows = own.shape[0]
    return call(
        functools.partial(combine_kernel, expert_count, first, shift, len(sums)),
        (wide, own, back, *sums),
        tuple((rows, width) for width in widths),
        0,
        "combine",
        types=(dtype,) * len(widths),
        hint=hint,
    )


def add_kernel(*refs):
    out_ref = refs[-1]
    count = len(refs) // 2
    first = 0
    for total_ref, part_ref in zip(refs[:count], refs[count:-1]):
        result = total_ref[...] + part_ref[...].astype(jnp.float32)
        out_ref[:, first : first + part_ref.shape[1]] = result.astype(jnp.bfloat16)
        first += part_ref.shape[1]


def add_last(totals, parts):
    shape = (parts[0].shape[0], sum(part.shape[1] for part in parts))
    return call(add_kernel, (*totals, *parts), (shape,), 0, "add_last", last=True)[0]


def swap(array, bits, places=(0, 1, 2, 3)):
    count = lax.axis_size("role")
    pairs = [(device, device ^ bits) for device in range(count) if device // 2 in places]
    return lax.ppermute(array, "role", pairs)


def swap_core(array):
    return lax.ppermute(array, "tp", [(0, 1), (1, 0)])


def route_multicast(
    q_lat, latent_cache, lengths, placement, tokens, expert_ids, gate_weights, w_gate, w_up, w_down
):
    role_count = lax.axis_size("role")
    token_count, route_count = expert_ids.shape
    half = tokens.shape[1]
    capacity = 3 * token_count * route_count // (2 * role_count)
    pair, mirror, row = 2, 6, 1

    wide, cross, down_away = prepare(
        tokens, w_down, expert_ids, gate_weights, role_count, capacity
    )
    wide_pair = swap(wide, pair)
    cross_in = swap(cross, row)
    w_gate, w_up = w_gate[0], w_up[0]
    down_other = swap_core(down_away)
    attended = attend(after(q_lat, wide), latent_cache, lengths, placement)
    wide_mirror = swap(after(wide, attended), mirror)
    cross_in = after(cross_in, attended)
    wide_pair = after(wide_pair, cross_in, down_other)
    cross_pair = cross_rows(wide_pair, role_count, capacity)
    cross_pair_in = swap(cross_pair, row)
    wide_mirror = after(wide_mirror, cross_pair)
    wide_far = swap(wide_mirror, pair)
    cross_mirror = cross_rows(wide_mirror, role_count, capacity)
    cross_mirror_in = swap(cross_mirror, row)
    cross_pair_in = after(cross_pair_in, cross_mirror)
    near_first = pack((after(wide, cross_pair_in), wide_pair, wide_mirror, cross_in), half)
    far_first = swap_core(near_first)
    wide_far = after(wide_far, near_first)
    cross_mirror_in = after(cross_mirror_in, wide_far)
    wide_far = after(wide_far, cross_mirror_in)
    cross_far = cross_rows(wide_far, role_count, capacity, 10**10)
    cross_far_in = swap(cross_far, row)
    near_second = pack((wide_far, cross_pair_in, cross_mirror_in), half)
    far_second = swap_core(near_second)
    hidden = hidden_units(near_first, after(far_first, near_second), w_gate, w_up)
    hidden_other = swap_core(hidden)
    hidden_second = hidden_units(near_second, after(far_second, hidden), w_gate, w_up)
    hidden_second_other = swap_core(hidden_second)
    cross_far_in = after(cross_far_in, hidden_second)
    far_third = swap_core(cross_far_in)
    down_weights = (w_down, down_other)
    hidden_other = after(hidden_other, cross_far_in)
    own, own_pair, own_mirror, back_own = down(
        (wide, wide_pair, wide_mirror),
        1,
        hidden,
        hidden_other,
        *down_weights,
        capacity,
        role_count,
    )
    far_third = after(far_third, own)
    hidden_third = hidden_units(cross_far_in, far_third, w_gate, w_up)
    hidden_third_other = swap_core(hidden_third)
    hidden_second_other = after(hidden_second_other, hidden_third)
    own_far, back_pair, back_mirror = down(
        (wide_far,), 2, hidden_second, hidden_second_other, *down_weights, capacity, role_count
    )
    hidden_third_other = after(hidden_third_other, own_far)
    split = half // 2
    widths = (split, half - split)
    back_far_left, back_far_right = last_down(
        hidden_third, hidden_third_other, *down_weights, capacity, widths
    )
    back_far_left = swap(back_far_left, row)
    back_far_right = swap(back_far_right, row)
    back_mirror = swap(back_mirror, row)
    back_pair = swap(back_pair, row)
    back_own = swap(back_own, row)

    (sum_far_left,) = combine(
        wide_far, own_far, back_far_left, (), role_count, 0, widths[:1]
    )
    from_far_left = swap(sum_far_left, pair)
    back_far_right = after(back_far_right, sum_far_left)
    (sum_far_right,) = combine(
        wide_far,
        own_far,
        back_far_right,
        (),
        role_count,
        split,
        widths[1:],
        shift=split,
    )
    from_far_right = swap(sum_far_right, pair)
    back_mirror = after(back_mirror, sum_far_right)
    from_far_left = after(from_far_left, back_mirror)
    (sum_mirror_left,) = combine(
        wide_mirror, own_mirror, back_mirror, (from_far_left,), role_count, 0, widths[:1]
    )
    from_mirror_left = swap(sum_mirror_left, mirror)
    from_far_right = after(from_far_right, sum_mirror_left)
    (sum_mirror_right,) = combine(
        wide_mirror, own_mirror, back_mirror, (from_far_right,), role_count, split, widths[1:]
    )
    from_mirror_right = swap(sum_mirror_right, mirror)
    back_pair = after(back_pair, sum_mirror_right)
    sum_pair_left, sum_pair_right = combine(
        wide_pair, own_pair, back_pair, (), role_count, 0, widths
    )
    from_pair_left = swap(sum_pair_left, pair)
    from_pair_right = swap(sum_pair_right, pair)
    back_own = after(back_own, sum_pair_left)
    from_mirror_left = after(from_mirror_left, back_own)
    (sum_left,) = combine(
        wide, own, back_own, (from_mirror_left,), role_count, 0, widths[:1], jnp.float32
    )
    from_mirror_right = after(from_mirror_right, sum_left)
    (sum_right,) = combine(
        wide, own, back_own, (from_mirror_right,), role_count, split, widths[1:], jnp.float32
    )
    from_pair_left = after(from_pair_left, sum_right)
    moe_result = add_last((sum_left, sum_right), (from_pair_left, from_pair_right))
    return (attended, moe_result)


def shards(
    q_lat, latent_cache, lengths, placement, tokens, expert_ids, gate_weights, w_gate, w_up, w_down
):
    if lax.axis_size("role") == 8 and lax.axis_size("tp") == 2:
        return route_multicast(
            q_lat,
            latent_cache,
            lengths,
            placement,
            tokens,
            expert_ids,
            gate_weights,
            w_gate,
            w_up,
            w_down,
        )
    attended = attend_local(q_lat, latent_cache, lengths, placement)
    routed = route_all_to_all(tokens, expert_ids, gate_weights, w_gate, w_up, w_down)
    return (attended, routed)


def solution(mesh):
    return jax.shard_map(
        shards,
        mesh=mesh,
        in_specs=(
            P(("groups", "role"), "tp", None),
            P(("groups", "role"), None, None),
            P("groups"),
            P("groups"),
            P(("groups", "role"), "tp"),
            P(("groups", "role"), None),
            P(("groups", "role"), None),
            P("role", None, "tp"),
            P("role", None, "tp"),
            P("role", "tp", None),
        ),
        out_specs=(P(("groups", "role"), "tp", None), P(("groups", "role"), "tp")),
        check_vma=False,
    )
```

```python
import functools

import jax
import jax.numpy as jnp
from jax import lax
from jax.experimental import pallas as pl
from jax.experimental.pallas import tpu as pltpu
from jax.sharding import PartitionSpec as P

KV_RANK = 512


score_scale = 192.0 ** (-0.5)


def attend_local(q_lat, latent_cache, lengths, placement):
    slot_count = q_lat.shape[0]
    offset = lax.axis_index("role") * slot_count
    slot_ids = offset + jnp.arange(slot_count, dtype=jnp.int32)
    matches = placement[None, :] == slot_ids[:, None]
    slot_length = jnp.sum(jnp.where(matches, lengths[None, :], 0), axis=1)
    scores = (
        jnp.einsum("shc,stc->sht", q_lat, latent_cache, preferred_element_type=jnp.float32)
        * score_scale
    )
    position = jnp.arange(latent_cache.shape[1], dtype=jnp.int32)
    visible = position[None, None, :] < slot_length[:, None, None]
    scores = jnp.where(visible, scores, -jnp.inf)
    highest = jnp.max(scores, axis=2, keepdims=True)
    raised = jnp.exp(scores - highest)
    attn_weights = (raised / jnp.sum(raised, axis=2, keepdims=True)).astype(jnp.bfloat16)
    values = latent_cache[:, :, :KV_RANK]
    return jnp.einsum(
        "sht,stc->shc", attn_weights, values, preferred_element_type=jnp.float32
    ).astype(jnp.bfloat16)


def route_all_to_all(tokens, expert_ids, gate_weights, w_gate, w_up, w_down):
    role_count = lax.axis_size("role")
    token_count = expert_ids.shape[0]
    route_count = expert_ids.shape[1]
    capacity = 3 * token_count * route_count // (2 * role_count)
    flat_ids = expert_ids.reshape(-1)
    onehot = (flat_ids[:, None] == jnp.arange(role_count, dtype=jnp.int32)[None, :]).astype(
        jnp.int32
    )
    earlier = jnp.cumsum(onehot, axis=0) - onehot
    slot_index = jnp.sum(earlier * onehot, axis=1)
    target = flat_ids * capacity + slot_index
    source = jnp.arange(token_count * route_count, dtype=jnp.int32) // route_count
    outgoing = lax.all_gather(tokens, "tp", axis=1, tiled=True)
    columns = outgoing.shape[1]
    buffer_rows = (
        jnp.zeros((role_count * capacity, columns), jnp.bfloat16).at[target].set(outgoing[source])
    )
    buffer_rows = buffer_rows.reshape(role_count, capacity, columns)
    gate_matrix = w_gate[0]
    up_matrix = w_up[0]
    down_matrix = w_down[0]
    received = lax.all_to_all(buffer_rows, "role", split_axis=0, concat_axis=0, tiled=True)
    item_count = received.shape[1]
    arrived = received.reshape(role_count * item_count, columns)
    gate_proj = jnp.dot(arrived, gate_matrix, preferred_element_type=jnp.float32)
    up_proj = jnp.dot(arrived, up_matrix, preferred_element_type=jnp.float32)
    expert_hidden = (jax.nn.silu(gate_proj) * up_proj).astype(jnp.bfloat16)
    partial_out = jnp.dot(expert_hidden, down_matrix, preferred_element_type=jnp.float32)
    summed = lax.psum_scatter(
        partial_out.astype(jnp.bfloat16), "tp", scatter_dimension=1, tiled=True
    )
    summed = summed.reshape(role_count, item_count, summed.shape[1])
    returned = lax.all_to_all(summed, "role", split_axis=0, concat_axis=0, tiled=True)
    half_width = returned.shape[2]
    flat_back = returned.reshape(role_count * capacity, half_width)
    chosen_rows = (
        flat_back[target].reshape(token_count, route_count, half_width).astype(jnp.float32)
    )
    moe_result = jnp.sum(chosen_rows * gate_weights[:, :, None], axis=1).astype(jnp.bfloat16)
    return moe_result


LANES = 128
VMEM_LIMIT = 16 * 1024 * 1024


def round_up(value, unit):
    return -(-value // unit) * unit


def call(kernel, operands, out_shapes, flops, name, scratch=(), types=None, last=False, hint=0):
    place = pl.BlockSpec(memory_space=pltpu.VMEM)
    return pl.pallas_call(
        kernel,
        in_specs=[place] * len(operands),
        out_specs=[place] * len(out_shapes),
        out_shape=[
            (jax.ShapeDtypeStruct if last else pltpu.VMEM)(
                shape, jnp.bfloat16 if types is None else types[index]
            )
            for index, shape in enumerate(out_shapes)
        ],
        scratch_shapes=list(scratch),
        name=name,
        compiler_params=pltpu.CompilerParams(vmem_limit_bytes=VMEM_LIMIT),
        cost_estimate=pl.CostEstimate(flops=hint, bytes_accessed=0, transcendentals=0),
    )(*[pltpu.with_memory_space_constraint(operand, pltpu.VMEM) for operand in operands])


def after(value, *earlier):
    return lax.optimization_barrier((value, *earlier))[0]


def lane_index(rows):
    return lax.broadcasted_iota(jnp.int32, (rows, LANES), 1)


def decode_gate(pieces, expert, expert_count):
    lane = lane_index(pieces.shape[0])
    wanted = lane == expert
    for piece in (1, 2):
        wanted = wanted | (lane == expert + piece * expert_count)
    return jnp.sum(jnp.where(wanted, pieces, 0.0), axis=1, keepdims=True)


def slot_matrix(gate):
    rows = gate.shape[0]
    named = jnp.broadcast_to((gate > 0.0).astype(jnp.float32), (rows, LANES))
    lower = lax.broadcasted_iota(jnp.int32, (rows, rows), 0) >= lax.broadcasted_iota(
        jnp.int32, (rows, rows), 1
    )
    rank = jnp.dot(
        lower.astype(jnp.bfloat16), named.astype(jnp.bfloat16), preferred_element_type=jnp.float32
    )
    slot = lane_index(rows).astype(jnp.float32)
    return jnp.where((named > 0.0) & (rank - 1.0 == slot), 1.0, 0.0).astype(jnp.bfloat16)


def compact(gate, rows_in, capacity):
    picked = lax.dot_general(
        slot_matrix(gate),
        rows_in,
        (((0,), (0,)), ((), ())),
        preferred_element_type=jnp.float32,
    )
    return picked[:capacity].astype(jnp.bfloat16)


def prepare_kernel(
    expert_count,
    tokens_hbm,
    down_hbm,
    ids_hbm,
    gates_hbm,
    wide_ref,
    cross_ref,
    away_ref,
    ids_ref,
    gates_ref,
    sems,
):
    rows, half = tokens_hbm.shape
    copy = pltpu.make_async_copy(tokens_hbm, wide_ref.at[:, :half], sems.at[0])
    first = [
        pltpu.make_async_copy(ids_hbm, ids_ref, sems.at[2]),
        pltpu.make_async_copy(gates_hbm, gates_ref, sems.at[3]),
    ]
    for part in first:
        part.start()
    copy.start()
    sibling = pl.multiple_of((1 - lax.axis_index("tp")) * half, LANES)
    away = pltpu.make_async_copy(down_hbm.at[0, :, pl.ds(sibling, half)], away_ref, sems.at[1])
    away.start()
    for part in first:
        part.wait()
    piece_rows = round_up(3 * expert_count, 16)
    line = lax.broadcasted_iota(jnp.int32, (piece_rows, rows), 0)
    named = line
    for piece in (1, 2):
        named = jnp.where(line >= piece * expert_count, line - piece * expert_count, named)
    dense = jnp.zeros((piece_rows, rows), jnp.float32)
    for choice in range(ids_ref.shape[0]):
        dense = dense + jnp.where(
            ids_ref[choice : choice + 1, :] == named, gates_ref[choice : choice + 1, :], 0.0
        )
    high = dense.astype(jnp.bfloat16).astype(jnp.float32)
    middle = (dense - high).astype(jnp.bfloat16).astype(jnp.float32)
    low = dense - high - middle
    pieces = jnp.where(line < expert_count, high, jnp.where(line < 2 * expert_count, middle, low))
    unit = lax.broadcasted_iota(jnp.int32, (piece_rows, LANES), 0) == lax.broadcasted_iota(
        jnp.int32, (piece_rows, LANES), 1
    )
    turned = lax.dot_general(
        pieces.astype(jnp.bfloat16),
        unit.astype(jnp.bfloat16),
        (((0,), (0,)), ((), ())),
        preferred_element_type=jnp.float32,
    )
    wide_ref[:, half:] = turned.astype(jnp.bfloat16)
    copy.wait()
    gate = decode_gate(turned, lax.axis_index("role") ^ 1, expert_count)
    cross_ref[...] = compact(gate, wide_ref[:, :half], cross_ref.shape[0])
    away.wait()


def prepare(tokens, w_down, expert_ids, gate_weights, expert_count, capacity):
    rows, half = tokens.shape
    shapes = [
        (rows, half + LANES),
        (capacity, half),
        (w_down.shape[1], half),
    ]
    whole = pl.BlockSpec(memory_space=pltpu.VMEM)
    return pl.pallas_call(
        functools.partial(prepare_kernel, expert_count),
        in_specs=[pl.BlockSpec(memory_space=pltpu.HBM)] * 4,
        out_specs=[whole] * len(shapes),
        out_shape=[pltpu.VMEM(shape, jnp.bfloat16) for shape in shapes],
        scratch_shapes=[
            pltpu.VMEM(expert_ids.shape[::-1], jnp.int32),
            pltpu.VMEM(gate_weights.shape[::-1], jnp.float32),
            pltpu.SemaphoreType.DMA((4,)),
        ],
        name="prepare",
        compiler_params=pltpu.CompilerParams(vmem_limit_bytes=VMEM_LIMIT),
        cost_estimate=pl.CostEstimate(flops=0, bytes_accessed=0, transcendentals=0),
    )(
        pltpu.with_memory_space_constraint(tokens, pltpu.HBM),
        pltpu.with_memory_space_constraint(w_down, pltpu.HBM),
        pltpu.with_memory_space_constraint(expert_ids.T, pltpu.HBM),
        pltpu.with_memory_space_constraint(gate_weights.T, pltpu.HBM),
    )


def cross_kernel(expert_count, wide_ref, cross_ref):
    half = cross_ref.shape[1]
    other = lax.axis_index("role") ^ 1
    gate = decode_gate(wide_ref[:, half:].astype(jnp.float32), other, expert_count)
    cross_ref[...] = compact(gate, wide_ref[:, :half], cross_ref.shape[0])


def cross_rows(wide, expert_count, capacity, hint=0):
    rows, width = wide.shape
    half = width - LANES
    return call(
        functools.partial(cross_kernel, expert_count),
        (wide,),
        ((capacity, half),),
        0,
        "cross_rows",
        hint=hint,
    )[0]


def row_starts(blocks):
    starts, rows = [], 0
    for block in blocks:
        starts.append(rows)
        rows += round_up(block.shape[0], 16)
    return tuple(starts), rows


def pack_kernel(starts, *refs):
    out_ref = refs[-1]
    for start, ref in zip(starts, refs):
        out_ref[start : start + ref.shape[0], :] = ref[:, : out_ref.shape[1]]


def pack(blocks, half, kept=(), hint=0):
    starts, rows = row_starts(blocks)
    return call(
        functools.partial(pack_kernel, starts),
        (*blocks, *kept),
        ((rows, half),),
        0,
        "pack_rows",
        hint=hint,
    )[0]


def hidden_kernel(near_ref, far_ref, gate_ref, up_ref, hidden_ref):
    half = near_ref.shape[1]
    core = lax.axis_index("tp")
    own = pl.ds(pl.multiple_of(core * half, LANES), half)
    sibling = pl.ds(pl.multiple_of((1 - core) * half, LANES), half)
    width = 256
    for first in range(0, hidden_ref.shape[1], width):
        units = slice(first, first + width)
        gate_proj, up_proj = (
            jnp.dot(near_ref[...], ref[own, units], preferred_element_type=jnp.float32)
            + jnp.dot(far_ref[...], ref[sibling, units], preferred_element_type=jnp.float32)
            for ref in (gate_ref, up_ref)
        )
        hidden_ref[:, units] = (jax.nn.silu(gate_proj) * up_proj).astype(jnp.bfloat16)


def hidden_units(near, far, w_gate, w_up):
    return call(
        hidden_kernel,
        (near, far, w_gate, w_up),
        ((near.shape[0], w_gate.shape[1]),),
        0,
        "hidden_units",
    )[0]


def down_kernel(expert_count, starts, wide_count, *refs):
    wides = refs[:wide_count]
    own_ref, other_ref, down_ref, down_other_ref = refs[wide_count : wide_count + 4]
    outs = refs[wide_count + 4 :]
    half = down_other_ref.shape[1]
    me = lax.axis_index("role")
    base = pl.multiple_of(lax.axis_index("tp") * half, LANES)
    gates = [decode_gate(ref[:, half:].astype(jnp.float32), me, expert_count) for ref in wides]
    width = 256
    for first in range(0, half, width):
        columns = slice(first, first + width)
        result = jnp.dot(
            own_ref[...],
            down_ref[0, :, pl.ds(pl.multiple_of(base + first, LANES), width)],
            preferred_element_type=jnp.float32,
        ) + jnp.dot(
            other_ref[...], down_other_ref[:, columns], preferred_element_type=jnp.float32
        )
        for index, (start, out_ref) in enumerate(zip(starts, outs)):
            block = result[start : start + out_ref.shape[0]].astype(jnp.bfloat16)
            if index < wide_count:
                block = gates[index] * block.astype(jnp.float32)
            out_ref[:, columns] = block


def down(wides, cross_count, hidden, hidden_other, w_down, down_other, capacity, expert_count):
    half = down_other.shape[1]
    shapes = [(wide.shape[0], half) for wide in wides] + [(capacity, half)] * cross_count
    starts, rows = [], 0
    for shape in shapes:
        starts.append(rows)
        rows += round_up(shape[0], 16)
    return call(
        functools.partial(down_kernel, expert_count, tuple(starts), len(wides)),
        (*wides, hidden, hidden_other, w_down, down_other),
        tuple(shapes),
        4 * rows * half * hidden.shape[1],
        "down",
        (),
        [jnp.float32] * len(wides) + [jnp.bfloat16] * cross_count,
    )


def attend_kernel(query_ref, latent_ref, lengths_ref, placement_ref, out_ref):
    slot_count, head_count, _ = query_ref.shape
    rank, context = out_ref.shape[2], latent_ref.shape[2]
    first = lax.axis_index("role") * slot_count
    position = lax.broadcasted_iota(jnp.int32, (head_count, context), 1)
    for slot in range(slot_count):
        here = placement_ref[...] == first + slot
        length = jnp.sum(jnp.where(here, lengths_ref[...], 0), axis=1, keepdims=True)
        scores = (
            jnp.dot(query_ref[slot], latent_ref[slot], preferred_element_type=jnp.float32)
            * score_scale
        )
        scores = jnp.where(position < length, scores, -jnp.inf)
        raised = jnp.exp(scores - jnp.max(scores, axis=1, keepdims=True))
        attn_weights = (raised / jnp.sum(raised, axis=1, keepdims=True)).astype(jnp.bfloat16)
        out_ref[slot] = lax.dot_general(
            attn_weights,
            latent_ref[slot, :rank, :],
            (((1,), (1,)), ((), ())),
            preferred_element_type=jnp.float32,
        ).astype(jnp.bfloat16)


def attend(q_lat, latent_cache, lengths, placement):
    slot_count, head_count, _ = q_lat.shape
    return pl.pallas_call(
        attend_kernel,
        out_shape=jax.ShapeDtypeStruct((slot_count, head_count, KV_RANK), jnp.bfloat16),
        name="attend",
        compiler_params=pltpu.CompilerParams(vmem_limit_bytes=VMEM_LIMIT),
        cost_estimate=pl.CostEstimate(flops=0, bytes_accessed=0, transcendentals=0),
    )(q_lat, latent_cache.transpose(0, 2, 1), lengths[None, :], placement[None, :])


def last_down_kernel(own_ref, other_ref, down_ref, down_other_ref, *outs):
    half = down_other_ref.shape[1]
    base = pl.multiple_of(lax.axis_index("tp") * half, LANES)
    start = 0
    for out_ref in outs:
        for first in range(0, out_ref.shape[1], 256):
            width = min(256, out_ref.shape[1] - first)
            column = start + first
            result = jnp.dot(
                own_ref[...],
                down_ref[0, :, pl.ds(pl.multiple_of(base + column, LANES), width)],
                preferred_element_type=jnp.float32,
            ) + jnp.dot(
                other_ref[...],
                down_other_ref[:, column : column + width],
                preferred_element_type=jnp.float32,
            )
            out_ref[:, first : first + width] = result[: out_ref.shape[0]].astype(jnp.bfloat16)
        start += out_ref.shape[1]


def last_down(hidden, hidden_other, w_down, down_other, capacity, widths):
    return call(
        last_down_kernel,
        (hidden, hidden_other, w_down, down_other),
        tuple((capacity, width) for width in widths),
        0,
        "last_down",
    )


def combine_kernel(expert_count, first, shift, sum_count, wide_ref, own_ref, back_ref, *refs):
    sums, outs = refs[:sum_count], refs[sum_count:]
    half = own_ref.shape[1]
    other = lax.axis_index("role") ^ 1
    gate = decode_gate(wide_ref[:, half:].astype(jnp.float32), other, expert_count)
    slots = slot_matrix(gate)[:, : back_ref.shape[0]]
    width = LANES
    for out_ref in outs:
        for column in range(0, out_ref.shape[1], width):
            columns = slice(first + column, first + column + width)
            spread = jnp.dot(
                slots,
                back_ref[:, columns.start - shift : columns.stop - shift],
                preferred_element_type=jnp.float32,
            )
            result = own_ref[:, columns] + gate * spread
            for ref in sums:
                result = result + ref[:, column : column + width].astype(jnp.float32)
            out_ref[:, column : column + width] = result.astype(out_ref.dtype)
        first += out_ref.shape[1]


def combine(
    wide, own, back, sums, expert_count, first, widths, dtype=jnp.bfloat16, shift=0, hint=0
):
    rows = own.shape[0]
    return call(
        functools.partial(combine_kernel, expert_count, first, shift, len(sums)),
        (wide, own, back, *sums),
        tuple((rows, width) for width in widths),
        0,
        "combine",
        types=(dtype,) * len(widths),
        hint=hint,
    )


def add_kernel(*refs):
    out_ref = refs[-1]
    count = len(refs) // 2
    first = 0
    for total_ref, part_ref in zip(refs[:count], refs[count:-1]):
        result = total_ref[...] + part_ref[...].astype(jnp.float32)
        out_ref[:, first : first + part_ref.shape[1]] = result.astype(jnp.bfloat16)
        first += part_ref.shape[1]


def add_last(totals, parts):
    shape = (parts[0].shape[0], sum(part.shape[1] for part in parts))
    return call(add_kernel, (*totals, *parts), (shape,), 0, "add_last", last=True)[0]


def swap(array, bits, places=(0, 1, 2, 3)):
    count = lax.axis_size("role")
    pairs = [(device, device ^ bits) for device in range(count) if device // 2 in places]
    return lax.ppermute(array, "role", pairs)


def swap_core(array):
    return lax.ppermute(array, "tp", [(0, 1), (1, 0)])


def route_multicast(
    q_lat, latent_cache, lengths, placement, tokens, expert_ids, gate_weights, w_gate, w_up, w_down
):
    role_count = lax.axis_size("role")
    token_count, route_count = expert_ids.shape
    half = tokens.shape[1]
    capacity = 3 * token_count * route_count // (2 * role_count)
    pair, mirror, row = 2, 6, 1

    wide, cross, down_away = prepare(
        tokens, w_down, expert_ids, gate_weights, role_count, capacity
    )
    wide_mirror = swap(wide, mirror)
    wide_pair = swap(wide, pair)
    cross_in = swap(cross, row)
    w_gate, w_up = w_gate[0], w_up[0]
    down_other = swap_core(down_away)
    attended = attend(after(q_lat, wide), latent_cache, lengths, placement)
    cross_in = after(cross_in, attended)
    wide_pair = after(wide_pair, cross_in, down_other)
    cross_pair = cross_rows(wide_pair, role_count, capacity)
    cross_pair_in = swap(cross_pair, row)
    wide_mirror = after(wide_mirror, cross_pair)
    wide_far = swap(wide_mirror, pair)
    cross_mirror = cross_rows(wide_mirror, role_count, capacity)
    cross_mirror_in = swap(cross_mirror, row)
    cross_pair_in = after(cross_pair_in, cross_mirror)
    near_first = pack((after(wide, cross_pair_in), wide_pair, wide_mirror, cross_in), half, (w_gate, w_up))
    far_first = swap_core(near_first)
    wide_far = after(wide_far, near_first)
    cross_mirror_in = after(cross_mirror_in, wide_far)
    wide_far = after(wide_far, cross_mirror_in)
    cross_far = cross_rows(wide_far, role_count, capacity, 10**10)
    cross_far_in = swap(cross_far, row)
    near_second = pack((wide_far, cross_pair_in, cross_mirror_in), half)
    far_second = swap_core(near_second)
    hidden = hidden_units(near_first, after(far_first, near_second), w_gate, w_up)
    hidden_other = swap_core(hidden)
    hidden_second = hidden_units(near_second, after(far_second, hidden), w_gate, w_up)
    hidden_second_other = swap_core(hidden_second)
    cross_far_in = after(cross_far_in, hidden_second)
    far_third = swap_core(cross_far_in)
    down_weights = (w_down, down_other)
    hidden_other = after(hidden_other, cross_far_in)
    own, own_pair, own_mirror, back_own = down(
        (wide, wide_pair, wide_mirror),
        1,
        hidden,
        hidden_other,
        *down_weights,
        capacity,
        role_count,
    )
    far_third = after(far_third, own)
    hidden_third = hidden_units(cross_far_in, far_third, w_gate, w_up)
    hidden_third_other = swap_core(hidden_third)
    hidden_second_other = after(hidden_second_other, hidden_third)
    own_far, back_pair, back_mirror = down(
        (wide_far,), 2, hidden_second, hidden_second_other, *down_weights, capacity, role_count
    )
    hidden_third_other = after(hidden_third_other, own_far)
    split = half // 2
    widths = (split, half - split)
    back_far_left, back_far_right = last_down(
        hidden_third, hidden_third_other, *down_weights, capacity, widths
    )
    back_far_left = swap(back_far_left, row)
    back_far_right = swap(back_far_right, row)
    back_mirror = swap(back_mirror, row)
    back_pair = swap(back_pair, row)
    back_own = swap(back_own, row)

    (sum_far_left,) = combine(
        wide_far, own_far, back_far_left, (), role_count, 0, widths[:1]
    )
    from_far_left = swap(sum_far_left, pair)
    back_far_right = after(back_far_right, sum_far_left)
    (sum_far_right,) = combine(
        wide_far,
        own_far,
        back_far_right,
        (),
        role_count,
        split,
        widths[1:],
        shift=split,
    )
    from_far_right = swap(sum_far_right, pair)
    back_mirror = after(back_mirror, sum_far_right)
    from_far_left = after(from_far_left, back_mirror)
    (sum_mirror_left,) = combine(
        wide_mirror, own_mirror, back_mirror, (from_far_left,), role_count, 0, widths[:1]
    )
    from_mirror_left = swap(sum_mirror_left, mirror)
    from_far_right = after(from_far_right, sum_mirror_left)
    (sum_mirror_right,) = combine(
        wide_mirror, own_mirror, back_mirror, (from_far_right,), role_count, split, widths[1:]
    )
    from_mirror_right = swap(sum_mirror_right, mirror)
    back_pair = after(back_pair, sum_mirror_right)
    sum_pair_left, sum_pair_right = combine(
        wide_pair, own_pair, back_pair, (), role_count, 0, widths
    )
    from_pair_left = swap(sum_pair_left, pair)
    from_pair_right = swap(sum_pair_right, pair)
    back_own = after(back_own, sum_pair_left)
    from_mirror_left = after(from_mirror_left, back_own)
    (sum_left,) = combine(
        wide, own, back_own, (from_mirror_left,), role_count, 0, widths[:1], jnp.float32
    )
    from_mirror_right = after(from_mirror_right, sum_left)
    (sum_right,) = combine(
        wide, own, back_own, (from_mirror_right,), role_count, split, widths[1:], jnp.float32
    )
    from_pair_left = after(from_pair_left, sum_right)
    moe_result = add_last((sum_left, sum_right), (from_pair_left, from_pair_right))
    return (attended, moe_result)


def shards(
    q_lat, latent_cache, lengths, placement, tokens, expert_ids, gate_weights, w_gate, w_up, w_down
):
    if lax.axis_size("role") == 8 and lax.axis_size("tp") == 2:
        return route_multicast(
            q_lat,
            latent_cache,
            lengths,
            placement,
            tokens,
            expert_ids,
            gate_weights,
            w_gate,
            w_up,
            w_down,
        )
    attended = attend_local(q_lat, latent_cache, lengths, placement)
    routed = route_all_to_all(tokens, expert_ids, gate_weights, w_gate, w_up, w_down)
    return (attended, routed)


def solution(mesh):
    return jax.shard_map(
        shards,
        mesh=mesh,
        in_specs=(
            P(("groups", "role"), "tp", None),
            P(("groups", "role"), None, None),
            P("groups"),
            P("groups"),
            P(("groups", "role"), "tp"),
            P(("groups", "role"), None),
            P(("groups", "role"), None),
            P("role", None, "tp"),
            P("role", None, "tp"),
            P("role", "tp", None),
        ),
        out_specs=(P(("groups", "role"), "tp", None), P(("groups", "role"), "tp")),
        check_vma=False,
    )
```

```python
import functools

import jax
import jax.numpy as jnp
from jax import lax
from jax.experimental import pallas as pl
from jax.experimental.pallas import tpu as pltpu
from jax.sharding import PartitionSpec as P

KV_RANK = 512


score_scale = 192.0 ** (-0.5)


def attend_local(q_lat, latent_cache, lengths, placement):
    slot_count = q_lat.shape[0]
    offset = lax.axis_index("role") * slot_count
    slot_ids = offset + jnp.arange(slot_count, dtype=jnp.int32)
    matches = placement[None, :] == slot_ids[:, None]
    slot_length = jnp.sum(jnp.where(matches, lengths[None, :], 0), axis=1)
    scores = (
        jnp.einsum("shc,stc->sht", q_lat, latent_cache, preferred_element_type=jnp.float32)
        * score_scale
    )
    position = jnp.arange(latent_cache.shape[1], dtype=jnp.int32)
    visible = position[None, None, :] < slot_length[:, None, None]
    scores = jnp.where(visible, scores, -jnp.inf)
    highest = jnp.max(scores, axis=2, keepdims=True)
    raised = jnp.exp(scores - highest)
    attn_weights = (raised / jnp.sum(raised, axis=2, keepdims=True)).astype(jnp.bfloat16)
    values = latent_cache[:, :, :KV_RANK]
    return jnp.einsum(
        "sht,stc->shc", attn_weights, values, preferred_element_type=jnp.float32
    ).astype(jnp.bfloat16)


def route_all_to_all(tokens, expert_ids, gate_weights, w_gate, w_up, w_down):
    role_count = lax.axis_size("role")
    token_count = expert_ids.shape[0]
    route_count = expert_ids.shape[1]
    capacity = 3 * token_count * route_count // (2 * role_count)
    flat_ids = expert_ids.reshape(-1)
    onehot = (flat_ids[:, None] == jnp.arange(role_count, dtype=jnp.int32)[None, :]).astype(
        jnp.int32
    )
    earlier = jnp.cumsum(onehot, axis=0) - onehot
    slot_index = jnp.sum(earlier * onehot, axis=1)
    target = flat_ids * capacity + slot_index
    source = jnp.arange(token_count * route_count, dtype=jnp.int32) // route_count
    outgoing = lax.all_gather(tokens, "tp", axis=1, tiled=True)
    columns = outgoing.shape[1]
    buffer_rows = (
        jnp.zeros((role_count * capacity, columns), jnp.bfloat16).at[target].set(outgoing[source])
    )
    buffer_rows = buffer_rows.reshape(role_count, capacity, columns)
    gate_matrix = w_gate[0]
    up_matrix = w_up[0]
    down_matrix = w_down[0]
    received = lax.all_to_all(buffer_rows, "role", split_axis=0, concat_axis=0, tiled=True)
    item_count = received.shape[1]
    arrived = received.reshape(role_count * item_count, columns)
    gate_proj = jnp.dot(arrived, gate_matrix, preferred_element_type=jnp.float32)
    up_proj = jnp.dot(arrived, up_matrix, preferred_element_type=jnp.float32)
    expert_hidden = (jax.nn.silu(gate_proj) * up_proj).astype(jnp.bfloat16)
    partial_out = jnp.dot(expert_hidden, down_matrix, preferred_element_type=jnp.float32)
    summed = lax.psum_scatter(
        partial_out.astype(jnp.bfloat16), "tp", scatter_dimension=1, tiled=True
    )
    summed = summed.reshape(role_count, item_count, summed.shape[1])
    returned = lax.all_to_all(summed, "role", split_axis=0, concat_axis=0, tiled=True)
    half_width = returned.shape[2]
    flat_back = returned.reshape(role_count * capacity, half_width)
    chosen_rows = (
        flat_back[target].reshape(token_count, route_count, half_width).astype(jnp.float32)
    )
    moe_result = jnp.sum(chosen_rows * gate_weights[:, :, None], axis=1).astype(jnp.bfloat16)
    return moe_result


LANES = 128
VMEM_LIMIT = 16 * 1024 * 1024


def round_up(value, unit):
    return -(-value // unit) * unit


def call(kernel, operands, out_shapes, flops, name, scratch=(), types=None, last=False, hint=0):
    place = pl.BlockSpec(memory_space=pltpu.VMEM)
    return pl.pallas_call(
        kernel,
        in_specs=[place] * len(operands),
        out_specs=[place] * len(out_shapes),
        out_shape=[
            (jax.ShapeDtypeStruct if last else pltpu.VMEM)(
                shape, jnp.bfloat16 if types is None else types[index]
            )
            for index, shape in enumerate(out_shapes)
        ],
        scratch_shapes=list(scratch),
        name=name,
        compiler_params=pltpu.CompilerParams(vmem_limit_bytes=VMEM_LIMIT),
        cost_estimate=pl.CostEstimate(flops=hint, bytes_accessed=0, transcendentals=0),
    )(*[pltpu.with_memory_space_constraint(operand, pltpu.VMEM) for operand in operands])


def after(value, *earlier):
    return lax.optimization_barrier((value, *earlier))[0]


def lane_index(rows):
    return lax.broadcasted_iota(jnp.int32, (rows, LANES), 1)


def decode_gate(pieces, expert, expert_count):
    lane = lane_index(pieces.shape[0])
    wanted = lane == expert
    for piece in (1, 2):
        wanted = wanted | (lane == expert + piece * expert_count)
    return jnp.sum(jnp.where(wanted, pieces, 0.0), axis=1, keepdims=True)


def slot_matrix(gate):
    rows = gate.shape[0]
    named = jnp.broadcast_to((gate > 0.0).astype(jnp.float32), (rows, LANES))
    lower = lax.broadcasted_iota(jnp.int32, (rows, rows), 0) >= lax.broadcasted_iota(
        jnp.int32, (rows, rows), 1
    )
    rank = jnp.dot(
        lower.astype(jnp.bfloat16), named.astype(jnp.bfloat16), preferred_element_type=jnp.float32
    )
    slot = lane_index(rows).astype(jnp.float32)
    return jnp.where((named > 0.0) & (rank - 1.0 == slot), 1.0, 0.0).astype(jnp.bfloat16)


def compact(gate, rows_in, capacity):
    picked = lax.dot_general(
        slot_matrix(gate),
        rows_in,
        (((0,), (0,)), ((), ())),
        preferred_element_type=jnp.float32,
    )
    return picked[:capacity].astype(jnp.bfloat16)


def prepare_kernel(
    expert_count,
    tokens_hbm,
    down_hbm,
    ids_hbm,
    gates_hbm,
    wide_ref,
    cross_ref,
    away_ref,
    ids_ref,
    gates_ref,
    sems,
):
    rows, half = tokens_hbm.shape
    copy = pltpu.make_async_copy(tokens_hbm, wide_ref.at[:, :half], sems.at[0])
    first = [
        pltpu.make_async_copy(ids_hbm, ids_ref, sems.at[2]),
        pltpu.make_async_copy(gates_hbm, gates_ref, sems.at[3]),
    ]
    for part in first:
        part.start()
    copy.start()
    sibling = pl.multiple_of((1 - lax.axis_index("tp")) * half, LANES)
    away = pltpu.make_async_copy(down_hbm.at[0, :, pl.ds(sibling, half)], away_ref, sems.at[1])
    away.start()
    for part in first:
        part.wait()
    piece_rows = round_up(3 * expert_count, 16)
    line = lax.broadcasted_iota(jnp.int32, (piece_rows, rows), 0)
    named = line
    for piece in (1, 2):
        named = jnp.where(line >= piece * expert_count, line - piece * expert_count, named)
    dense = jnp.zeros((piece_rows, rows), jnp.float32)
    for choice in range(ids_ref.shape[0]):
        dense = dense + jnp.where(
            ids_ref[choice : choice + 1, :] == named, gates_ref[choice : choice + 1, :], 0.0
        )
    high = dense.astype(jnp.bfloat16).astype(jnp.float32)
    middle = (dense - high).astype(jnp.bfloat16).astype(jnp.float32)
    low = dense - high - middle
    pieces = jnp.where(line < expert_count, high, jnp.where(line < 2 * expert_count, middle, low))
    unit = lax.broadcasted_iota(jnp.int32, (piece_rows, LANES), 0) == lax.broadcasted_iota(
        jnp.int32, (piece_rows, LANES), 1
    )
    turned = lax.dot_general(
        pieces.astype(jnp.bfloat16),
        unit.astype(jnp.bfloat16),
        (((0,), (0,)), ((), ())),
        preferred_element_type=jnp.float32,
    )
    wide_ref[:, half:] = turned.astype(jnp.bfloat16)
    copy.wait()
    gate = decode_gate(turned, lax.axis_index("role") ^ 1, expert_count)
    cross_ref[...] = compact(gate, wide_ref[:, :half], cross_ref.shape[0])
    away.wait()


def prepare(tokens, w_down, expert_ids, gate_weights, expert_count, capacity):
    rows, half = tokens.shape
    shapes = [
        (rows, half + LANES),
        (capacity, half),
        (w_down.shape[1], half),
    ]
    whole = pl.BlockSpec(memory_space=pltpu.VMEM)
    return pl.pallas_call(
        functools.partial(prepare_kernel, expert_count),
        in_specs=[pl.BlockSpec(memory_space=pltpu.HBM)] * 4,
        out_specs=[whole] * len(shapes),
        out_shape=[pltpu.VMEM(shape, jnp.bfloat16) for shape in shapes],
        scratch_shapes=[
            pltpu.VMEM(expert_ids.shape[::-1], jnp.int32),
            pltpu.VMEM(gate_weights.shape[::-1], jnp.float32),
            pltpu.SemaphoreType.DMA((4,)),
        ],
        name="prepare",
        compiler_params=pltpu.CompilerParams(vmem_limit_bytes=VMEM_LIMIT),
        cost_estimate=pl.CostEstimate(flops=0, bytes_accessed=0, transcendentals=0),
    )(
        pltpu.with_memory_space_constraint(tokens, pltpu.HBM),
        pltpu.with_memory_space_constraint(w_down, pltpu.HBM),
        pltpu.with_memory_space_constraint(expert_ids.T, pltpu.HBM),
        pltpu.with_memory_space_constraint(gate_weights.T, pltpu.HBM),
    )


def cross_kernel(expert_count, wide_ref, cross_ref):
    half = cross_ref.shape[1]
    other = lax.axis_index("role") ^ 1
    gate = decode_gate(wide_ref[:, half:].astype(jnp.float32), other, expert_count)
    cross_ref[...] = compact(gate, wide_ref[:, :half], cross_ref.shape[0])


def cross_rows(wide, expert_count, capacity, hint=0):
    rows, width = wide.shape
    half = width - LANES
    return call(
        functools.partial(cross_kernel, expert_count),
        (wide,),
        ((capacity, half),),
        0,
        "cross_rows",
        hint=hint,
    )[0]


def row_starts(blocks):
    starts, rows = [], 0
    for block in blocks:
        starts.append(rows)
        rows += round_up(block.shape[0], 16)
    return tuple(starts), rows


def pack_kernel(starts, *refs):
    out_ref = refs[-1]
    for start, ref in zip(starts, refs):
        out_ref[start : start + ref.shape[0], :] = ref[:, : out_ref.shape[1]]


def pack(blocks, half, kept=(), hint=0):
    starts, rows = row_starts(blocks)
    return call(
        functools.partial(pack_kernel, starts),
        (*blocks, *kept),
        ((rows, half),),
        0,
        "pack_rows",
        hint=hint,
    )[0]


def hidden_kernel(near_ref, far_ref, gate_ref, up_ref, hidden_ref):
    half = near_ref.shape[1]
    core = lax.axis_index("tp")
    own = pl.ds(pl.multiple_of(core * half, LANES), half)
    sibling = pl.ds(pl.multiple_of((1 - core) * half, LANES), half)
    width = 256
    for first in range(0, hidden_ref.shape[1], width):
        units = slice(first, first + width)
        gate_proj, up_proj = (
            jnp.dot(near_ref[...], ref[own, units], preferred_element_type=jnp.float32)
            + jnp.dot(far_ref[...], ref[sibling, units], preferred_element_type=jnp.float32)
            for ref in (gate_ref, up_ref)
        )
        hidden_ref[:, units] = (jax.nn.silu(gate_proj) * up_proj).astype(jnp.bfloat16)


def hidden_units(near, far, w_gate, w_up):
    return call(
        hidden_kernel,
        (near, far, w_gate, w_up),
        ((near.shape[0], w_gate.shape[1]),),
        0,
        "hidden_units",
    )[0]


def down_kernel(expert_count, starts, wide_count, *refs):
    wides = refs[:wide_count]
    own_ref, other_ref, down_ref, down_other_ref = refs[wide_count : wide_count + 4]
    outs = refs[wide_count + 4 :]
    half = down_other_ref.shape[1]
    me = lax.axis_index("role")
    base = pl.multiple_of(lax.axis_index("tp") * half, LANES)
    gates = [decode_gate(ref[:, half:].astype(jnp.float32), me, expert_count) for ref in wides]
    width = 256
    for first in range(0, half, width):
        columns = slice(first, first + width)
        result = jnp.dot(
            own_ref[...],
            down_ref[0, :, pl.ds(pl.multiple_of(base + first, LANES), width)],
            preferred_element_type=jnp.float32,
        ) + jnp.dot(
            other_ref[...], down_other_ref[:, columns], preferred_element_type=jnp.float32
        )
        for index, (start, out_ref) in enumerate(zip(starts, outs)):
            block = result[start : start + out_ref.shape[0]].astype(jnp.bfloat16)
            if index < wide_count:
                block = gates[index] * block.astype(jnp.float32)
            out_ref[:, columns] = block


def down(wides, cross_count, hidden, hidden_other, w_down, down_other, capacity, expert_count):
    half = down_other.shape[1]
    shapes = [(wide.shape[0], half) for wide in wides] + [(capacity, half)] * cross_count
    starts, rows = [], 0
    for shape in shapes:
        starts.append(rows)
        rows += round_up(shape[0], 16)
    return call(
        functools.partial(down_kernel, expert_count, tuple(starts), len(wides)),
        (*wides, hidden, hidden_other, w_down, down_other),
        tuple(shapes),
        4 * rows * half * hidden.shape[1],
        "down",
        (),
        [jnp.float32] * len(wides) + [jnp.bfloat16] * cross_count,
    )


def attend_kernel(query_ref, latent_ref, lengths_ref, placement_ref, out_ref):
    slot_count, head_count, _ = query_ref.shape
    rank, context = out_ref.shape[2], latent_ref.shape[2]
    first = lax.axis_index("role") * slot_count
    position = lax.broadcasted_iota(jnp.int32, (head_count, context), 1)
    for slot in range(slot_count):
        here = placement_ref[...] == first + slot
        length = jnp.sum(jnp.where(here, lengths_ref[...], 0), axis=1, keepdims=True)
        scores = (
            jnp.dot(query_ref[slot], latent_ref[slot], preferred_element_type=jnp.float32)
            * score_scale
        )
        scores = jnp.where(position < length, scores, -jnp.inf)
        raised = jnp.exp(scores - jnp.max(scores, axis=1, keepdims=True))
        attn_weights = (raised / jnp.sum(raised, axis=1, keepdims=True)).astype(jnp.bfloat16)
        out_ref[slot] = lax.dot_general(
            attn_weights,
            latent_ref[slot, :rank, :],
            (((1,), (1,)), ((), ())),
            preferred_element_type=jnp.float32,
        ).astype(jnp.bfloat16)


def attend(q_lat, latent_cache, lengths, placement):
    slot_count, head_count, _ = q_lat.shape
    return pl.pallas_call(
        attend_kernel,
        out_shape=jax.ShapeDtypeStruct((slot_count, head_count, KV_RANK), jnp.bfloat16),
        name="attend",
        compiler_params=pltpu.CompilerParams(vmem_limit_bytes=VMEM_LIMIT),
        cost_estimate=pl.CostEstimate(flops=0, bytes_accessed=0, transcendentals=0),
    )(q_lat, latent_cache.transpose(0, 2, 1), lengths[None, :], placement[None, :])


def last_down_kernel(own_ref, other_ref, down_ref, down_other_ref, *outs):
    half = down_other_ref.shape[1]
    base = pl.multiple_of(lax.axis_index("tp") * half, LANES)
    start = 0
    for out_ref in outs:
        for first in range(0, out_ref.shape[1], 256):
            width = min(256, out_ref.shape[1] - first)
            column = start + first
            result = jnp.dot(
                own_ref[...],
                down_ref[0, :, pl.ds(pl.multiple_of(base + column, LANES), width)],
                preferred_element_type=jnp.float32,
            ) + jnp.dot(
                other_ref[...],
                down_other_ref[:, column : column + width],
                preferred_element_type=jnp.float32,
            )
            out_ref[:, first : first + width] = result[: out_ref.shape[0]].astype(jnp.bfloat16)
        start += out_ref.shape[1]


def last_down(hidden, hidden_other, w_down, down_other, capacity, widths):
    return call(
        last_down_kernel,
        (hidden, hidden_other, w_down, down_other),
        tuple((capacity, width) for width in widths),
        0,
        "last_down",
    )


def combine_kernel(expert_count, first, shift, sum_count, wide_ref, own_ref, back_ref, *refs):
    sums, outs = refs[:sum_count], refs[sum_count:]
    half = own_ref.shape[1]
    other = lax.axis_index("role") ^ 1
    gate = decode_gate(wide_ref[:, half:].astype(jnp.float32), other, expert_count)
    slots = slot_matrix(gate)[:, : back_ref.shape[0]]
    width = LANES
    for out_ref in outs:
        for column in range(0, out_ref.shape[1], width):
            columns = slice(first + column, first + column + width)
            spread = jnp.dot(
                slots,
                back_ref[:, columns.start - shift : columns.stop - shift],
                preferred_element_type=jnp.float32,
            )
            result = own_ref[:, columns] + gate * spread
            for ref in sums:
                result = result + ref[:, column : column + width].astype(jnp.float32)
            out_ref[:, column : column + width] = result.astype(out_ref.dtype)
        first += out_ref.shape[1]


def combine(
    wide, own, back, sums, expert_count, first, widths, dtype=jnp.bfloat16, shift=0, hint=0
):
    rows = own.shape[0]
    return call(
        functools.partial(combine_kernel, expert_count, first, shift, len(sums)),
        (wide, own, back, *sums),
        tuple((rows, width) for width in widths),
        0,
        "combine",
        types=(dtype,) * len(widths),
        hint=hint,
    )


def add_kernel(*refs):
    out_ref = refs[-1]
    count = len(refs) // 2
    first = 0
    for total_ref, part_ref in zip(refs[:count], refs[count:-1]):
        result = total_ref[...] + part_ref[...].astype(jnp.float32)
        out_ref[:, first : first + part_ref.shape[1]] = result.astype(jnp.bfloat16)
        first += part_ref.shape[1]


def add_last(totals, parts):
    shape = (parts[0].shape[0], sum(part.shape[1] for part in parts))
    return call(add_kernel, (*totals, *parts), (shape,), 0, "add_last", last=True)[0]


def swap(array, bits, places=(0, 1, 2, 3)):
    count = lax.axis_size("role")
    pairs = [(device, device ^ bits) for device in range(count) if device // 2 in places]
    return lax.ppermute(array, "role", pairs)


def swap_core(array):
    return lax.ppermute(array, "tp", [(0, 1), (1, 0)])


def route_multicast(
    q_lat, latent_cache, lengths, placement, tokens, expert_ids, gate_weights, w_gate, w_up, w_down
):
    role_count = lax.axis_size("role")
    token_count, route_count = expert_ids.shape
    half = tokens.shape[1]
    capacity = 3 * token_count * route_count // (2 * role_count)
    pair, mirror, row = 2, 6, 1

    wide, cross, down_away = prepare(
        tokens, w_down, expert_ids, gate_weights, role_count, capacity
    )
    wide_mirror = swap(wide, mirror)
    wide_pair = swap(wide, pair)
    cross_in = swap(cross, row)
    w_gate, w_up = w_gate[0], w_up[0]
    down_other = swap_core(down_away)
    attended = attend(after(q_lat, wide), latent_cache, lengths, placement)
    cross_in = after(cross_in, attended)
    wide_mirror = after(wide_mirror, cross_in, down_other)
    wide_far = swap(wide_mirror, pair)
    cross_mirror = cross_rows(wide_mirror, role_count, capacity)
    cross_mirror_in = swap(cross_mirror, row)
    wide_pair = after(wide_pair, cross_mirror)
    cross_pair = cross_rows(wide_pair, role_count, capacity)
    cross_pair_in = swap(cross_pair, row)
    near_first = pack(
        (after(wide, cross_pair), wide_pair, wide_mirror, cross_in), half, (w_gate, w_up)
    )
    far_first = swap_core(near_first)
    cross_mirror_in = after(cross_mirror_in, near_first)
    wide_far = after(wide_far, cross_mirror_in)
    cross_pair_in = after(cross_pair_in, wide_far)
    wide_far = after(wide_far, cross_pair_in)
    cross_far = cross_rows(wide_far, role_count, capacity, 10**10)
    cross_far_in = swap(cross_far, row)
    near_second = pack((wide_far, cross_pair_in, cross_mirror_in), half)
    far_second = swap_core(near_second)
    hidden = hidden_units(near_first, after(far_first, near_second), w_gate, w_up)
    hidden_other = swap_core(hidden)
    hidden_second = hidden_units(near_second, after(far_second, hidden), w_gate, w_up)
    hidden_second_other = swap_core(hidden_second)
    cross_far_in = after(cross_far_in, hidden_second)
    far_third = swap_core(cross_far_in)
    down_weights = (w_down, down_other)
    hidden_other = after(hidden_other, cross_far_in)
    own, own_pair, own_mirror, back_own = down(
        (wide, wide_pair, wide_mirror),
        1,
        hidden,
        hidden_other,
        *down_weights,
        capacity,
        role_count,
    )
    far_third = after(far_third, own)
    hidden_third = hidden_units(cross_far_in, far_third, w_gate, w_up)
    hidden_third_other = swap_core(hidden_third)
    hidden_second_other = after(hidden_second_other, hidden_third)
    own_far, back_pair, back_mirror = down(
        (wide_far,), 2, hidden_second, hidden_second_other, *down_weights, capacity, role_count
    )
    hidden_third_other = after(hidden_third_other, own_far)
    split = half // 2
    widths = (split, half - split)
    back_far_left, back_far_right = last_down(
        hidden_third, hidden_third_other, *down_weights, capacity, widths
    )
    back_far_left = swap(back_far_left, row)
    back_far_right = swap(back_far_right, row)
    back_mirror = swap(back_mirror, row)
    back_pair = swap(back_pair, row)
    back_own = swap(back_own, row)

    (sum_far_left,) = combine(
        wide_far, own_far, back_far_left, (), role_count, 0, widths[:1]
    )
    from_far_left = swap(sum_far_left, pair)
    back_far_right = after(back_far_right, sum_far_left)
    (sum_far_right,) = combine(
        wide_far,
        own_far,
        back_far_right,
        (),
        role_count,
        split,
        widths[1:],
        shift=split,
    )
    from_far_right = swap(sum_far_right, pair)
    back_mirror = after(back_mirror, sum_far_right)
    from_far_left = after(from_far_left, back_mirror)
    (sum_mirror_left,) = combine(
        wide_mirror, own_mirror, back_mirror, (from_far_left,), role_count, 0, widths[:1]
    )
    from_mirror_left = swap(sum_mirror_left, mirror)
    from_far_right = after(from_far_right, sum_mirror_left)
    (sum_mirror_right,) = combine(
        wide_mirror, own_mirror, back_mirror, (from_far_right,), role_count, split, widths[1:]
    )
    from_mirror_right = swap(sum_mirror_right, mirror)
    back_pair = after(back_pair, sum_mirror_right)
    sum_pair_left, sum_pair_right = combine(
        wide_pair, own_pair, back_pair, (), role_count, 0, widths
    )
    from_pair_left = swap(sum_pair_left, pair)
    from_pair_right = swap(sum_pair_right, pair)
    back_own = after(back_own, sum_pair_left)
    from_mirror_left = after(from_mirror_left, back_own)
    (sum_left,) = combine(
        wide, own, back_own, (from_mirror_left,), role_count, 0, widths[:1], jnp.float32
    )
    from_mirror_right = after(from_mirror_right, sum_left)
    (sum_right,) = combine(
        wide, own, back_own, (from_mirror_right,), role_count, split, widths[1:], jnp.float32
    )
    from_pair_left = after(from_pair_left, sum_right)
    moe_result = add_last((sum_left, sum_right), (from_pair_left, from_pair_right))
    return (attended, moe_result)


def shards(
    q_lat, latent_cache, lengths, placement, tokens, expert_ids, gate_weights, w_gate, w_up, w_down
):
    if lax.axis_size("role") == 8 and lax.axis_size("tp") == 2:
        return route_multicast(
            q_lat,
            latent_cache,
            lengths,
            placement,
            tokens,
            expert_ids,
            gate_weights,
            w_gate,
            w_up,
            w_down,
        )
    attended = attend_local(q_lat, latent_cache, lengths, placement)
    routed = route_all_to_all(tokens, expert_ids, gate_weights, w_gate, w_up, w_down)
    return (attended, routed)


def solution(mesh):
    return jax.shard_map(
        shards,
        mesh=mesh,
        in_specs=(
            P(("groups", "role"), "tp", None),
            P(("groups", "role"), None, None),
            P("groups"),
            P("groups"),
            P(("groups", "role"), "tp"),
            P(("groups", "role"), None),
            P(("groups", "role"), None),
            P("role", None, "tp"),
            P("role", None, "tp"),
            P("role", "tp", None),
        ),
        out_specs=(P(("groups", "role"), "tp", None), P(("groups", "role"), "tp")),
        check_vma=False,
    )
```

```python
import functools

import jax
import jax.numpy as jnp
from jax import lax
from jax.experimental import pallas as pl
from jax.experimental.pallas import tpu as pltpu
from jax.sharding import PartitionSpec as P

KV_RANK = 512


score_scale = 192.0 ** (-0.5)


def attend_local(q_lat, latent_cache, lengths, placement):
    slot_count = q_lat.shape[0]
    offset = lax.axis_index("role") * slot_count
    slot_ids = offset + jnp.arange(slot_count, dtype=jnp.int32)
    matches = placement[None, :] == slot_ids[:, None]
    slot_length = jnp.sum(jnp.where(matches, lengths[None, :], 0), axis=1)
    scores = (
        jnp.einsum("shc,stc->sht", q_lat, latent_cache, preferred_element_type=jnp.float32)
        * score_scale
    )
    position = jnp.arange(latent_cache.shape[1], dtype=jnp.int32)
    visible = position[None, None, :] < slot_length[:, None, None]
    scores = jnp.where(visible, scores, -jnp.inf)
    highest = jnp.max(scores, axis=2, keepdims=True)
    raised = jnp.exp(scores - highest)
    attn_weights = (raised / jnp.sum(raised, axis=2, keepdims=True)).astype(jnp.bfloat16)
    values = latent_cache[:, :, :KV_RANK]
    return jnp.einsum(
        "sht,stc->shc", attn_weights, values, preferred_element_type=jnp.float32
    ).astype(jnp.bfloat16)


def route_all_to_all(tokens, expert_ids, gate_weights, w_gate, w_up, w_down):
    role_count = lax.axis_size("role")
    token_count = expert_ids.shape[0]
    route_count = expert_ids.shape[1]
    capacity = 3 * token_count * route_count // (2 * role_count)
    flat_ids = expert_ids.reshape(-1)
    onehot = (flat_ids[:, None] == jnp.arange(role_count, dtype=jnp.int32)[None, :]).astype(
        jnp.int32
    )
    earlier = jnp.cumsum(onehot, axis=0) - onehot
    slot_index = jnp.sum(earlier * onehot, axis=1)
    target = flat_ids * capacity + slot_index
    source = jnp.arange(token_count * route_count, dtype=jnp.int32) // route_count
    outgoing = lax.all_gather(tokens, "tp", axis=1, tiled=True)
    columns = outgoing.shape[1]
    buffer_rows = (
        jnp.zeros((role_count * capacity, columns), jnp.bfloat16).at[target].set(outgoing[source])
    )
    buffer_rows = buffer_rows.reshape(role_count, capacity, columns)
    gate_matrix = w_gate[0]
    up_matrix = w_up[0]
    down_matrix = w_down[0]
    received = lax.all_to_all(buffer_rows, "role", split_axis=0, concat_axis=0, tiled=True)
    item_count = received.shape[1]
    arrived = received.reshape(role_count * item_count, columns)
    gate_proj = jnp.dot(arrived, gate_matrix, preferred_element_type=jnp.float32)
    up_proj = jnp.dot(arrived, up_matrix, preferred_element_type=jnp.float32)
    expert_hidden = (jax.nn.silu(gate_proj) * up_proj).astype(jnp.bfloat16)
    partial_out = jnp.dot(expert_hidden, down_matrix, preferred_element_type=jnp.float32)
    summed = lax.psum_scatter(
        partial_out.astype(jnp.bfloat16), "tp", scatter_dimension=1, tiled=True
    )
    summed = summed.reshape(role_count, item_count, summed.shape[1])
    returned = lax.all_to_all(summed, "role", split_axis=0, concat_axis=0, tiled=True)
    half_width = returned.shape[2]
    flat_back = returned.reshape(role_count * capacity, half_width)
    chosen_rows = (
        flat_back[target].reshape(token_count, route_count, half_width).astype(jnp.float32)
    )
    moe_result = jnp.sum(chosen_rows * gate_weights[:, :, None], axis=1).astype(jnp.bfloat16)
    return moe_result


LANES = 128
VMEM_LIMIT = 16 * 1024 * 1024


def round_up(value, unit):
    return -(-value // unit) * unit


def call(kernel, operands, out_shapes, flops, name, scratch=(), types=None, last=False, hint=0):
    place = pl.BlockSpec(memory_space=pltpu.VMEM)
    return pl.pallas_call(
        kernel,
        in_specs=[place] * len(operands),
        out_specs=[place] * len(out_shapes),
        out_shape=[
            (jax.ShapeDtypeStruct if last else pltpu.VMEM)(
                shape, jnp.bfloat16 if types is None else types[index]
            )
            for index, shape in enumerate(out_shapes)
        ],
        scratch_shapes=list(scratch),
        name=name,
        compiler_params=pltpu.CompilerParams(vmem_limit_bytes=VMEM_LIMIT),
        cost_estimate=pl.CostEstimate(flops=hint, bytes_accessed=0, transcendentals=0),
    )(*[pltpu.with_memory_space_constraint(operand, pltpu.VMEM) for operand in operands])


def after(value, *earlier):
    return lax.optimization_barrier((value, *earlier))[0]


def lane_index(rows):
    return lax.broadcasted_iota(jnp.int32, (rows, LANES), 1)


def decode_gate(pieces, expert, expert_count):
    lane = lane_index(pieces.shape[0])
    wanted = lane == expert
    for piece in (1, 2):
        wanted = wanted | (lane == expert + piece * expert_count)
    return jnp.sum(jnp.where(wanted, pieces, 0.0), axis=1, keepdims=True)


def slot_matrix(gate):
    rows = gate.shape[0]
    named = jnp.broadcast_to((gate > 0.0).astype(jnp.float32), (rows, LANES))
    lower = lax.broadcasted_iota(jnp.int32, (rows, rows), 0) >= lax.broadcasted_iota(
        jnp.int32, (rows, rows), 1
    )
    rank = jnp.dot(
        lower.astype(jnp.bfloat16), named.astype(jnp.bfloat16), preferred_element_type=jnp.float32
    )
    slot = lane_index(rows).astype(jnp.float32)
    return jnp.where((named > 0.0) & (rank - 1.0 == slot), 1.0, 0.0).astype(jnp.bfloat16)


def compact(gate, rows_in, capacity):
    picked = lax.dot_general(
        slot_matrix(gate),
        rows_in,
        (((0,), (0,)), ((), ())),
        preferred_element_type=jnp.float32,
    )
    return picked[:capacity].astype(jnp.bfloat16)


def prepare_kernel(
    expert_count,
    tokens_hbm,
    down_hbm,
    ids_hbm,
    gates_hbm,
    wide_ref,
    cross_ref,
    away_ref,
    ids_ref,
    gates_ref,
    sems,
):
    rows, half = tokens_hbm.shape
    copy = pltpu.make_async_copy(tokens_hbm, wide_ref.at[:, :half], sems.at[0])
    first = [
        pltpu.make_async_copy(ids_hbm, ids_ref, sems.at[2]),
        pltpu.make_async_copy(gates_hbm, gates_ref, sems.at[3]),
    ]
    for part in first:
        part.start()
    copy.start()
    sibling = pl.multiple_of((1 - lax.axis_index("tp")) * half, LANES)
    away = pltpu.make_async_copy(down_hbm.at[0, :, pl.ds(sibling, half)], away_ref, sems.at[1])
    away.start()
    for part in first:
        part.wait()
    piece_rows = round_up(3 * expert_count, 16)
    line = lax.broadcasted_iota(jnp.int32, (piece_rows, rows), 0)
    named = line
    for piece in (1, 2):
        named = jnp.where(line >= piece * expert_count, line - piece * expert_count, named)
    dense = jnp.zeros((piece_rows, rows), jnp.float32)
    for choice in range(ids_ref.shape[0]):
        dense = dense + jnp.where(
            ids_ref[choice : choice + 1, :] == named, gates_ref[choice : choice + 1, :], 0.0
        )
    high = dense.astype(jnp.bfloat16).astype(jnp.float32)
    middle = (dense - high).astype(jnp.bfloat16).astype(jnp.float32)
    low = dense - high - middle
    pieces = jnp.where(line < expert_count, high, jnp.where(line < 2 * expert_count, middle, low))
    unit = lax.broadcasted_iota(jnp.int32, (piece_rows, LANES), 0) == lax.broadcasted_iota(
        jnp.int32, (piece_rows, LANES), 1
    )
    turned = lax.dot_general(
        pieces.astype(jnp.bfloat16),
        unit.astype(jnp.bfloat16),
        (((0,), (0,)), ((), ())),
        preferred_element_type=jnp.float32,
    )
    wide_ref[:, half:] = turned.astype(jnp.bfloat16)
    copy.wait()
    gate = decode_gate(turned, lax.axis_index("role") ^ 1, expert_count)
    cross_ref[...] = compact(gate, wide_ref[:, :half], cross_ref.shape[0])
    away.wait()


def prepare(tokens, w_down, expert_ids, gate_weights, expert_count, capacity):
    rows, half = tokens.shape
    shapes = [
        (rows, half + LANES),
        (capacity, half),
        (w_down.shape[1], half),
    ]
    whole = pl.BlockSpec(memory_space=pltpu.VMEM)
    return pl.pallas_call(
        functools.partial(prepare_kernel, expert_count),
        in_specs=[pl.BlockSpec(memory_space=pltpu.HBM)] * 4,
        out_specs=[whole] * len(shapes),
        out_shape=[pltpu.VMEM(shape, jnp.bfloat16) for shape in shapes],
        scratch_shapes=[
            pltpu.VMEM(expert_ids.shape[::-1], jnp.int32),
            pltpu.VMEM(gate_weights.shape[::-1], jnp.float32),
            pltpu.SemaphoreType.DMA((4,)),
        ],
        name="prepare",
        compiler_params=pltpu.CompilerParams(vmem_limit_bytes=VMEM_LIMIT),
        cost_estimate=pl.CostEstimate(flops=0, bytes_accessed=0, transcendentals=0),
    )(
        pltpu.with_memory_space_constraint(tokens, pltpu.HBM),
        pltpu.with_memory_space_constraint(w_down, pltpu.HBM),
        pltpu.with_memory_space_constraint(expert_ids.T, pltpu.HBM),
        pltpu.with_memory_space_constraint(gate_weights.T, pltpu.HBM),
    )


def cross_kernel(expert_count, wide_ref, cross_ref):
    half = cross_ref.shape[1]
    other = lax.axis_index("role") ^ 1
    gate = decode_gate(wide_ref[:, half:].astype(jnp.float32), other, expert_count)
    cross_ref[...] = compact(gate, wide_ref[:, :half], cross_ref.shape[0])


def cross_rows(wide, expert_count, capacity, hint=0):
    rows, width = wide.shape
    half = width - LANES
    return call(
        functools.partial(cross_kernel, expert_count),
        (wide,),
        ((capacity, half),),
        0,
        "cross_rows",
        hint=hint,
    )[0]


def row_starts(blocks):
    starts, rows = [], 0
    for block in blocks:
        starts.append(rows)
        rows += round_up(block.shape[0], 16)
    return tuple(starts), rows


def pack_kernel(starts, *refs):
    out_ref = refs[-1]
    for start, ref in zip(starts, refs):
        out_ref[start : start + ref.shape[0], :] = ref[:, : out_ref.shape[1]]


def pack(blocks, half, kept=(), hint=0):
    starts, rows = row_starts(blocks)
    return call(
        functools.partial(pack_kernel, starts),
        (*blocks, *kept),
        ((rows, half),),
        0,
        "pack_rows",
        hint=hint,
    )[0]


def hidden_kernel(near_ref, far_ref, gate_ref, up_ref, hidden_ref):
    half = near_ref.shape[1]
    core = lax.axis_index("tp")
    own = pl.ds(pl.multiple_of(core * half, LANES), half)
    sibling = pl.ds(pl.multiple_of((1 - core) * half, LANES), half)
    width = 256
    for first in range(0, hidden_ref.shape[1], width):
        units = slice(first, first + width)
        gate_proj, up_proj = (
            jnp.dot(near_ref[...], ref[own, units], preferred_element_type=jnp.float32)
            + jnp.dot(far_ref[...], ref[sibling, units], preferred_element_type=jnp.float32)
            for ref in (gate_ref, up_ref)
        )
        hidden_ref[:, units] = (jax.nn.silu(gate_proj) * up_proj).astype(jnp.bfloat16)


def hidden_units(near, far, w_gate, w_up):
    return call(
        hidden_kernel,
        (near, far, w_gate, w_up),
        ((near.shape[0], w_gate.shape[1]),),
        0,
        "hidden_units",
    )[0]


def down_kernel(expert_count, starts, wide_count, *refs):
    wides = refs[:wide_count]
    own_ref, other_ref, down_ref, down_other_ref = refs[wide_count : wide_count + 4]
    outs = refs[wide_count + 4 :]
    half = down_other_ref.shape[1]
    me = lax.axis_index("role")
    base = pl.multiple_of(lax.axis_index("tp") * half, LANES)
    gates = [decode_gate(ref[:, half:].astype(jnp.float32), me, expert_count) for ref in wides]
    width = 256
    for first in range(0, half, width):
        columns = slice(first, first + width)
        result = jnp.dot(
            own_ref[...],
            down_ref[0, :, pl.ds(pl.multiple_of(base + first, LANES), width)],
            preferred_element_type=jnp.float32,
        ) + jnp.dot(
            other_ref[...], down_other_ref[:, columns], preferred_element_type=jnp.float32
        )
        for index, (start, out_ref) in enumerate(zip(starts, outs)):
            block = result[start : start + out_ref.shape[0]].astype(jnp.bfloat16)
            if index < wide_count:
                block = gates[index] * block.astype(jnp.float32)
            out_ref[:, columns] = block


def down(wides, cross_count, hidden, hidden_other, w_down, down_other, capacity, expert_count):
    half = down_other.shape[1]
    shapes = [(wide.shape[0], half) for wide in wides] + [(capacity, half)] * cross_count
    starts, rows = [], 0
    for shape in shapes:
        starts.append(rows)
        rows += round_up(shape[0], 16)
    return call(
        functools.partial(down_kernel, expert_count, tuple(starts), len(wides)),
        (*wides, hidden, hidden_other, w_down, down_other),
        tuple(shapes),
        4 * rows * half * hidden.shape[1],
        "down",
        (),
        [jnp.float32] * len(wides) + [jnp.bfloat16] * cross_count,
    )


def attend_kernel(query_ref, latent_ref, lengths_ref, placement_ref, out_ref):
    slot_count, head_count, _ = query_ref.shape
    rank, context = out_ref.shape[2], latent_ref.shape[2]
    first = lax.axis_index("role") * slot_count
    position = lax.broadcasted_iota(jnp.int32, (head_count, context), 1)
    for slot in range(slot_count):
        here = placement_ref[...] == first + slot
        length = jnp.sum(jnp.where(here, lengths_ref[...], 0), axis=1, keepdims=True)
        scores = (
            jnp.dot(query_ref[slot], latent_ref[slot], preferred_element_type=jnp.float32)
            * score_scale
        )
        scores = jnp.where(position < length, scores, -jnp.inf)
        raised = jnp.exp(scores - jnp.max(scores, axis=1, keepdims=True))
        attn_weights = (raised / jnp.sum(raised, axis=1, keepdims=True)).astype(jnp.bfloat16)
        out_ref[slot] = lax.dot_general(
            attn_weights,
            latent_ref[slot, :rank, :],
            (((1,), (1,)), ((), ())),
            preferred_element_type=jnp.float32,
        ).astype(jnp.bfloat16)


def attend(q_lat, latent_cache, lengths, placement):
    slot_count, head_count, _ = q_lat.shape
    return pl.pallas_call(
        attend_kernel,
        out_shape=jax.ShapeDtypeStruct((slot_count, head_count, KV_RANK), jnp.bfloat16),
        name="attend",
        compiler_params=pltpu.CompilerParams(vmem_limit_bytes=VMEM_LIMIT),
        cost_estimate=pl.CostEstimate(flops=0, bytes_accessed=0, transcendentals=0),
    )(q_lat, latent_cache.transpose(0, 2, 1), lengths[None, :], placement[None, :])


def last_down_kernel(own_ref, other_ref, down_ref, down_other_ref, *outs):
    half = down_other_ref.shape[1]
    base = pl.multiple_of(lax.axis_index("tp") * half, LANES)
    start = 0
    for out_ref in outs:
        for first in range(0, out_ref.shape[1], 256):
            width = min(256, out_ref.shape[1] - first)
            column = start + first
            result = jnp.dot(
                own_ref[...],
                down_ref[0, :, pl.ds(pl.multiple_of(base + column, LANES), width)],
                preferred_element_type=jnp.float32,
            ) + jnp.dot(
                other_ref[...],
                down_other_ref[:, column : column + width],
                preferred_element_type=jnp.float32,
            )
            out_ref[:, first : first + width] = result[: out_ref.shape[0]].astype(jnp.bfloat16)
        start += out_ref.shape[1]


def last_down(hidden, hidden_other, w_down, down_other, capacity, widths):
    return call(
        last_down_kernel,
        (hidden, hidden_other, w_down, down_other),
        tuple((capacity, width) for width in widths),
        0,
        "last_down",
    )


def combine_kernel(expert_count, first, shift, sum_count, wide_ref, own_ref, back_ref, *refs):
    sums, outs = refs[:sum_count], refs[sum_count:]
    half = own_ref.shape[1]
    other = lax.axis_index("role") ^ 1
    gate = decode_gate(wide_ref[:, half:].astype(jnp.float32), other, expert_count)
    slots = slot_matrix(gate)[:, : back_ref.shape[0]]
    width = LANES
    for out_ref in outs:
        for column in range(0, out_ref.shape[1], width):
            columns = slice(first + column, first + column + width)
            spread = jnp.dot(
                slots,
                back_ref[:, columns.start - shift : columns.stop - shift],
                preferred_element_type=jnp.float32,
            )
            result = own_ref[:, columns] + gate * spread
            for ref in sums:
                result = result + ref[:, column : column + width].astype(jnp.float32)
            out_ref[:, column : column + width] = result.astype(out_ref.dtype)
        first += out_ref.shape[1]


def combine(
    wide, own, back, sums, expert_count, first, widths, dtype=jnp.bfloat16, shift=0, hint=0
):
    rows = own.shape[0]
    return call(
        functools.partial(combine_kernel, expert_count, first, shift, len(sums)),
        (wide, own, back, *sums),
        tuple((rows, width) for width in widths),
        0,
        "combine",
        types=(dtype,) * len(widths),
        hint=hint,
    )


def add_kernel(*refs):
    out_ref = refs[-1]
    count = len(refs) // 2
    first = 0
    for total_ref, part_ref in zip(refs[:count], refs[count:-1]):
        result = total_ref[...] + part_ref[...].astype(jnp.float32)
        out_ref[:, first : first + part_ref.shape[1]] = result.astype(jnp.bfloat16)
        first += part_ref.shape[1]


def add_last(totals, parts):
    shape = (parts[0].shape[0], sum(part.shape[1] for part in parts))
    return call(add_kernel, (*totals, *parts), (shape,), 0, "add_last", last=True)[0]


def swap(array, bits, places=(0, 1, 2, 3)):
    count = lax.axis_size("role")
    pairs = [(device, device ^ bits) for device in range(count) if device // 2 in places]
    return lax.ppermute(array, "role", pairs)


def swap_core(array):
    return lax.ppermute(array, "tp", [(0, 1), (1, 0)])


def route_multicast(
    q_lat, latent_cache, lengths, placement, tokens, expert_ids, gate_weights, w_gate, w_up, w_down
):
    role_count = lax.axis_size("role")
    token_count, route_count = expert_ids.shape
    half = tokens.shape[1]
    capacity = 3 * token_count * route_count // (2 * role_count)
    pair, mirror, row = 2, 6, 1

    wide, cross, down_away = prepare(
        tokens, w_down, expert_ids, gate_weights, role_count, capacity
    )
    wide_mirror = swap(wide, mirror)
    wide_pair = swap(wide, pair)
    cross_in = swap(cross, row)
    w_gate, w_up = w_gate[0], w_up[0]
    attended = attend(after(q_lat, wide), latent_cache, lengths, placement)
    cross_in = after(cross_in, attended)
    down_other = swap_core(after(down_away, attended))
    wide_pair = after(wide_pair, cross_in)
    cross_pair = cross_rows(wide_pair, role_count, capacity)
    cross_pair_in = swap(cross_pair, row)
    wide_mirror = after(wide_mirror, cross_pair)
    wide_far = swap(wide_mirror, pair)
    cross_mirror = cross_rows(wide_mirror, role_count, capacity)
    cross_mirror_in = swap(cross_mirror, row)
    cross_pair_in = after(cross_pair_in, cross_mirror)
    near_first = pack((after(wide, cross_pair_in), wide_pair, wide_mirror, cross_in), half, (w_gate, w_up))
    far_first = swap_core(near_first)
    wide_far = after(wide_far, near_first)
    cross_mirror_in = after(cross_mirror_in, wide_far)
    wide_far = after(wide_far, cross_mirror_in)
    cross_far = cross_rows(wide_far, role_count, capacity, 10**10)
    cross_far_in = swap(cross_far, row)
    near_second = pack((wide_far, cross_pair_in, cross_mirror_in), half)
    far_second = swap_core(near_second)
    hidden = hidden_units(near_first, after(far_first, near_second), w_gate, w_up)
    hidden_other = swap_core(hidden)
    hidden_second = hidden_units(near_second, after(far_second, hidden), w_gate, w_up)
    hidden_second_other = swap_core(hidden_second)
    cross_far_in = after(cross_far_in, hidden_second)
    far_third = swap_core(cross_far_in)
    down_weights = (w_down, down_other)
    hidden_other = after(hidden_other, cross_far_in)
    own, own_pair, own_mirror, back_own = down(
        (wide, wide_pair, wide_mirror),
        1,
        hidden,
        hidden_other,
        *down_weights,
        capacity,
        role_count,
    )
    far_third = after(far_third, own)
    hidden_third = hidden_units(cross_far_in, far_third, w_gate, w_up)
    hidden_third_other = swap_core(hidden_third)
    hidden_second_other = after(hidden_second_other, hidden_third)
    own_far, back_pair, back_mirror = down(
        (wide_far,), 2, hidden_second, hidden_second_other, *down_weights, capacity, role_count
    )
    hidden_third_other = after(hidden_third_other, own_far)
    split = half // 2
    widths = (split, half - split)
    back_far_left, back_far_right = last_down(
        hidden_third, hidden_third_other, *down_weights, capacity, widths
    )
    back_far_left = swap(back_far_left, row)
    back_far_right = swap(back_far_right, row)
    back_mirror = swap(back_mirror, row)
    back_pair = swap(back_pair, row)
    back_own = swap(back_own, row)

    (sum_far_left,) = combine(
        wide_far, own_far, back_far_left, (), role_count, 0, widths[:1]
    )
    from_far_left = swap(sum_far_left, pair)
    back_far_right = after(back_far_right, sum_far_left)
    (sum_far_right,) = combine(
        wide_far,
        own_far,
        back_far_right,
        (),
        role_count,
        split,
        widths[1:],
        shift=split,
    )
    from_far_right = swap(sum_far_right, pair)
    back_mirror = after(back_mirror, sum_far_right)
    from_far_left = after(from_far_left, back_mirror)
    (sum_mirror_left,) = combine(
        wide_mirror, own_mirror, back_mirror, (from_far_left,), role_count, 0, widths[:1]
    )
    from_mirror_left = swap(sum_mirror_left, mirror)
    from_far_right = after(from_far_right, sum_mirror_left)
    (sum_mirror_right,) = combine(
        wide_mirror, own_mirror, back_mirror, (from_far_right,), role_count, split, widths[1:]
    )
    from_mirror_right = swap(sum_mirror_right, mirror)
    back_pair = after(back_pair, sum_mirror_right)
    sum_pair_left, sum_pair_right = combine(
        wide_pair, own_pair, back_pair, (), role_count, 0, widths
    )
    from_pair_left = swap(sum_pair_left, pair)
    from_pair_right = swap(sum_pair_right, pair)
    back_own = after(back_own, sum_pair_left)
    from_mirror_left = after(from_mirror_left, back_own)
    (sum_left,) = combine(
        wide, own, back_own, (from_mirror_left,), role_count, 0, widths[:1], jnp.float32
    )
    from_mirror_right = after(from_mirror_right, sum_left)
    (sum_right,) = combine(
        wide, own, back_own, (from_mirror_right,), role_count, split, widths[1:], jnp.float32
    )
    from_pair_left = after(from_pair_left, sum_right)
    moe_result = add_last((sum_left, sum_right), (from_pair_left, from_pair_right))
    return (attended, moe_result)


def shards(
    q_lat, latent_cache, lengths, placement, tokens, expert_ids, gate_weights, w_gate, w_up, w_down
):
    if lax.axis_size("role") == 8 and lax.axis_size("tp") == 2:
        return route_multicast(
            q_lat,
            latent_cache,
            lengths,
            placement,
            tokens,
            expert_ids,
            gate_weights,
            w_gate,
            w_up,
            w_down,
        )
    attended = attend_local(q_lat, latent_cache, lengths, placement)
    routed = route_all_to_all(tokens, expert_ids, gate_weights, w_gate, w_up, w_down)
    return (attended, routed)


def solution(mesh):
    return jax.shard_map(
        shards,
        mesh=mesh,
        in_specs=(
            P(("groups", "role"), "tp", None),
            P(("groups", "role"), None, None),
            P("groups"),
            P("groups"),
            P(("groups", "role"), "tp"),
            P(("groups", "role"), None),
            P(("groups", "role"), None),
            P("role", None, "tp"),
            P("role", None, "tp"),
            P("role", "tp", None),
        ),
        out_specs=(P(("groups", "role"), "tp", None), P(("groups", "role"), "tp")),
        check_vma=False,
    )
```

```python
import functools

import jax
import jax.numpy as jnp
from jax import lax
from jax.experimental import pallas as pl
from jax.experimental.pallas import tpu as pltpu
from jax.sharding import PartitionSpec as P

KV_RANK = 512


score_scale = 192.0 ** (-0.5)


def attend_local(q_lat, latent_cache, lengths, placement):
    slot_count = q_lat.shape[0]
    offset = lax.axis_index("role") * slot_count
    slot_ids = offset + jnp.arange(slot_count, dtype=jnp.int32)
    matches = placement[None, :] == slot_ids[:, None]
    slot_length = jnp.sum(jnp.where(matches, lengths[None, :], 0), axis=1)
    scores = (
        jnp.einsum("shc,stc->sht", q_lat, latent_cache, preferred_element_type=jnp.float32)
        * score_scale
    )
    position = jnp.arange(latent_cache.shape[1], dtype=jnp.int32)
    visible = position[None, None, :] < slot_length[:, None, None]
    scores = jnp.where(visible, scores, -jnp.inf)
    highest = jnp.max(scores, axis=2, keepdims=True)
    raised = jnp.exp(scores - highest)
    attn_weights = (raised / jnp.sum(raised, axis=2, keepdims=True)).astype(jnp.bfloat16)
    values = latent_cache[:, :, :KV_RANK]
    return jnp.einsum(
        "sht,stc->shc", attn_weights, values, preferred_element_type=jnp.float32
    ).astype(jnp.bfloat16)


def route_all_to_all(tokens, expert_ids, gate_weights, w_gate, w_up, w_down):
    role_count = lax.axis_size("role")
    token_count = expert_ids.shape[0]
    route_count = expert_ids.shape[1]
    capacity = 3 * token_count * route_count // (2 * role_count)
    flat_ids = expert_ids.reshape(-1)
    onehot = (flat_ids[:, None] == jnp.arange(role_count, dtype=jnp.int32)[None, :]).astype(
        jnp.int32
    )
    earlier = jnp.cumsum(onehot, axis=0) - onehot
    slot_index = jnp.sum(earlier * onehot, axis=1)
    target = flat_ids * capacity + slot_index
    source = jnp.arange(token_count * route_count, dtype=jnp.int32) // route_count
    outgoing = lax.all_gather(tokens, "tp", axis=1, tiled=True)
    columns = outgoing.shape[1]
    buffer_rows = (
        jnp.zeros((role_count * capacity, columns), jnp.bfloat16).at[target].set(outgoing[source])
    )
    buffer_rows = buffer_rows.reshape(role_count, capacity, columns)
    gate_matrix = w_gate[0]
    up_matrix = w_up[0]
    down_matrix = w_down[0]
    received = lax.all_to_all(buffer_rows, "role", split_axis=0, concat_axis=0, tiled=True)
    item_count = received.shape[1]
    arrived = received.reshape(role_count * item_count, columns)
    gate_proj = jnp.dot(arrived, gate_matrix, preferred_element_type=jnp.float32)
    up_proj = jnp.dot(arrived, up_matrix, preferred_element_type=jnp.float32)
    expert_hidden = (jax.nn.silu(gate_proj) * up_proj).astype(jnp.bfloat16)
    partial_out = jnp.dot(expert_hidden, down_matrix, preferred_element_type=jnp.float32)
    summed = lax.psum_scatter(
        partial_out.astype(jnp.bfloat16), "tp", scatter_dimension=1, tiled=True
    )
    summed = summed.reshape(role_count, item_count, summed.shape[1])
    returned = lax.all_to_all(summed, "role", split_axis=0, concat_axis=0, tiled=True)
    half_width = returned.shape[2]
    flat_back = returned.reshape(role_count * capacity, half_width)
    chosen_rows = (
        flat_back[target].reshape(token_count, route_count, half_width).astype(jnp.float32)
    )
    moe_result = jnp.sum(chosen_rows * gate_weights[:, :, None], axis=1).astype(jnp.bfloat16)
    return moe_result


LANES = 128
VMEM_LIMIT = 16 * 1024 * 1024


def round_up(value, unit):
    return -(-value // unit) * unit


def call(kernel, operands, out_shapes, flops, name, scratch=(), types=None, last=False, hint=0):
    place = pl.BlockSpec(memory_space=pltpu.VMEM)
    return pl.pallas_call(
        kernel,
        in_specs=[place] * len(operands),
        out_specs=[place] * len(out_shapes),
        out_shape=[
            (jax.ShapeDtypeStruct if last else pltpu.VMEM)(
                shape, jnp.bfloat16 if types is None else types[index]
            )
            for index, shape in enumerate(out_shapes)
        ],
        scratch_shapes=list(scratch),
        name=name,
        compiler_params=pltpu.CompilerParams(vmem_limit_bytes=VMEM_LIMIT),
        cost_estimate=pl.CostEstimate(flops=hint, bytes_accessed=0, transcendentals=0),
    )(*[pltpu.with_memory_space_constraint(operand, pltpu.VMEM) for operand in operands])


def after(value, *earlier):
    return lax.optimization_barrier((value, *earlier))[0]


def lane_index(rows):
    return lax.broadcasted_iota(jnp.int32, (rows, LANES), 1)


def decode_gate(pieces, expert, expert_count):
    lane = lane_index(pieces.shape[0])
    wanted = lane == expert
    for piece in (1, 2):
        wanted = wanted | (lane == expert + piece * expert_count)
    return jnp.sum(jnp.where(wanted, pieces, 0.0), axis=1, keepdims=True)


def slot_matrix(gate):
    rows = gate.shape[0]
    named = jnp.broadcast_to((gate > 0.0).astype(jnp.float32), (rows, LANES))
    lower = lax.broadcasted_iota(jnp.int32, (rows, rows), 0) >= lax.broadcasted_iota(
        jnp.int32, (rows, rows), 1
    )
    rank = jnp.dot(
        lower.astype(jnp.bfloat16), named.astype(jnp.bfloat16), preferred_element_type=jnp.float32
    )
    slot = lane_index(rows).astype(jnp.float32)
    return jnp.where((named > 0.0) & (rank - 1.0 == slot), 1.0, 0.0).astype(jnp.bfloat16)


def compact(gate, rows_in, capacity):
    picked = lax.dot_general(
        slot_matrix(gate),
        rows_in,
        (((0,), (0,)), ((), ())),
        preferred_element_type=jnp.float32,
    )
    return picked[:capacity].astype(jnp.bfloat16)


def prepare_kernel(
    expert_count,
    tokens_hbm,
    ids_hbm,
    gates_hbm,
    wide_ref,
    cross_ref,
    ids_ref,
    gates_ref,
    sems,
):
    rows, half = tokens_hbm.shape
    copy = pltpu.make_async_copy(tokens_hbm, wide_ref.at[:, :half], sems.at[0])
    first = [
        pltpu.make_async_copy(ids_hbm, ids_ref, sems.at[2]),
        pltpu.make_async_copy(gates_hbm, gates_ref, sems.at[3]),
    ]
    for part in first:
        part.start()
    copy.start()
    for part in first:
        part.wait()
    piece_rows = round_up(3 * expert_count, 16)
    line = lax.broadcasted_iota(jnp.int32, (piece_rows, rows), 0)
    named = line
    for piece in (1, 2):
        named = jnp.where(line >= piece * expert_count, line - piece * expert_count, named)
    dense = jnp.zeros((piece_rows, rows), jnp.float32)
    for choice in range(ids_ref.shape[0]):
        dense = dense + jnp.where(
            ids_ref[choice : choice + 1, :] == named, gates_ref[choice : choice + 1, :], 0.0
        )
    high = dense.astype(jnp.bfloat16).astype(jnp.float32)
    middle = (dense - high).astype(jnp.bfloat16).astype(jnp.float32)
    low = dense - high - middle
    pieces = jnp.where(line < expert_count, high, jnp.where(line < 2 * expert_count, middle, low))
    unit = lax.broadcasted_iota(jnp.int32, (piece_rows, LANES), 0) == lax.broadcasted_iota(
        jnp.int32, (piece_rows, LANES), 1
    )
    turned = lax.dot_general(
        pieces.astype(jnp.bfloat16),
        unit.astype(jnp.bfloat16),
        (((0,), (0,)), ((), ())),
        preferred_element_type=jnp.float32,
    )
    wide_ref[:, half:] = turned.astype(jnp.bfloat16)
    copy.wait()
    gate = decode_gate(turned, lax.axis_index("role") ^ 1, expert_count)
    cross_ref[...] = compact(gate, wide_ref[:, :half], cross_ref.shape[0])


def prepare(tokens, expert_ids, gate_weights, expert_count, capacity):
    rows, half = tokens.shape
    shapes = [
        (rows, half + LANES),
        (capacity, half),
    ]
    whole = pl.BlockSpec(memory_space=pltpu.VMEM)
    return pl.pallas_call(
        functools.partial(prepare_kernel, expert_count),
        in_specs=[pl.BlockSpec(memory_space=pltpu.HBM)] * 3,
        out_specs=[whole] * len(shapes),
        out_shape=[pltpu.VMEM(shape, jnp.bfloat16) for shape in shapes],
        scratch_shapes=[
            pltpu.VMEM(expert_ids.shape[::-1], jnp.int32),
            pltpu.VMEM(gate_weights.shape[::-1], jnp.float32),
            pltpu.SemaphoreType.DMA((4,)),
        ],
        name="prepare",
        compiler_params=pltpu.CompilerParams(vmem_limit_bytes=VMEM_LIMIT),
        cost_estimate=pl.CostEstimate(flops=0, bytes_accessed=0, transcendentals=0),
    )(
        pltpu.with_memory_space_constraint(tokens, pltpu.HBM),
        pltpu.with_memory_space_constraint(expert_ids.T, pltpu.HBM),
        pltpu.with_memory_space_constraint(gate_weights.T, pltpu.HBM),
    )


def cross_kernel(expert_count, wide_ref, cross_ref):
    half = cross_ref.shape[1]
    other = lax.axis_index("role") ^ 1
    gate = decode_gate(wide_ref[:, half:].astype(jnp.float32), other, expert_count)
    cross_ref[...] = compact(gate, wide_ref[:, :half], cross_ref.shape[0])


def cross_rows(wide, expert_count, capacity, hint=0):
    rows, width = wide.shape
    half = width - LANES
    return call(
        functools.partial(cross_kernel, expert_count),
        (wide,),
        ((capacity, half),),
        0,
        "cross_rows",
        hint=hint,
    )[0]


def row_starts(blocks):
    starts, rows = [], 0
    for block in blocks:
        starts.append(rows)
        rows += round_up(block.shape[0], 16)
    return tuple(starts), rows


def pack_kernel(starts, *refs):
    out_ref = refs[-1]
    for start, ref in zip(starts, refs):
        out_ref[start : start + ref.shape[0], :] = ref[:, : out_ref.shape[1]]


def pack(blocks, half, kept=(), hint=0):
    starts, rows = row_starts(blocks)
    return call(
        functools.partial(pack_kernel, starts),
        (*blocks, *kept),
        ((rows, half),),
        0,
        "pack_rows",
        hint=hint,
    )[0]


def hidden_kernel(near_ref, far_ref, gate_ref, up_ref, hidden_ref):
    half = near_ref.shape[1]
    core = lax.axis_index("tp")
    own = pl.ds(pl.multiple_of(core * half, LANES), half)
    sibling = pl.ds(pl.multiple_of((1 - core) * half, LANES), half)
    width = 256
    for first in range(0, hidden_ref.shape[1], width):
        units = slice(first, first + width)
        gate_proj, up_proj = (
            jnp.dot(near_ref[...], ref[own, units], preferred_element_type=jnp.float32)
            + jnp.dot(far_ref[...], ref[sibling, units], preferred_element_type=jnp.float32)
            for ref in (gate_ref, up_ref)
        )
        hidden_ref[:, units] = (jax.nn.silu(gate_proj) * up_proj).astype(jnp.bfloat16)


def hidden_units(near, far, w_gate, w_up):
    return call(
        hidden_kernel,
        (near, far, w_gate, w_up),
        ((near.shape[0], w_gate.shape[1]),),
        0,
        "hidden_units",
    )[0]


def down_kernel(expert_count, starts, wide_count, *refs):
    wides = refs[:wide_count]
    own_ref, other_ref, down_ref, down_other_ref = refs[wide_count : wide_count + 4]
    outs = refs[wide_count + 4 :]
    half = down_other_ref.shape[1]
    me = lax.axis_index("role")
    base = pl.multiple_of(lax.axis_index("tp") * half, LANES)
    gates = [decode_gate(ref[:, half:].astype(jnp.float32), me, expert_count) for ref in wides]
    width = 256
    for first in range(0, half, width):
        columns = slice(first, first + width)
        result = jnp.dot(
            own_ref[...],
            down_ref[0, :, pl.ds(pl.multiple_of(base + first, LANES), width)],
            preferred_element_type=jnp.float32,
        ) + jnp.dot(
            other_ref[...], down_other_ref[:, columns], preferred_element_type=jnp.float32
        )
        for index, (start, out_ref) in enumerate(zip(starts, outs)):
            block = result[start : start + out_ref.shape[0]].astype(jnp.bfloat16)
            if index < wide_count:
                block = gates[index] * block.astype(jnp.float32)
            out_ref[:, columns] = block


def down(wides, cross_count, hidden, hidden_other, w_down, down_other, capacity, expert_count):
    half = down_other.shape[1]
    shapes = [(wide.shape[0], half) for wide in wides] + [(capacity, half)] * cross_count
    starts, rows = [], 0
    for shape in shapes:
        starts.append(rows)
        rows += round_up(shape[0], 16)
    return call(
        functools.partial(down_kernel, expert_count, tuple(starts), len(wides)),
        (*wides, hidden, hidden_other, w_down, down_other),
        tuple(shapes),
        4 * rows * half * hidden.shape[1],
        "down",
        (),
        [jnp.float32] * len(wides) + [jnp.bfloat16] * cross_count,
    )


def attend_kernel(
    query_ref, latent_ref, lengths_ref, placement_ref, down_hbm, out_ref, away_ref, sem
):
    half = away_ref.shape[1]
    sibling = pl.multiple_of((1 - lax.axis_index("tp")) * half, LANES)
    away = pltpu.make_async_copy(down_hbm.at[0, :, pl.ds(sibling, half)], away_ref, sem)
    away.start()
    slot_count, head_count, _ = query_ref.shape
    rank, context = out_ref.shape[2], latent_ref.shape[2]
    first = lax.axis_index("role") * slot_count
    position = lax.broadcasted_iota(jnp.int32, (head_count, context), 1)
    for slot in range(slot_count):
        here = placement_ref[...] == first + slot
        length = jnp.sum(jnp.where(here, lengths_ref[...], 0), axis=1, keepdims=True)
        scores = (
            jnp.dot(query_ref[slot], latent_ref[slot], preferred_element_type=jnp.float32)
            * score_scale
        )
        scores = jnp.where(position < length, scores, -jnp.inf)
        raised = jnp.exp(scores - jnp.max(scores, axis=1, keepdims=True))
        attn_weights = (raised / jnp.sum(raised, axis=1, keepdims=True)).astype(jnp.bfloat16)
        out_ref[slot] = lax.dot_general(
            attn_weights,
            latent_ref[slot, :rank, :],
            (((1,), (1,)), ((), ())),
            preferred_element_type=jnp.float32,
        ).astype(jnp.bfloat16)
    away.wait()


def attend(q_lat, latent_cache, lengths, placement, w_down):
    slot_count, head_count, _ = q_lat.shape
    place = pl.BlockSpec(memory_space=pltpu.VMEM)
    return pl.pallas_call(
        attend_kernel,
        in_specs=[place] * 4 + [pl.BlockSpec(memory_space=pltpu.HBM)],
        out_specs=[place] * 2,
        out_shape=[
            jax.ShapeDtypeStruct((slot_count, head_count, KV_RANK), jnp.bfloat16),
            pltpu.VMEM((w_down.shape[1], w_down.shape[2] // 2), jnp.bfloat16),
        ],
        scratch_shapes=[pltpu.SemaphoreType.DMA],
        name="attend",
        compiler_params=pltpu.CompilerParams(vmem_limit_bytes=VMEM_LIMIT),
        cost_estimate=pl.CostEstimate(flops=0, bytes_accessed=0, transcendentals=0),
    )(
        q_lat,
        latent_cache.transpose(0, 2, 1),
        lengths[None, :],
        placement[None, :],
        pltpu.with_memory_space_constraint(w_down, pltpu.HBM),
    )


def last_down_kernel(own_ref, other_ref, down_ref, down_other_ref, *outs):
    half = down_other_ref.shape[1]
    base = pl.multiple_of(lax.axis_index("tp") * half, LANES)
    start = 0
    for out_ref in outs:
        for first in range(0, out_ref.shape[1], 256):
            width = min(256, out_ref.shape[1] - first)
            column = start + first
            result = jnp.dot(
                own_ref[...],
                down_ref[0, :, pl.ds(pl.multiple_of(base + column, LANES), width)],
                preferred_element_type=jnp.float32,
            ) + jnp.dot(
                other_ref[...],
                down_other_ref[:, column : column + width],
                preferred_element_type=jnp.float32,
            )
            out_ref[:, first : first + width] = result[: out_ref.shape[0]].astype(jnp.bfloat16)
        start += out_ref.shape[1]


def last_down(hidden, hidden_other, w_down, down_other, capacity, widths):
    return call(
        last_down_kernel,
        (hidden, hidden_other, w_down, down_other),
        tuple((capacity, width) for width in widths),
        0,
        "last_down",
    )


def combine_kernel(expert_count, first, shift, sum_count, wide_ref, own_ref, back_ref, *refs):
    sums, outs = refs[:sum_count], refs[sum_count:]
    half = own_ref.shape[1]
    other = lax.axis_index("role") ^ 1
    gate = decode_gate(wide_ref[:, half:].astype(jnp.float32), other, expert_count)
    slots = slot_matrix(gate)[:, : back_ref.shape[0]]
    width = LANES
    for out_ref in outs:
        for column in range(0, out_ref.shape[1], width):
            columns = slice(first + column, first + column + width)
            spread = jnp.dot(
                slots,
                back_ref[:, columns.start - shift : columns.stop - shift],
                preferred_element_type=jnp.float32,
            )
            result = own_ref[:, columns] + gate * spread
            for ref in sums:
                result = result + ref[:, column : column + width].astype(jnp.float32)
            out_ref[:, column : column + width] = result.astype(out_ref.dtype)
        first += out_ref.shape[1]


def combine(
    wide, own, back, sums, expert_count, first, widths, dtype=jnp.bfloat16, shift=0, hint=0
):
    rows = own.shape[0]
    return call(
        functools.partial(combine_kernel, expert_count, first, shift, len(sums)),
        (wide, own, back, *sums),
        tuple((rows, width) for width in widths),
        0,
        "combine",
        types=(dtype,) * len(widths),
        hint=hint,
    )


def add_kernel(*refs):
    out_ref = refs[-1]
    count = len(refs) // 2
    first = 0
    for total_ref, part_ref in zip(refs[:count], refs[count:-1]):
        result = total_ref[...] + part_ref[...].astype(jnp.float32)
        out_ref[:, first : first + part_ref.shape[1]] = result.astype(jnp.bfloat16)
        first += part_ref.shape[1]


def add_last(totals, parts):
    shape = (parts[0].shape[0], sum(part.shape[1] for part in parts))
    return call(add_kernel, (*totals, *parts), (shape,), 0, "add_last", last=True)[0]


def swap(array, bits, places=(0, 1, 2, 3)):
    count = lax.axis_size("role")
    pairs = [(device, device ^ bits) for device in range(count) if device // 2 in places]
    return lax.ppermute(array, "role", pairs)


def swap_core(array):
    return lax.ppermute(array, "tp", [(0, 1), (1, 0)])


def route_multicast(
    q_lat, latent_cache, lengths, placement, tokens, expert_ids, gate_weights, w_gate, w_up, w_down
):
    role_count = lax.axis_size("role")
    token_count, route_count = expert_ids.shape
    half = tokens.shape[1]
    capacity = 3 * token_count * route_count // (2 * role_count)
    pair, mirror, row = 2, 6, 1

    wide, cross = prepare(
        tokens, expert_ids, gate_weights, role_count, capacity
    )
    wide_mirror = swap(wide, mirror)
    wide_pair = swap(wide, pair)
    cross_in = swap(cross, row)
    w_gate, w_up = w_gate[0], w_up[0]
    attended, down_away = attend(
        after(q_lat, wide), latent_cache, lengths, placement, w_down
    )
    cross_in = after(cross_in, attended)
    down_other = swap_core(after(down_away, attended))
    wide_pair = after(wide_pair, cross_in)
    cross_pair = cross_rows(wide_pair, role_count, capacity)
    cross_pair_in = swap(cross_pair, row)
    wide_mirror = after(wide_mirror, cross_pair)
    wide_far = swap(wide_mirror, pair)
    cross_mirror = cross_rows(wide_mirror, role_count, capacity)
    cross_mirror_in = swap(cross_mirror, row)
    cross_pair_in = after(cross_pair_in, cross_mirror)
    near_first = pack((after(wide, cross_pair_in), wide_pair, wide_mirror, cross_in), half, (w_gate, w_up))
    far_first = swap_core(near_first)
    wide_far = after(wide_far, near_first)
    cross_mirror_in = after(cross_mirror_in, wide_far)
    wide_far = after(wide_far, cross_mirror_in)
    cross_far = cross_rows(wide_far, role_count, capacity, 10**10)
    cross_far_in = swap(cross_far, row)
    near_second = pack((wide_far, cross_pair_in, cross_mirror_in), half)
    far_second = swap_core(near_second)
    hidden = hidden_units(near_first, after(far_first, near_second), w_gate, w_up)
    hidden_other = swap_core(hidden)
    hidden_second = hidden_units(near_second, after(far_second, hidden), w_gate, w_up)
    hidden_second_other = swap_core(hidden_second)
    cross_far_in = after(cross_far_in, hidden_second)
    far_third = swap_core(cross_far_in)
    down_weights = (w_down, down_other)
    hidden_other = after(hidden_other, cross_far_in)
    own, own_pair, own_mirror, back_own = down(
        (wide, wide_pair, wide_mirror),
        1,
        hidden,
        hidden_other,
        *down_weights,
        capacity,
        role_count,
    )
    far_third = after(far_third, own)
    hidden_third = hidden_units(cross_far_in, far_third, w_gate, w_up)
    hidden_third_other = swap_core(hidden_third)
    hidden_second_other = after(hidden_second_other, hidden_third)
    own_far, back_pair, back_mirror = down(
        (wide_far,), 2, hidden_second, hidden_second_other, *down_weights, capacity, role_count
    )
    hidden_third_other = after(hidden_third_other, own_far)
    split = half // 2
    widths = (split, half - split)
    back_far_left, back_far_right = last_down(
        hidden_third, hidden_third_other, *down_weights, capacity, widths
    )
    back_far_left = swap(back_far_left, row)
    back_far_right = swap(back_far_right, row)
    back_mirror = swap(back_mirror, row)
    back_pair = swap(back_pair, row)
    back_own = swap(back_own, row)

    (sum_far_left,) = combine(
        wide_far, own_far, back_far_left, (), role_count, 0, widths[:1]
    )
    from_far_left = swap(sum_far_left, pair)
    back_far_right = after(back_far_right, sum_far_left)
    (sum_far_right,) = combine(
        wide_far,
        own_far,
        back_far_right,
        (),
        role_count,
        split,
        widths[1:],
        shift=split,
    )
    from_far_right = swap(sum_far_right, pair)
    back_mirror = after(back_mirror, sum_far_right)
    from_far_left = after(from_far_left, back_mirror)
    (sum_mirror_left,) = combine(
        wide_mirror, own_mirror, back_mirror, (from_far_left,), role_count, 0, widths[:1]
    )
    from_mirror_left = swap(sum_mirror_left, mirror)
    from_far_right = after(from_far_right, sum_mirror_left)
    (sum_mirror_right,) = combine(
        wide_mirror, own_mirror, back_mirror, (from_far_right,), role_count, split, widths[1:]
    )
    from_mirror_right = swap(sum_mirror_right, mirror)
    back_pair = after(back_pair, sum_mirror_right)
    sum_pair_left, sum_pair_right = combine(
        wide_pair, own_pair, back_pair, (), role_count, 0, widths
    )
    from_pair_left = swap(sum_pair_left, pair)
    from_pair_right = swap(sum_pair_right, pair)
    back_own = after(back_own, sum_pair_left)
    from_mirror_left = after(from_mirror_left, back_own)
    (sum_left,) = combine(
        wide, own, back_own, (from_mirror_left,), role_count, 0, widths[:1], jnp.float32
    )
    from_mirror_right = after(from_mirror_right, sum_left)
    (sum_right,) = combine(
        wide, own, back_own, (from_mirror_right,), role_count, split, widths[1:], jnp.float32
    )
    from_pair_left = after(from_pair_left, sum_right)
    moe_result = add_last((sum_left, sum_right), (from_pair_left, from_pair_right))
    return (attended, moe_result)


def shards(
    q_lat, latent_cache, lengths, placement, tokens, expert_ids, gate_weights, w_gate, w_up, w_down
):
    if lax.axis_size("role") == 8 and lax.axis_size("tp") == 2:
        return route_multicast(
            q_lat,
            latent_cache,
            lengths,
            placement,
            tokens,
            expert_ids,
            gate_weights,
            w_gate,
            w_up,
            w_down,
        )
    attended = attend_local(q_lat, latent_cache, lengths, placement)
    routed = route_all_to_all(tokens, expert_ids, gate_weights, w_gate, w_up, w_down)
    return (attended, routed)


def solution(mesh):
    return jax.shard_map(
        shards,
        mesh=mesh,
        in_specs=(
            P(("groups", "role"), "tp", None),
            P(("groups", "role"), None, None),
            P("groups"),
            P("groups"),
            P(("groups", "role"), "tp"),
            P(("groups", "role"), None),
            P(("groups", "role"), None),
            P("role", None, "tp"),
            P("role", None, "tp"),
            P("role", "tp", None),
        ),
        out_specs=(P(("groups", "role"), "tp", None), P(("groups", "role"), "tp")),
        check_vma=False,
    )
```
